32 devices in a mesh: dp: 4 (over z), own: 8 (over y, x, core).
Axes of the slice: x: 2, y: 2, z: 4, core: 2. Of those that a mesh axis runs over, the one named last changes fastest.
Arguments:
- inputs: bfloat16 [1024, 8192], P('dp', 'own'), may hold values from -6 to 6
- out_grad: bfloat16 [1024, 8192], P('dp', 'own'), may hold values from -6 to 6
- int_values: bfloat16 [3, 3328, 128, 128], P(None, 'own'), may hold values from -127 to 127, as said below
- scales: float32 [3, 3328], P(None, 'own'), may hold values from 0.00011792096 to 0.0004684968
- block_rows: int32 [3, 128, 26], replicated, may hold values from 0 to 63, as said below
- holder: int32 [3, 128, 26], replicated, may hold values from 0 to 7, as said below
- slot_index: int32 [3, 128, 26], replicated, may hold values from 0 to 415, as said below
Outputs:
- input_grad: bfloat16 [1024, 8192], P('dp', 'own')
- grad_weights: bfloat16 [3, 3328, 128, 128], P(None, 'own', 'dp')
The draws below stay inside these ranges and needn't reach their ends.
Inputs may be any that keep to these rules, and one draw needn't show every extreme that they name: int_values holds whole numbers. `block_rows`: the 26 row blocks of each block column of each matrix are distinct and increasing. For each matrix and each group of 16 consecutive block columns, no holder holds more than 70 of the group's blocks, and some holder holds exactly 70; each holder holds exactly 416 blocks of each matrix. For each matrix the pairs (holder, slot_index) are distinct, so every slot of every holder holds one block.
All inputs are finite; a program needn't handle non-finite values.
Results may differ from the reference program's by a relative error of at most 0.015.
Values may be sent and summed in bfloat16 or wider, within the bound.
No kernel may reach another device: no remote copies, remote signals or barrier semaphores. Data moves between devices by JAX's collectives and lax.ppermute only.
A program may use at most 512 MiB of HBM per device.

```python
import math
import jax
import jax.numpy as jnp
from jax import lax

D = 8192
BLOCK = 128
KEEP = 26
TOK_DEV = 256
TOKENS = 1024
RBLK = 64
FBLK = 128
COLS_DEV = 16
SLOTS = 416
N_DP = 4
N_OWN = 8


def ownership(key):
    group = COLS_DEV * KEEP
    active = 3 * N_OWN // 4
    index = jnp.arange(N_OWN, dtype=jnp.int32)
    profile = jnp.where(index < active, (index + 1) * group // active - index * group // active, 0).astype(jnp.int32)
    ends = jnp.cumsum(profile)
    starts = ends - profile
    loads = profile[(index[:, None] - index[None, :]) % N_OWN]
    before = jnp.cumsum(loads, axis=1) - loads
    holders = []
    slots = []
    for which in range(3):
        base = jax.random.fold_in(jax.random.fold_in(key, 71), which)
        order = jax.random.permutation(jax.random.fold_in(base, 1), N_OWN).astype(jnp.int32)
        spots = jax.vmap(lambda k: jax.random.permutation(k, group))(jax.random.split(jax.random.fold_in(base, 2), N_OWN)).astype(jnp.int32)
        places = jax.vmap(lambda k: jax.random.permutation(k, group))(jax.random.split(jax.random.fold_in(base, 3), N_OWN)).astype(jnp.int32)
        level = jnp.sum((ends[None, None, :] <= spots[:, :, None]).astype(jnp.int32), axis=2)
        columns = jnp.broadcast_to(index[:, None], level.shape)
        rank_turn = (level + columns) % N_OWN
        owner = order[rank_turn]
        offset = before[rank_turn, columns] + spots - starts[level]
        holders.append(owner)
        slots.append(places[owner, offset])
    holder = jnp.stack(holders).reshape(3, FBLK, KEEP).astype(jnp.int32)
    slot_index = jnp.stack(slots).reshape(3, FBLK, KEEP).astype(jnp.int32)
    return (holder, slot_index)


def draw_holder(key, part):
    return ownership(key)[0]


def draw_slot_index(key, part):
    return ownership(key)[1]


def draw_block_rows(key, part):
    keys = jax.random.split(jax.random.fold_in(key, 5), 3 * FBLK)
    picks = jax.vmap(lambda k: jax.random.permutation(k, RBLK)[:KEEP])(keys)
    return jnp.sort(picks, axis=1).reshape(3, FBLK, KEEP).astype(jnp.int32)


def draw_int_values(key, part):
    values = jax.random.randint(jax.random.fold_in(key, 9), (3, N_OWN * SLOTS, BLOCK, BLOCK), -127, 128)
    return values.astype(jnp.float32).astype(jnp.bfloat16)


def levels(key, extent, cuts, least, high):
    def one(dim, parts):
        steps = jax.random.uniform(jax.random.fold_in(jax.random.fold_in(key, 6), dim), (parts,), jnp.float32, least / len(cuts), high / len(cuts))
        return jnp.repeat(jnp.exp(steps), extent[dim] // parts).reshape((-1,) + (1,) * (len(extent) - dim - 1))

    level = one(*cuts[0])
    for cut in cuts[1:]:
        level = level * one(*cut)
    return level


def centred(stream_key, dims, spread, bound, cuts=(), kind=jnp.bfloat16):
    drawn = spread * jax.random.normal(stream_key, dims, jnp.float32)
    if cuts:
        drawn = drawn * levels(stream_key, dims, cuts, -0.22, 0.18)
    return jnp.clip(drawn, -bound, bound).astype(kind)


def setup_inputs(seed: int = 0) -> dict:
    seeds = jax.random.split(jax.random.key(seed), 8)
    return {
        "inputs": centred(seeds[0], (TOKENS, D), 1.0, 6.0, ((0, 4), (1, 8))),
        "out_grad": centred(seeds[1], (TOKENS, D), 1.0, 6.0, ((0, 4), (1, 8))),
        "int_values": draw_int_values(jax.random.fold_in(seeds[7], 71), 0),
        "scales": jnp.clip(jnp.exp(math.log(0.0004684968) - 1.3795147 * jax.random.uniform(seeds[3], (3, N_OWN * SLOTS), jnp.float32) ** levels(seeds[3], (3, N_OWN * SLOTS), ((1, 8),), -0.2, 0.2)), 0.00011792096, 0.0004684968),
        "block_rows": draw_block_rows(jax.random.fold_in(seeds[7], 71), 0),
        "holder": draw_holder(jax.random.fold_in(seeds[7], 71), 0),
        "slot_index": draw_slot_index(jax.random.fold_in(seeds[7], 71), 0),
    }


def rounded(value):
    return lax.optimization_barrier(value.astype(jnp.bfloat16)).astype(jnp.float32)

def reference(inputs, out_grad, int_values, scales, block_rows, holder, slot_index):
    weights = (int_values.astype(jnp.float32) * scales[:, :, None, None]).astype(jnp.bfloat16)
    factor = 1.0 / math.sqrt(TOKENS)
    input_rows = inputs.reshape(TOKENS, RBLK, BLOCK)
    cotangent_rows = out_grad.reshape(TOKENS, RBLK, BLOCK)
    location = (holder * SLOTS + slot_index).astype(jnp.int32)
    rows_group = jnp.transpose(block_rows.reshape(3, N_OWN, COLS_DEV, KEEP), (1, 0, 2, 3))
    where_group = jnp.transpose(location.reshape(3, N_OWN, COLS_DEV, KEEP), (1, 0, 2, 3))

    def split_tokens(value):
        return value.reshape((N_DP, TOK_DEV) + value.shape[1:])

    def one_group(total, pieces):
        rows_here, where_here = pieces
        w_gate = weights[0][where_here[0]].astype(jnp.float32)
        w_up = weights[1][where_here[1]].astype(jnp.float32)
        w_down = weights[2][where_here[2]].astype(jnp.float32)
        inputs_gate = input_rows[:, rows_here[0]].astype(jnp.float32)
        inputs_up = input_rows[:, rows_here[1]].astype(jnp.float32)
        cotangent_down = cotangent_rows[:, rows_here[2]].astype(jnp.float32)
        gate = jnp.einsum('tckd,ckdf->tcf', inputs_gate, w_gate)
        up_value = jnp.einsum('tckd,ckdf->tcf', inputs_up, w_up)
        grad_act = jnp.einsum('tckd,ckfd->tcf', cotangent_down, w_down)
        sigmoid_g = jax.nn.sigmoid(gate)
        activated = gate * sigmoid_g
        value = rounded(activated * up_value)
        grad_gate = rounded(grad_act * up_value * sigmoid_g * (1.0 + gate * (1.0 - sigmoid_g)))
        grad_up = rounded(grad_act * activated)
        back_gate = jnp.einsum('tcf,ckdf->tckd', grad_gate, w_gate).reshape(TOKENS, COLS_DEV * KEEP, BLOCK)
        back_up = jnp.einsum('tcf,ckdf->tckd', grad_up, w_up).reshape(TOKENS, COLS_DEV * KEEP, BLOCK)
        partial_value = jnp.zeros((TOKENS, RBLK, BLOCK), jnp.float32)
        partial_value = partial_value.at[:, rows_here[0].reshape(-1)].add(back_gate)
        partial_value = partial_value.at[:, rows_here[1].reshape(-1)].add(back_up)
        total = total + rounded(partial_value)
        terms = [jnp.einsum('ntckd,ntcf->nckdf', split_tokens(inputs_gate), split_tokens(grad_gate)), jnp.einsum('ntckd,ntcf->nckdf', split_tokens(inputs_up), split_tokens(grad_up)), jnp.einsum('ntcf,ntckd->nckfd', split_tokens(value), split_tokens(cotangent_down))]
        grads = jnp.stack([lax.optimization_barrier(jnp.sum(rounded(term * factor), axis=0)) for term in terms]).astype(jnp.bfloat16)
        return (total, grads)
    start = jnp.zeros((TOKENS, RBLK, BLOCK), jnp.float32)
    total, grads = lax.scan(one_group, start, (rows_group, where_group))
    grads = jnp.transpose(grads, (1, 0, 2, 3, 4, 5)).reshape(3, FBLK * KEEP, BLOCK, BLOCK)
    result = jnp.zeros((3, N_OWN * SLOTS, BLOCK, BLOCK), jnp.bfloat16)
    for which in range(3):
        result = result.at[which, location[which].reshape(-1)].set(grads[which])
    return (total.reshape(TOKENS, D).astype(jnp.bfloat16), result)
```

```python
import functools
import math

import jax
import jax.numpy as jnp
from jax import lax
from jax.experimental import pallas as pl
from jax.experimental.pallas import tpu as pltpu
from jax.sharding import PartitionSpec as P

F32 = jnp.float32
BF16 = jnp.bfloat16
NT = (((1,), (1,)), ((), ()))
PARAMS = pltpu.CompilerParams(vmem_limit_bytes=56 * 2**20)


def whole(shape):
    return pl.BlockSpec(shape, lambda *_: (0,) * len(shape))


def pack(which, ints, scales, slots, quarter, rows_each):
    slot_count, block = ints.shape[1], ints.shape[2]
    places = slots.shape[0]

    def kernel(slots, quarter, scales, ints, out):
        def place(index, _):
            slot = slots[index]
            out[index] = (ints[0, slot].astype(F32) * scales[slot]).astype(BF16)
            return _

        lax.fori_loop(0, places, place, 0, unroll=8)

    return pl.pallas_call(
        kernel,
        out_shape=jax.ShapeDtypeStruct((places, rows_each, block), BF16),
        grid_spec=pltpu.PrefetchScalarGridSpec(
            num_scalar_prefetch=3,
            grid=(1,),
            in_specs=[
                pl.BlockSpec(
                    (1, slot_count, rows_each, block), lambda g, s, q, c: (which, 0, q[0], 0)
                )
            ],
            out_specs=whole((places, rows_each, block)),
        ),
        compiler_params=PARAMS,
        cost_estimate=pl.CostEstimate(
            flops=places * rows_each * block * 2,
            bytes_accessed=4 * places * rows_each * block,
            transcendentals=0,
        ),
        name="pack",
    )(slots, quarter, scales, ints)


def forward(x, arrived, flat, rows, columns, row_blocks):
    places, rows_each, block = arrived.shape
    tokens, depth = x.shape
    keep = flat.shape[0] // columns
    quarters = block // rows_each

    def kernel(flat, rows, x, arrived, dense, out):
        step = pl.program_id(0)
        dense[...] = jnp.zeros_like(dense)
        for half in range(2):
            base = (step * 2 + half) * keep
            lanes = slice(half * block, (half + 1) * block)

            def place(k, _):
                dense[rows[base + k], :, lanes] = arrived[flat[base + k]]
                return _

            lax.fori_loop(0, keep, place, 0, unroll=2)
        weights = dense[...].reshape(depth, 2 * block)
        result = jnp.dot(x[...], weights, preferred_element_type=F32)
        turned = jnp.transpose(result).astype(BF16)
        for half in range(2):
            for q in range(quarters):
                first = half * block + q * rows_each
                out[q, half] = turned[first : first + rows_each]

    return pl.pallas_call(
        kernel,
        out_shape=(
            jax.ShapeDtypeStruct((row_blocks, rows_each, columns * block), BF16),
            jax.ShapeDtypeStruct((quarters, columns, rows_each, tokens), BF16),
        ),
        grid_spec=pltpu.PrefetchScalarGridSpec(
            num_scalar_prefetch=2,
            grid=(columns // 2,),
            in_specs=[whole((tokens, depth)), whole((places, rows_each, block))],
            out_specs=(
                pl.BlockSpec((row_blocks, rows_each, 2 * block), lambda g, f, r: (0, 0, g)),
                pl.BlockSpec((quarters, 2, rows_each, tokens), lambda g, f, r: (0, g, 0, 0)),
            ),
        ),
        compiler_params=PARAMS,
        cost_estimate=pl.CostEstimate(
            flops=2 * tokens * depth * columns * block,
            bytes_accessed=2 * depth * columns * block + 4 * tokens * depth,
            transcendentals=0,
        ),
        name="forward",
    )(flat, rows, x, arrived)


def forward_down(cotangent, arrived, flat, rows, columns, row_blocks):
    owners, tokens, width = cotangent.shape
    places, rows_each, block = arrived.shape
    keep = flat.shape[0] // columns
    hidden = columns * rows_each
    per_owner = row_blocks // owners

    def kernel(flat, rows, cotangent, arrived, out, dense):
        step = pl.program_id(0)

        @pl.when(step == 0)
        def _():
            dense[...] = jnp.zeros_like(dense)
            out[...] = jnp.zeros_like(out)
            for c in range(columns):

                def place(k, _):
                    row = rows[c * keep + k]
                    lane = pl.multiple_of((row % per_owner) * block, block)
                    dense[row // per_owner, c * rows_each : (c + 1) * rows_each, pl.ds(lane, block)] = (
                        arrived[flat[c * keep + k]]
                    )
                    return _

                lax.fori_loop(0, keep, place, 0, unroll=2)

        out[...] += lax.dot_general(dense[step], cotangent[0], NT, preferred_element_type=F32)

    return pl.pallas_call(
        kernel,
        out_shape=jax.ShapeDtypeStruct((hidden, tokens), F32),
        grid_spec=pltpu.PrefetchScalarGridSpec(
            num_scalar_prefetch=2,
            grid=(owners,),
            in_specs=[
                pl.BlockSpec((1, tokens, width), lambda g, f, r: (g, 0, 0)),
                whole((places, rows_each, block)),
            ],
            out_specs=whole((hidden, tokens)),
            scratch_shapes=[pltpu.VMEM((owners, hidden, width), BF16)],
        ),
        compiler_params=PARAMS,
        cost_estimate=pl.CostEstimate(
            flops=2 * tokens * hidden * owners * width,
            bytes_accessed=2 * tokens * owners * width,
            transcendentals=0,
        ),
        name="forward_down",
    )(flat, rows, cotangent, arrived)


def weight_grad(x_turned, grad, flat, rows, places, row_blocks, factor):
    quarters, columns, rows_each, tokens = grad.shape
    depth = x_turned.shape[0]
    block = quarters * rows_each
    keep = flat.shape[0] // columns

    def kernel(flat, rows, x_turned, grad, out, result):
        step = pl.program_id(0)
        right = jnp.concatenate(
            [grad[q, half] for half in range(2) for q in range(quarters)], axis=0
        )
        product = lax.dot_general(x_turned[...], right, NT, preferred_element_type=F32)
        result[...] = (product * factor).astype(BF16).reshape(result.shape)
        for half in range(2):
            base = (step * 2 + half) * keep
            lanes = slice(half * block, (half + 1) * block)

            def place(k, _):
                out[flat[base + k]] = result[rows[base + k], :, lanes]
                return _

            lax.fori_loop(0, keep, place, 0, unroll=2)

    return pl.pallas_call(
        kernel,
        out_shape=jax.ShapeDtypeStruct((places, rows_each, block), BF16),
        grid_spec=pltpu.PrefetchScalarGridSpec(
            num_scalar_prefetch=2,
            grid=(columns // 2,),
            in_specs=[
                whole((depth, tokens)),
                pl.BlockSpec((quarters, 2, rows_each, tokens), lambda g, f, r: (0, g, 0, 0)),
            ],
            out_specs=whole((places, rows_each, block)),
            scratch_shapes=[pltpu.VMEM((row_blocks, rows_each, 2 * block), BF16)],
        ),
        compiler_params=PARAMS,
        cost_estimate=pl.CostEstimate(
            flops=2 * tokens * depth * columns * block,
            bytes_accessed=4 * tokens * depth + 2 * places * rows_each * block,
            transcendentals=0,
        ),
        name="weight_grad",
    )(flat, rows, x_turned, grad)


def weight_grad_down(value, cotangent, flat, rows, places, block, columns, row_blocks, factor):
    owners, tokens, width = cotangent.shape
    hidden = value.shape[0]
    rows_each = hidden // columns
    keep = flat.shape[0] // columns
    per_owner = row_blocks // owners

    def kernel(flat, rows, value, cotangent, out, result):
        step = pl.program_id(0)
        product = jnp.dot(value[...], cotangent[0], preferred_element_type=F32)
        result[step] = (product * factor).astype(BF16)

        @pl.when(step == owners - 1)
        def _():
            for c in range(columns):

                def place(k, _):
                    row = rows[c * keep + k]
                    lane = pl.multiple_of((row % per_owner) * block, block)
                    out[flat[c * keep + k]] = result[
                        row // per_owner, c * rows_each : (c + 1) * rows_each, pl.ds(lane, block)
                    ]
                    return _

                lax.fori_loop(0, keep, place, 0, unroll=2)

    return pl.pallas_call(
        kernel,
        out_shape=jax.ShapeDtypeStruct((places, rows_each, block), BF16),
        grid_spec=pltpu.PrefetchScalarGridSpec(
            num_scalar_prefetch=2,
            grid=(owners,),
            in_specs=[
                whole((hidden, tokens)),
                pl.BlockSpec((1, tokens, width), lambda g, f, r: (g, 0, 0)),
            ],
            out_specs=whole((places, rows_each, block)),
            scratch_shapes=[pltpu.VMEM((owners, hidden, width), BF16)],
        ),
        compiler_params=PARAMS,
        cost_estimate=pl.CostEstimate(
            flops=2 * tokens * hidden * owners * width,
            bytes_accessed=2 * tokens * owners * width + 2 * places * rows_each * block,
            transcendentals=0,
        ),
        name="weight_grad_down",
    )(flat, rows, value, cotangent)


def unpack(which, returned, slots, counts, slot_count, total):
    places, rows_each, block = returned.shape
    owners = counts.shape[0]
    capacity = places // owners

    def kernel(slots, counts, returned, *refs):
        out = refs[-1]

        def one(owner, _):
            def place(p, _):
                index = owner * capacity + p
                out[0, slots[index]] = returned[index]
                return _

            return lax.fori_loop(0, counts[owner], place, _)

        lax.fori_loop(0, owners, one, 0)

    shape = (3, slot_count, rows_each, block)
    extra = [] if total is None else [total]
    return pl.pallas_call(
        kernel,
        out_shape=jax.ShapeDtypeStruct(shape, BF16),
        grid_spec=pltpu.PrefetchScalarGridSpec(
            num_scalar_prefetch=2,
            grid=(1,),
            in_specs=[whole((places, rows_each, block))]
            + [pl.BlockSpec(memory_space=pl.ANY)] * len(extra),
            out_specs=pl.BlockSpec((1,) + shape[1:], lambda g, s, c: (which, 0, 0, 0)),
        ),
        input_output_aliases={3: 0} if extra else {},
        compiler_params=PARAMS,
        cost_estimate=pl.CostEstimate(
            flops=0, bytes_accessed=4 * places * rows_each * block, transcendentals=0
        ),
        name="unpack",
    )(slots, counts, returned, *extra)


def silu_parts(gate, up_value, grad_act):
    sigmoid_g = jax.nn.sigmoid(gate)
    activated = gate * sigmoid_g
    value = (activated * up_value).astype(BF16)
    grad_gate = (grad_act * up_value * sigmoid_g * (1.0 + gate * (1.0 - sigmoid_g))).astype(BF16)
    grad_up = (grad_act * activated).astype(BF16)
    return (value, grad_gate, grad_up)


def per_device(inputs, out_grad, int_values, scales, block_rows, holder, slot_index):
    own_count = lax.axis_size("own")
    data_count = lax.axis_size("dp")
    own_index = lax.axis_index("own")
    data_index = lax.axis_index("dp")
    local_tokens, local_width = inputs.shape
    tokens = local_tokens * data_count
    slot_count = int_values.shape[1]
    block = int_values.shape[2]
    keep = block_rows.shape[2]
    width = local_width * own_count
    row_blocks = width // block
    columns = block_rows.shape[1] // own_count
    group = columns * keep
    active = 3 * own_count // 4
    capacity = (group + active - 1) // active
    places = own_count * capacity
    rows_each = block // data_count
    depth = row_blocks * rows_each
    hidden = columns * rows_each
    factor = 1.0 / math.sqrt(tokens)

    holder_group = holder.reshape(3, own_count, group)
    slot_group = slot_index.reshape(3, own_count, group)
    mine = (holder_group == own_index).astype(jnp.int32)
    rank = jnp.cumsum(mine, axis=2) - 1
    spots = jnp.arange(capacity, dtype=jnp.int32)
    picked = (mine[..., None] == 1) & (rank[..., None] == spots)
    bucket_slot = jnp.sum(jnp.where(picked, slot_group[..., None], 0), axis=2)
    bucket_slot = bucket_slot.reshape(3, places)
    bucket_used = jnp.sum(mine, axis=2)
    own_holder = lax.dynamic_index_in_dim(holder_group, own_index, 1, keepdims=False)
    entries = jnp.arange(group, dtype=jnp.int32)
    earlier = (own_holder[:, :, None] == own_holder[:, None, :]) & (
        entries[None, :, None] < entries[None, None, :]
    )
    position = jnp.sum(earlier.astype(jnp.int32), axis=1)
    flat = own_holder * capacity + position
    rows = lax.dynamic_index_in_dim(
        block_rows.reshape(3, own_count, group), own_index, 1, keepdims=False
    )
    quarter = data_index.astype(jnp.int32).reshape(1)

    def fetch(which):
        sending = pack(which, int_values, scales[which], bucket_slot[which], quarter, rows_each)
        sending = sending.reshape(own_count, capacity, rows_each, block)
        arrived = lax.all_to_all(sending, "own", split_axis=0, concat_axis=0, tiled=True)
        return arrived.reshape(places, rows_each, block)

    local = inputs.reshape(local_tokens, row_blocks // own_count, data_count, rows_each)
    local = local.transpose(2, 0, 1, 3).reshape(data_count, local_tokens, depth // own_count)
    local = lax.all_to_all(local, "dp", split_axis=0, concat_axis=0, tiled=True)
    gathered = lax.all_gather(local.reshape(tokens, depth // own_count), "own", axis=0)
    x = gathered.transpose(1, 0, 2).reshape(tokens, depth)
    x_turned = gathered.transpose(0, 2, 1).reshape(depth, tokens)
    cotangent = lax.all_gather(out_grad, "dp", axis=0, tiled=True)
    cotangent = lax.all_gather(cotangent, "own", axis=0)

    gate_weights, gate_part = forward(x, fetch(0), flat[0], rows[0], columns, row_blocks)
    gate = lax.psum_scatter(gate_part, "dp", scatter_dimension=0)
    up_weights, up_part = forward(x, fetch(1), flat[1], rows[1], columns, row_blocks)
    up_value = lax.psum_scatter(up_part, "dp", scatter_dimension=0)
    grad_act = forward_down(cotangent, fetch(2), flat[2], rows[2], columns, row_blocks)

    value, grad_gate, grad_up = silu_parts(
        gate.reshape(hidden, tokens).astype(F32), up_value.reshape(hidden, tokens).astype(F32), grad_act
    )
    shape = (columns, rows_each, tokens)
    all_gate = lax.all_gather(grad_gate.reshape(shape), "dp", axis=0)
    all_up = lax.all_gather(grad_up.reshape(shape), "dp", axis=0)

    def give_back(which, leaving, total):
        leaving = leaving.reshape(own_count, capacity, rows_each, block)
        returned = lax.all_to_all(leaving, "own", split_axis=0, concat_axis=0, tiled=True)
        returned = returned.reshape(places, rows_each, block)
        return unpack(which, returned, bucket_slot[which], bucket_used[which], slot_count, total)

    leaving_down = weight_grad_down(
        value, cotangent, flat[2], rows[2], places, block, columns, row_blocks, factor
    )
    total = give_back(2, leaving_down, None)
    leaving_gate = weight_grad(x_turned, all_gate, flat[0], rows[0], places, row_blocks, factor)
    total = give_back(0, leaving_gate, total)
    leaving_up = weight_grad(x_turned, all_up, flat[1], rows[1], places, row_blocks, factor)
    total = give_back(1, leaving_up, total)

    def natural(grad):
        return grad.transpose(1, 0, 2, 3).reshape(columns * block, tokens)

    back = jnp.dot(
        gate_weights.reshape(depth, columns * block), natural(all_gate), preferred_element_type=F32
    ) + jnp.dot(
        up_weights.reshape(depth, columns * block), natural(all_up), preferred_element_type=F32
    )
    back = back.astype(BF16).reshape(own_count, depth // own_count, tokens)
    back = lax.psum_scatter(back, "own", scatter_dimension=0)
    back = back.reshape(depth // own_count, data_count, local_tokens).transpose(1, 0, 2)
    back = lax.all_to_all(back, "dp", split_axis=0, concat_axis=0, tiled=True)
    back = back.reshape(data_count, row_blocks // own_count, rows_each, local_tokens)
    input_grad = back.transpose(3, 1, 0, 2).reshape(local_tokens, local_width)
    return (input_grad, total)


def solution(mesh):
    placed = (
        P("dp", "own"),
        P("dp", "own"),
        P(None, "own", None, None),
        P(None, "own"),
        P(),
        P(),
        P(),
    )
    return jax.shard_map(
        per_device,
        mesh=mesh,
        in_specs=placed,
        out_specs=(P("dp", "own"), P(None, "own", "dp", None)),
        check_vma=False,
    )
```

```python
import functools
import math

import jax
import jax.numpy as jnp
from jax import lax
from jax.experimental import pallas as pl
from jax.experimental.pallas import tpu as pltpu
from jax.sharding import PartitionSpec as P

F32 = jnp.float32
BF16 = jnp.bfloat16
NT = (((1,), (1,)), ((), ()))
PARAMS = pltpu.CompilerParams(vmem_limit_bytes=56 * 2**20)


def whole(shape):
    return pl.BlockSpec(shape, lambda *_: (0,) * len(shape))


def pack(which, ints, scales, slots, quarter, rows_each):
    slot_count, block = ints.shape[1], ints.shape[2]
    places = slots.shape[0]

    def kernel(slots, quarter, scales, ints, out):
        def place(index, _):
            slot = slots[index]
            out[index] = (ints[0, slot].astype(F32) * scales[slot]).astype(BF16)
            return _

        lax.fori_loop(0, places, place, 0, unroll=8)

    return pl.pallas_call(
        kernel,
        out_shape=jax.ShapeDtypeStruct((places, rows_each, block), BF16),
        grid_spec=pltpu.PrefetchScalarGridSpec(
            num_scalar_prefetch=3,
            grid=(1,),
            in_specs=[
                pl.BlockSpec(
                    (1, slot_count, rows_each, block), lambda g, s, q, c: (which, 0, q[0], 0)
                )
            ],
            out_specs=whole((places, rows_each, block)),
        ),
        compiler_params=PARAMS,
        cost_estimate=pl.CostEstimate(
            flops=places * rows_each * block * 2,
            bytes_accessed=4 * places * rows_each * block,
            transcendentals=0,
        ),
        name="pack",
    )(slots, quarter, scales, ints)


def forward(x, arrived, flat, rows, quarter, columns, row_blocks):
    places, rows_each, block = arrived.shape
    tokens, depth = x.shape
    keep = flat.shape[0] // columns
    quarters = block // rows_each

    def kernel(flat, rows, quarter, x, arrived, dense, *refs):
        outs, turned = refs[:-1], refs[-1]
        step = pl.program_id(0)
        dense[...] = jnp.zeros_like(dense)
        for half in range(2):
            base = (step * 2 + half) * keep
            lanes = slice(half * block, (half + 1) * block)

            def place(k, _):
                dense[rows[base + k], :, lanes] = arrived[flat[base + k]]
                return _

            lax.fori_loop(0, keep, place, 0, unroll=2)
        weights = dense[...].reshape(depth, 2 * block)
        result = jnp.dot(x[...], weights, preferred_element_type=F32)
        turned[...] = jnp.transpose(result).astype(BF16).reshape(turned.shape)
        for shift in range(quarters):
            wanted = lax.rem(quarter[0] + shift, quarters)
            for half in range(2):
                outs[shift][half] = turned[half, wanted]

    part = jax.ShapeDtypeStruct((columns, rows_each, tokens), BF16)
    part_spec = pl.BlockSpec((2, rows_each, tokens), lambda g, f, r, q: (g, 0, 0))
    dense, *parts = pl.pallas_call(
        kernel,
        out_shape=[jax.ShapeDtypeStruct((row_blocks, rows_each, columns * block), BF16)]
        + [part] * quarters,
        grid_spec=pltpu.PrefetchScalarGridSpec(
            num_scalar_prefetch=3,
            grid=(columns // 2,),
            in_specs=[whole((tokens, depth)), whole((places, rows_each, block))],
            out_specs=[
                pl.BlockSpec((row_blocks, rows_each, 2 * block), lambda g, f, r, q: (0, 0, g))
            ]
            + [part_spec] * quarters,
            scratch_shapes=[pltpu.VMEM((2, quarters, rows_each, tokens), BF16)],
        ),
        compiler_params=PARAMS,
        cost_estimate=pl.CostEstimate(
            flops=2 * tokens * depth * columns * block,
            bytes_accessed=2 * depth * columns * block + 4 * tokens * depth,
            transcendentals=0,
        ),
        name="forward",
    )(flat, rows, quarter, x, arrived)
    return dense, parts


def build_down(arrived, flat, rows, columns, row_blocks, owners):
    places, rows_each, block = arrived.shape
    keep = flat.shape[0] // columns
    hidden = columns * rows_each
    per_owner = row_blocks // owners
    shape = (owners, hidden, per_owner * block)

    def kernel(flat, rows, arrived, dense):
        dense[...] = jnp.zeros_like(dense)
        for c in range(columns):

            def place(k, _):
                row = rows[c * keep + k]
                lane = pl.multiple_of((row % per_owner) * block, block)
                dense[row // per_owner, c * rows_each : (c + 1) * rows_each, pl.ds(lane, block)] = (
                    arrived[flat[c * keep + k]]
                )
                return _

            lax.fori_loop(0, keep, place, 0, unroll=2)

    return pl.pallas_call(
        kernel,
        out_shape=jax.ShapeDtypeStruct(shape, BF16),
        grid_spec=pltpu.PrefetchScalarGridSpec(
            num_scalar_prefetch=2,
            grid=(1,),
            in_specs=[whole((places, rows_each, block))],
            out_specs=whole(shape),
        ),
        compiler_params=PARAMS,
        cost_estimate=pl.CostEstimate(
            flops=0, bytes_accessed=2 * math.prod(shape), transcendentals=0
        ),
        name="build_down",
    )(flat, rows, arrived)


def forward_down(cotangent, dense, part, total):
    owners, tokens, width = cotangent.shape
    hidden = dense.shape[1]
    parts = total[1]
    earlier = [] if total[0] is None else [total[0]]

    def kernel(part, cotangent, dense, *refs):
        out = refs[-1]

        @pl.when(pl.program_id(0) == 0)
        def _():
            out[...] = jnp.zeros_like(out)

        out[...] += lax.dot_general(dense[0], cotangent[0], NT, preferred_element_type=F32)

    return pl.pallas_call(
        kernel,
        out_shape=jax.ShapeDtypeStruct((hidden, parts * tokens), F32),
        grid_spec=pltpu.PrefetchScalarGridSpec(
            num_scalar_prefetch=1,
            grid=(owners,),
            in_specs=[
                pl.BlockSpec((1, tokens, width), lambda g, p: (g, 0, 0)),
                pl.BlockSpec((1, hidden, width), lambda g, p: (g, 0, 0)),
            ]
            + [pl.BlockSpec(memory_space=pl.ANY)] * len(earlier),
            out_specs=pl.BlockSpec((hidden, tokens), lambda g, p: (0, p[0])),
        ),
        input_output_aliases={3: 0} if earlier else {},
        compiler_params=PARAMS,
        cost_estimate=pl.CostEstimate(
            flops=2 * tokens * hidden * owners * width,
            bytes_accessed=2 * (tokens + hidden) * owners * width,
            transcendentals=0,
        ),
        name="forward_down",
    )(part, cotangent, dense, *earlier)


def weight_grad(x_turned, grads, flat, rows, quarter, places, row_blocks, factor):
    columns, rows_each, tokens = grads[0].shape
    depth = x_turned.shape[0]
    quarters = (len(grads) + 1) // 2
    block = quarters * rows_each
    keep = flat.shape[0] // columns

    def kernel(flat, rows, quarter, x_turned, *refs):
        parts, (out, natural, result) = refs[:-3], refs[-3:]
        step = pl.program_id(0)
        for half in range(2):
            natural[half, quarter[0]] = parts[0][half]
            for shift in range(1, quarters):
                at = lax.rem(quarter[0] + quarters - shift, quarters)
                natural[half, at] = parts[2 * shift - 1][half] + parts[2 * shift][half]
        right = natural[...].reshape(2 * block, tokens)
        product = lax.dot_general(x_turned[...], right, NT, preferred_element_type=F32)
        result[...] = (product * factor).astype(BF16).reshape(result.shape)
        for half in range(2):
            base = (step * 2 + half) * keep
            lanes = slice(half * block, (half + 1) * block)

            def place(k, _):
                out[flat[base + k]] = result[rows[base + k], :, lanes]
                return _

            lax.fori_loop(0, keep, place, 0, unroll=2)

    part_spec = pl.BlockSpec((2, rows_each, tokens), lambda g, f, r, q: (g, 0, 0))
    return pl.pallas_call(
        kernel,
        out_shape=(
            jax.ShapeDtypeStruct((places, rows_each, block), BF16),
            jax.ShapeDtypeStruct((columns, quarters, rows_each, tokens), BF16),
        ),
        grid_spec=pltpu.PrefetchScalarGridSpec(
            num_scalar_prefetch=3,
            grid=(columns // 2,),
            in_specs=[whole((depth, tokens))] + [part_spec] * len(grads),
            out_specs=(
                whole((places, rows_each, block)),
                pl.BlockSpec((2, quarters, rows_each, tokens), lambda g, f, r, q: (g, 0, 0, 0)),
            ),
            scratch_shapes=[pltpu.VMEM((row_blocks, rows_each, 2 * block), BF16)],
        ),
        compiler_params=PARAMS,
        cost_estimate=pl.CostEstimate(
            flops=2 * tokens * depth * columns * block,
            bytes_accessed=8 * tokens * depth + 2 * places * rows_each * block,
            transcendentals=0,
        ),
        name="weight_grad",
    )(flat, rows, quarter, x_turned, *grads)


def weight_grad_down(
    value, cotangents, flat, rows, quarter, places, block, columns, row_blocks, factor
):
    owners, tokens, width = cotangents[0].shape
    parts = len(cotangents)
    hidden = value.shape[0]
    rows_each = hidden // columns
    keep = flat.shape[0] // columns
    per_owner = row_blocks // owners

    def kernel(flat, rows, quarter, value, *refs):
        cotangents, (out, joined, result) = refs[:-3], refs[-3:]
        step = pl.program_id(0)
        for shift in range(parts):
            joined[lax.rem(quarter[0] + parts - shift, parts)] = cotangents[shift][0]
        right = joined[...].reshape(parts * tokens, width)
        product = jnp.dot(value[...], right, preferred_element_type=F32)
        result[step] = (product * factor).astype(BF16)

        @pl.when(step == owners - 1)
        def _():
            for c in range(columns):

                def place(k, _):
                    row = rows[c * keep + k]
                    lane = pl.multiple_of((row % per_owner) * block, block)
                    out[flat[c * keep + k]] = result[
                        row // per_owner, c * rows_each : (c + 1) * rows_each, pl.ds(lane, block)
                    ]
                    return _

                lax.fori_loop(0, keep, place, 0, unroll=2)

    part_spec = pl.BlockSpec((1, tokens, width), lambda g, f, r, q: (g, 0, 0))
    return pl.pallas_call(
        kernel,
        out_shape=jax.ShapeDtypeStruct((places, rows_each, block), BF16),
        grid_spec=pltpu.PrefetchScalarGridSpec(
            num_scalar_prefetch=3,
            grid=(owners,),
            in_specs=[whole((hidden, parts * tokens))] + [part_spec] * parts,
            out_specs=whole((places, rows_each, block)),
            scratch_shapes=[
                pltpu.VMEM((parts, tokens, width), BF16),
                pltpu.VMEM((owners, hidden, width), BF16),
            ],
        ),
        compiler_params=PARAMS,
        cost_estimate=pl.CostEstimate(
            flops=2 * parts * tokens * hidden * owners * width,
            bytes_accessed=2 * parts * tokens * owners * width + 2 * places * rows_each * block,
            transcendentals=0,
        ),
        name="weight_grad_down",
    )(flat, rows, quarter, value, *cotangents)


def unpack(which, returned, slots, counts, slot_count, total):
    places, rows_each, block = returned.shape
    owners = counts.shape[0]
    capacity = places // owners

    def kernel(slots, counts, returned, *refs):
        out = refs[-1]

        def one(owner, _):
            def place(p, _):
                index = owner * capacity + p
                out[0, slots[index]] = returned[index]
                return _

            return lax.fori_loop(0, counts[owner], place, _)

        lax.fori_loop(0, owners, one, 0)

    shape = (3, slot_count, rows_each, block)
    extra = [] if total is None else [total]
    return pl.pallas_call(
        kernel,
        out_shape=jax.ShapeDtypeStruct(shape, BF16),
        grid_spec=pltpu.PrefetchScalarGridSpec(
            num_scalar_prefetch=2,
            grid=(1,),
            in_specs=[whole((places, rows_each, block))]
            + [pl.BlockSpec(memory_space=pl.ANY)] * len(extra),
            out_specs=pl.BlockSpec((1,) + shape[1:], lambda g, s, c: (which, 0, 0, 0)),
        ),
        input_output_aliases={3: 0} if extra else {},
        compiler_params=PARAMS,
        cost_estimate=pl.CostEstimate(
            flops=0, bytes_accessed=4 * places * rows_each * block, transcendentals=0
        ),
        name="unpack",
    )(slots, counts, returned, *extra)


def silu_parts(gate, up_value, grad_act):
    sigmoid_g = jax.nn.sigmoid(gate)
    activated = gate * sigmoid_g
    value = (activated * up_value).astype(BF16)
    grad_gate = (grad_act * up_value * sigmoid_g * (1.0 + gate * (1.0 - sigmoid_g))).astype(BF16)
    grad_up = (grad_act * activated).astype(BF16)
    return (value, grad_gate, grad_up)


def per_device(inputs, out_grad, int_values, scales, block_rows, holder, slot_index):
    own_count = lax.axis_size("own")
    data_count = lax.axis_size("dp")
    own_index = lax.axis_index("own")
    data_index = lax.axis_index("dp")
    local_tokens, local_width = inputs.shape
    tokens = local_tokens * data_count
    slot_count = int_values.shape[1]
    block = int_values.shape[2]
    keep = block_rows.shape[2]
    width = local_width * own_count
    row_blocks = width // block
    columns = block_rows.shape[1] // own_count
    group = columns * keep
    active = 3 * own_count // 4
    capacity = (group + active - 1) // active
    places = own_count * capacity
    rows_each = block // data_count
    depth = row_blocks * rows_each
    hidden = columns * rows_each
    factor = 1.0 / math.sqrt(tokens)

    holder_group = holder.reshape(3, own_count, group)
    slot_group = slot_index.reshape(3, own_count, group)
    mine = (holder_group == own_index).astype(jnp.int32)
    rank = jnp.cumsum(mine, axis=2) - 1
    spots = jnp.arange(capacity, dtype=jnp.int32)
    picked = (mine[..., None] == 1) & (rank[..., None] == spots)
    bucket_slot = jnp.sum(jnp.where(picked, slot_group[..., None], 0), axis=2)
    bucket_slot = bucket_slot.reshape(3, places)
    bucket_used = jnp.sum(mine, axis=2)
    own_holder = lax.dynamic_index_in_dim(holder_group, own_index, 1, keepdims=False)
    entries = jnp.arange(group, dtype=jnp.int32)
    earlier = (own_holder[:, :, None] == own_holder[:, None, :]) & (
        entries[None, :, None] < entries[None, None, :]
    )
    position = jnp.sum(earlier.astype(jnp.int32), axis=1)
    flat = own_holder * capacity + position
    rows = lax.dynamic_index_in_dim(
        block_rows.reshape(3, own_count, group), own_index, 1, keepdims=False
    )
    quarter = data_index.astype(jnp.int32).reshape(1)

    def pass_on(value):
        up = [(i, i + 1) for i in range(data_count - 1)]
        down = [(i + 1, i) for i in range(data_count - 1)]
        above, below = [value], [value]
        for _ in range(1, data_count):
            below.append(lax.ppermute(below[-1], "dp", up))
            above.append(lax.ppermute(above[-1], "dp", down))
        return [(below[s], above[data_count - s]) for s in range(1, data_count)]

    def exchange(parts):
        kept = [parts[0]]
        for s in range(1, data_count):
            turn = [(i, (i + s) % data_count) for i in range(data_count)]
            kept.append(lax.ppermute(parts[s], "dp", turn))
        return kept

    def summed(parts):
        return sum(part.astype(F32) for part in parts).reshape(hidden, tokens)

    def send(which):
        sending = pack(which, int_values, scales[which], bucket_slot[which], quarter, rows_each)
        return sending.reshape(own_count, capacity, rows_each, block)

    def receive(sending):
        arrived = lax.all_to_all(sending, "own", split_axis=0, concat_axis=0, tiled=True)
        return arrived.reshape(places, rows_each, block)

    local = inputs.reshape(local_tokens, row_blocks // own_count, data_count, rows_each)
    local = local.transpose(2, 0, 1, 3).reshape(data_count, local_tokens, depth // own_count)
    local = lax.all_to_all(local, "dp", split_axis=0, concat_axis=0, tiled=True)
    local, cotangent_local = lax.optimization_barrier((local, out_grad))
    sending_gate, cotangent_passed = lax.optimization_barrier((send(0), cotangent_local))
    gathered = lax.all_gather(local.reshape(tokens, depth // own_count), "own", axis=0)

    cotangents = [lax.all_gather(cotangent_local, "own", axis=0)]
    for lower, upper in pass_on(cotangent_passed):
        cotangents.append(lax.all_gather(lower + upper, "own", axis=0))

    arrived_gate = receive(sending_gate)
    sending_up, sending_down = send(1), send(2)
    gathered, arrived_gate, sending_up, sending_down = lax.optimization_barrier(
        (gathered, arrived_gate, sending_up, sending_down)
    )
    x = gathered.transpose(1, 0, 2).reshape(tokens, depth)
    x_turned = gathered.transpose(0, 2, 1).reshape(depth, tokens)
    gate_weights, parts = forward(x, arrived_gate, flat[0], rows[0], quarter, columns, row_blocks)
    gate_parts = exchange(parts)
    arrived_up = receive(sending_up)
    up_weights, parts = forward(x, arrived_up, flat[1], rows[1], quarter, columns, row_blocks)
    up_parts = exchange(parts)
    down_weights = build_down(
        receive(sending_down), flat[2], rows[2], columns, row_blocks, own_count
    )
    grad_act = None
    for shift, cotangent in enumerate(cotangents):
        part = jnp.remainder(quarter - shift, data_count)
        grad_act = forward_down(cotangent, down_weights, part, (grad_act, data_count))

    value, grad_gate, grad_up = silu_parts(summed(gate_parts), summed(up_parts), grad_act)
    shape = (columns, rows_each, tokens)
    grad_gate, grad_up = grad_gate.reshape(shape), grad_up.reshape(shape)
    passed = pass_on(grad_up)
    all_up = [grad_up] + [part for pair in passed for part in pair]
    grad_gate, *all_up = lax.optimization_barrier((grad_gate, *all_up))
    passed = pass_on(grad_gate)
    all_gate = [grad_gate] + [part for pair in passed for part in pair]

    def give_back(which, leaving, total):
        leaving = leaving.reshape(own_count, capacity, rows_each, block)
        returned = lax.all_to_all(leaving, "own", split_axis=0, concat_axis=0, tiled=True)
        returned = returned.reshape(places, rows_each, block)
        return unpack(which, returned, bucket_slot[which], bucket_used[which], slot_count, total)

    leaving_down = weight_grad_down(
        value, cotangents, flat[2], rows[2], quarter, places, block, columns, row_blocks, factor
    )
    total = give_back(2, leaving_down, None)
    leaving_up, whole_up = weight_grad(
        x_turned, all_up, flat[1], rows[1], quarter, places, row_blocks, factor
    )
    total = give_back(1, leaving_up, total)
    leaving_gate, whole_gate = weight_grad(
        x_turned, all_gate, flat[0], rows[0], quarter, places, row_blocks, factor
    )
    total = give_back(0, leaving_gate, total)

    def through(weights, grad):
        return jnp.dot(
            weights.reshape(depth, columns * block),
            grad.reshape(columns * block, tokens),
            preferred_element_type=F32,
        )

    back = through(up_weights, whole_up) + through(gate_weights, whole_gate)
    back = back.astype(BF16).reshape(own_count, depth // own_count, tokens)
    back = lax.psum_scatter(back, "own", scatter_dimension=0)
    back = back.reshape(depth // own_count, data_count, local_tokens).transpose(1, 0, 2)
    back = lax.all_to_all(back, "dp", split_axis=0, concat_axis=0, tiled=True)
    back = back.reshape(data_count, row_blocks // own_count, rows_each, local_tokens)
    input_grad = back.transpose(3, 1, 0, 2).reshape(local_tokens, local_width)
    return (input_grad, total)


def solution(mesh):
    placed = (
        P("dp", "own"),
        P("dp", "own"),
        P(None, "own", None, None),
        P(None, "own"),
        P(),
        P(),
        P(),
    )
    return jax.shard_map(
        per_device,
        mesh=mesh,
        in_specs=placed,
        out_specs=(P("dp", "own"), P(None, "own", "dp", None)),
        check_vma=False,
    )
```

```python
import functools
import math

import jax
import jax.numpy as jnp
from jax import lax
from jax.experimental import pallas as pl
from jax.experimental.pallas import tpu as pltpu
from jax.sharding import PartitionSpec as P

F32 = jnp.float32
BF16 = jnp.bfloat16
NT = (((1,), (1,)), ((), ()))
COST = pl.CostEstimate(flops=1024, bytes_accessed=1024, transcendentals=0)
PARAMS = pltpu.CompilerParams(vmem_limit_bytes=56 * 2**20)


def whole(shape):
    return pl.BlockSpec(shape, lambda *_: (0,) * len(shape))


def waiting(after):
    return [pl.BlockSpec(memory_space=pl.ANY)] * len(after)


def mark(value):
    return value.reshape((-1,) + value.shape[-2:])[0, :16, :128]


def tie(value, *after):
    def kernel(*refs):
        pass

    return pl.pallas_call(
        kernel,
        out_shape=jax.ShapeDtypeStruct(value.shape, value.dtype),
        in_specs=waiting((value,) + after),
        out_specs=pl.BlockSpec(memory_space=pl.ANY),
        input_output_aliases={0: 0},
        compiler_params=PARAMS,
        name="tie",
    )(value, *after)


def pack(which, ints, scales, slots, quarter, rows_each, after=()):
    slot_count, block = ints.shape[1], ints.shape[2]
    places = slots.shape[0]

    def kernel(slots, quarter, scales, ints, *refs):
        out = refs[-1]

        def place(index, _):
            slot = slots[index]
            out[index] = (ints[0, slot].astype(F32) * scales[slot]).astype(BF16)
            return _

        lax.fori_loop(0, places, place, 0, unroll=8)

    return pl.pallas_call(
        kernel,
        out_shape=jax.ShapeDtypeStruct((places, rows_each, block), BF16),
        grid_spec=pltpu.PrefetchScalarGridSpec(
            num_scalar_prefetch=3,
            grid=(1,),
            in_specs=[
                pl.BlockSpec(
                    (1, slot_count, rows_each, block), lambda g, s, q, c: (which, 0, q[0], 0)
                )
            ]
            + waiting(after),
            out_specs=whole((places, rows_each, block)),
        ),
        compiler_params=PARAMS,
        cost_estimate=COST,
        name="pack",
    )(slots, quarter, scales, ints, *after)


def forward(x, arrived, flat, rows, columns, row_blocks):
    places, rows_each, block = arrived.shape
    tokens, depth = x.shape
    keep = flat.shape[0] // columns
    quarters = block // rows_each

    def kernel(flat, rows, x, arrived, dense, out):
        step = pl.program_id(0)
        dense[...] = jnp.zeros_like(dense)
        for half in range(2):
            base = (step * 2 + half) * keep
            lanes = slice(half * block, (half + 1) * block)

            def place(k, _):
                dense[rows[base + k], :, lanes] = arrived[flat[base + k]]
                return _

            lax.fori_loop(0, keep, place, 0, unroll=2)
        weights = dense[...].reshape(depth, 2 * block)
        result = jnp.dot(x[...], weights, preferred_element_type=F32)
        turned = jnp.transpose(result).astype(BF16)
        for half in range(2):
            for q in range(quarters):
                first = half * block + q * rows_each
                out[q, half] = turned[first : first + rows_each]

    return pl.pallas_call(
        kernel,
        out_shape=(
            jax.ShapeDtypeStruct((row_blocks, rows_each, columns * block), BF16),
            jax.ShapeDtypeStruct((quarters, columns, rows_each, tokens), BF16),
        ),
        grid_spec=pltpu.PrefetchScalarGridSpec(
            num_scalar_prefetch=2,
            grid=(columns // 2,),
            in_specs=[whole((tokens, depth)), whole((places, rows_each, block))],
            out_specs=(
                pl.BlockSpec((row_blocks, rows_each, 2 * block), lambda g, f, r: (0, 0, g)),
                pl.BlockSpec((quarters, 2, rows_each, tokens), lambda g, f, r: (0, g, 0, 0)),
            ),
        ),
        compiler_params=PARAMS,
        cost_estimate=COST,
        name="forward",
    )(flat, rows, x, arrived)


def forward_down(cotangents, arrived, flat, rows, first, columns, row_blocks):
    chips, tokens, width = cotangents[0].shape
    owners = 2 * chips
    places, rows_each, block = arrived.shape
    keep = flat.shape[0] // columns
    hidden = columns * rows_each
    per_owner = row_blocks // owners

    def kernel(flat, rows, first, mine, other, arrived, out, dense):
        step = pl.program_id(0)

        @pl.when(step == 0)
        def _():
            dense[...] = jnp.zeros_like(dense)
            out[...] = jnp.zeros_like(out)
            for c in range(columns):

                def place(k, _):
                    row = rows[c * keep + k]
                    lane = pl.multiple_of((row % per_owner) * block, block)
                    dense[row // per_owner, c * rows_each : (c + 1) * rows_each, pl.ds(lane, block)] = (
                        arrived[flat[c * keep + k]]
                    )
                    return _

                lax.fori_loop(0, keep, place, 0, unroll=2)

        for core, cotangent in enumerate((mine, other)):
            weights = dense[2 * step + lax.rem(first[0] + core, 2)]
            out[...] += lax.dot_general(weights, cotangent[0], NT, preferred_element_type=F32)

    share = pl.BlockSpec((1, tokens, width), lambda g, f, r, p: (g, 0, 0))
    return pl.pallas_call(
        kernel,
        out_shape=jax.ShapeDtypeStruct((hidden, tokens), F32),
        grid_spec=pltpu.PrefetchScalarGridSpec(
            num_scalar_prefetch=3,
            grid=(chips,),
            in_specs=[share, share, whole((places, rows_each, block))],
            out_specs=whole((hidden, tokens)),
            scratch_shapes=[pltpu.VMEM((owners, hidden, width), BF16)],
        ),
        compiler_params=PARAMS,
        cost_estimate=COST,
        name="forward_down",
    )(flat, rows, first, *cotangents, arrived)


def weight_grad(x_turned, grad, flat, rows, places, row_blocks, factor, after=()):
    quarters, columns, rows_each, tokens = grad.shape
    depth = x_turned.shape[0]
    block = quarters * rows_each
    keep = flat.shape[0] // columns

    def kernel(flat, rows, x_turned, grad, *refs):
        out, natural, result = refs[-3:]
        step = pl.program_id(0)
        for half in range(2):
            for q in range(quarters):
                natural[half, q] = grad[q, half]
        right = natural[...].reshape(2 * block, tokens)
        product = lax.dot_general(x_turned[...], right, NT, preferred_element_type=F32)
        result[...] = (product * factor).astype(BF16).reshape(result.shape)
        for half in range(2):
            base = (step * 2 + half) * keep
            lanes = slice(half * block, (half + 1) * block)

            def place(k, _):
                out[flat[base + k]] = result[rows[base + k], :, lanes]
                return _

            lax.fori_loop(0, keep, place, 0, unroll=2)

    return pl.pallas_call(
        kernel,
        out_shape=(
            jax.ShapeDtypeStruct((places, rows_each, block), BF16),
            jax.ShapeDtypeStruct((columns, quarters, rows_each, tokens), BF16),
        ),
        grid_spec=pltpu.PrefetchScalarGridSpec(
            num_scalar_prefetch=2,
            grid=(columns // 2,),
            in_specs=[
                whole((depth, tokens)),
                pl.BlockSpec((quarters, 2, rows_each, tokens), lambda g, f, r: (0, g, 0, 0)),
            ]
            + waiting(after),
            out_specs=(
                whole((places, rows_each, block)),
                pl.BlockSpec((2, quarters, rows_each, tokens), lambda g, f, r: (g, 0, 0, 0)),
            ),
            scratch_shapes=[pltpu.VMEM((row_blocks, rows_each, 2 * block), BF16)],
        ),
        compiler_params=PARAMS,
        cost_estimate=COST,
        name="weight_grad",
    )(flat, rows, x_turned, grad, *after)


def weight_grad_down(
    value, cotangents, flat, rows, first, places, block, columns, row_blocks, factor
):
    chips, tokens, width = cotangents[0].shape
    owners = 2 * chips
    hidden = value.shape[0]
    rows_each = hidden // columns
    keep = flat.shape[0] // columns
    per_owner = row_blocks // owners

    def kernel(flat, rows, first, value, mine, other, out, result):
        step = pl.program_id(0)
        for core, cotangent in enumerate((mine, other)):
            product = jnp.dot(value[...], cotangent[0], preferred_element_type=F32)
            result[2 * step + lax.rem(first[0] + core, 2)] = (product * factor).astype(BF16)

        @pl.when(step == chips - 1)
        def _():
            for c in range(columns):

                def place(k, _):
                    row = rows[c * keep + k]
                    lane = pl.multiple_of((row % per_owner) * block, block)
                    out[flat[c * keep + k]] = result[
                        row // per_owner, c * rows_each : (c + 1) * rows_each, pl.ds(lane, block)
                    ]
                    return _

                lax.fori_loop(0, keep, place, 0, unroll=2)

    share = pl.BlockSpec((1, tokens, width), lambda g, f, r, p: (g, 0, 0))
    return pl.pallas_call(
        kernel,
        out_shape=jax.ShapeDtypeStruct((places, rows_each, block), BF16),
        grid_spec=pltpu.PrefetchScalarGridSpec(
            num_scalar_prefetch=3,
            grid=(chips,),
            in_specs=[whole((hidden, tokens)), share, share],
            out_specs=whole((places, rows_each, block)),
            scratch_shapes=[pltpu.VMEM((owners, hidden, width), BF16)],
        ),
        compiler_params=PARAMS,
        cost_estimate=COST,
        name="weight_grad_down",
    )(flat, rows, first, value, *cotangents)


def unpack(which, returned, slots, counts, slot_count, total):
    places, rows_each, block = returned.shape
    owners = counts.shape[0]
    capacity = places // owners

    def kernel(slots, counts, returned, *refs):
        out = refs[-1]

        def one(owner, _):
            def place(p, _):
                index = owner * capacity + p
                out[0, slots[index]] = returned[index]
                return _

            return lax.fori_loop(0, counts[owner], place, _)

        lax.fori_loop(0, owners, one, 0)

    shape = (3, slot_count, rows_each, block)
    extra = [] if total is None else [total]
    return pl.pallas_call(
        kernel,
        out_shape=jax.ShapeDtypeStruct(shape, BF16),
        grid_spec=pltpu.PrefetchScalarGridSpec(
            num_scalar_prefetch=2,
            grid=(1,),
            in_specs=[whole((places, rows_each, block))]
            + [pl.BlockSpec(memory_space=pl.ANY)] * len(extra),
            out_specs=pl.BlockSpec((1,) + shape[1:], lambda g, s, c: (which, 0, 0, 0)),
        ),
        input_output_aliases={3: 0} if extra else {},
        compiler_params=PARAMS,
        cost_estimate=COST,
        name="unpack",
    )(slots, counts, returned, *extra)


def in_order(kept, quarter, after=()):
    count, shape = len(kept), kept[0].shape

    def kernel(quarter, *refs):
        for shift in range(count):
            refs[-1][lax.rem(quarter[0] + count - shift, count)] = refs[shift][...]

    return pl.pallas_call(
        kernel,
        out_shape=jax.ShapeDtypeStruct((count,) + shape, kept[0].dtype),
        grid_spec=pltpu.PrefetchScalarGridSpec(
            num_scalar_prefetch=1,
            grid=(1,),
            in_specs=[whole(shape)] * count + waiting(after),
            out_specs=whole((count,) + shape),
        ),
        compiler_params=PARAMS,
        cost_estimate=COST,
        name="in_order",
    )(quarter, *kept, *after)


def silu_parts(gate, up_value, grad_act):
    sigmoid_g = jax.nn.sigmoid(gate)
    activated = gate * sigmoid_g
    value = (activated * up_value).astype(BF16)
    grad_gate = (grad_act * up_value * sigmoid_g * (1.0 + gate * (1.0 - sigmoid_g))).astype(BF16)
    grad_up = (grad_act * activated).astype(BF16)
    return (value, grad_gate, grad_up)


def per_device(inputs, out_grad, int_values, scales, block_rows, holder, slot_index):
    own_count = lax.axis_size("own")
    data_count = lax.axis_size("dp")
    own_index = lax.axis_index("own")
    data_index = lax.axis_index("dp")
    local_tokens, local_width = inputs.shape
    tokens = local_tokens * data_count
    slot_count = int_values.shape[1]
    block = int_values.shape[2]
    keep = block_rows.shape[2]
    width = local_width * own_count
    row_blocks = width // block
    columns = block_rows.shape[1] // own_count
    group = columns * keep
    active = 3 * own_count // 4
    capacity = (group + active - 1) // active
    places = own_count * capacity
    rows_each = block // data_count
    depth = row_blocks * rows_each
    hidden = columns * rows_each
    factor = 1.0 / math.sqrt(tokens)

    holder_group = holder.reshape(3, own_count, group)
    slot_group = slot_index.reshape(3, own_count, group)
    mine = (holder_group == own_index).astype(jnp.int32)
    rank = jnp.cumsum(mine, axis=2) - 1
    spots = jnp.arange(capacity, dtype=jnp.int32)
    picked = (mine[..., None] == 1) & (rank[..., None] == spots)
    bucket_slot = jnp.sum(jnp.where(picked, slot_group[..., None], 0), axis=2)
    bucket_slot = bucket_slot.reshape(3, places)
    bucket_used = jnp.sum(mine, axis=2)
    own_holder = lax.dynamic_index_in_dim(holder_group, own_index, 1, keepdims=False)
    entries = jnp.arange(group, dtype=jnp.int32)
    earlier = (own_holder[:, :, None] == own_holder[:, None, :]) & (
        entries[None, :, None] < entries[None, None, :]
    )
    position = jnp.sum(earlier.astype(jnp.int32), axis=1)
    flat = own_holder * capacity + position
    rows = lax.dynamic_index_in_dim(
        block_rows.reshape(3, own_count, group), own_index, 1, keepdims=False
    )
    quarter = data_index.astype(jnp.int32).reshape(1)

    def exchange(parts):
        kept = [parts[0]]
        for s in range(1, data_count):
            turn = [(i, (i + s) % data_count) for i in range(data_count)]
            kept.append(lax.ppermute(parts[s], "dp", turn))
        return kept

    def send(which, after=()):
        sending = pack(
            which, int_values, scales[which], bucket_slot[which], quarter, rows_each, after
        )
        return sending.reshape(own_count, capacity, rows_each, block)

    def receive(sending):
        arrived = lax.all_to_all(sending, "own", split_axis=0, concat_axis=0, tiled=True)
        return arrived.reshape(places, rows_each, block)

    local = inputs.reshape(local_tokens, row_blocks // own_count, data_count, rows_each)
    local = local.transpose(2, 0, 1, 3).reshape(data_count, local_tokens, depth // own_count)
    twice = jnp.concatenate([local, local])
    local = exchange(
        [lax.dynamic_index_in_dim(twice, data_index + s, 0, keepdims=False) for s in range(data_count)]
    )
    cotangent = exchange([out_grad] * data_count)
    sending_gate = send(0)
    local = in_order(local, quarter, (mark(sending_gate),))
    gathered = lax.all_gather(local.reshape(tokens, depth // own_count), "own", axis=0)
    sending_up = send(1, (mark(local),))
    sending_down = send(2, (mark(sending_up),))
    arrived_gate = receive(sending_gate)
    chips = [[core + 2 * chip for chip in range(own_count // 2)] for core in range(2)]
    swap = [(i, i ^ 1) for i in range(own_count)]
    cotangent = lax.all_gather(
        in_order(cotangent, quarter, (mark(local),)).reshape(tokens, local_width), "own", axis=0, axis_index_groups=chips
    )
    core = jnp.remainder(own_index, 2).astype(jnp.int32).reshape(1)

    x = gathered.transpose(1, 0, 2).reshape(tokens, depth)
    x_turned = gathered.transpose(0, 2, 1).reshape(depth, tokens)
    gate_weights, part = forward(x, arrived_gate, flat[0], rows[0], columns, row_blocks)
    gate = lax.psum_scatter(part, "dp", scatter_dimension=0)
    arrived_up = receive(tie(sending_up, mark(gate_weights)))
    up_weights, part = forward(x, arrived_up, flat[1], rows[1], columns, row_blocks)
    up_value = lax.psum_scatter(part, "dp", scatter_dimension=0)
    cotangent = tie(cotangent, mark(up_weights))
    cotangents = (cotangent, lax.ppermute(cotangent, "own", swap))
    arrived_down = receive(tie(sending_down, mark(up_weights)))
    grad_act = forward_down(
        cotangents, arrived_down, flat[2], rows[2], core, columns, row_blocks
    )
    value, grad_gate, grad_up = silu_parts(
        gate.reshape(hidden, tokens).astype(F32), up_value.reshape(hidden, tokens).astype(F32), grad_act
    )
    shape = (columns, rows_each, tokens)

    def give_back(leaving):
        leaving = leaving.reshape(own_count, capacity, rows_each, block)
        returned = lax.all_to_all(leaving, "own", split_axis=0, concat_axis=0, tiled=True)
        return returned.reshape(places, rows_each, block)

    def keep_in(total, which, returned):
        return unpack(which, returned, bucket_slot[which], bucket_used[which], slot_count, total)

    def through(weights, grad):
        return jnp.dot(
            weights.reshape(depth, columns * block),
            grad.reshape(columns * block, tokens),
            preferred_element_type=F32,
        )

    all_up = lax.all_gather(grad_up.reshape(shape), "dp", axis=0)
    leaving_down = weight_grad_down(
        value, cotangents, flat[2], rows[2], core, places, block, columns, row_blocks, factor
    )
    grad_gate = tie(grad_gate, mark(leaving_down))
    returned_down = give_back(leaving_down)
    all_gate = lax.all_gather(grad_gate.reshape(shape), "dp", axis=0)
    leaving_up, whole_up = weight_grad(
        x_turned, all_up, flat[1], rows[1], places, row_blocks, factor
    )
    back_up = through(up_weights, whole_up)
    returned_up = give_back(leaving_up)
    leaving_gate, whole_gate = weight_grad(
        x_turned, all_gate, flat[0], rows[0], places, row_blocks, factor, (mark(returned_up), mark(back_up))
    )
    returned_gate = give_back(leaving_gate)
    total = keep_in(None, 2, returned_down)
    total = keep_in(total, 1, returned_up)
    total = keep_in(total, 0, returned_gate)

    back = back_up + through(gate_weights, whole_gate)
    back = back.astype(BF16).reshape(own_count, depth // own_count, tokens)
    back = lax.psum_scatter(back, "own", scatter_dimension=0)
    back = back.reshape(depth // own_count, data_count, local_tokens).transpose(1, 0, 2)
    back = lax.all_to_all(back, "dp", split_axis=0, concat_axis=0, tiled=True)
    back = back.reshape(data_count, row_blocks // own_count, rows_each, local_tokens)
    input_grad = back.transpose(3, 1, 0, 2).reshape(local_tokens, local_width)
    return (input_grad, total)


def solution(mesh):
    placed = (
        P("dp", "own"),
        P("dp", "own"),
        P(None, "own", None, None),
        P(None, "own"),
        P(),
        P(),
        P(),
    )
    return jax.shard_map(
        per_device,
        mesh=mesh,
        in_specs=placed,
        out_specs=(P("dp", "own"), P(None, "own", "dp", None)),
        check_vma=False,
    )
```

```python
import functools
import math

import jax
import jax.numpy as jnp
from jax import lax
from jax.experimental import pallas as pl
from jax.experimental.pallas import tpu as pltpu
from jax.sharding import PartitionSpec as P

F32 = jnp.float32
BF16 = jnp.bfloat16
NT = (((1,), (1,)), ((), ()))
COST = pl.CostEstimate(flops=1024, bytes_accessed=1024, transcendentals=0)
PARAMS = pltpu.CompilerParams(vmem_limit_bytes=56 * 2**20)


def whole(shape):
    return pl.BlockSpec(shape, lambda *_: (0,) * len(shape))


def waiting(after):
    return [pl.BlockSpec(memory_space=pl.ANY)] * len(after)


def mark(value):
    return value.reshape((-1,) + value.shape[-2:])[0, :16, :128]


def tie(value, *after):
    def kernel(*refs):
        pass

    return pl.pallas_call(
        kernel,
        out_shape=jax.ShapeDtypeStruct(value.shape, value.dtype),
        in_specs=waiting((value,) + after),
        out_specs=pl.BlockSpec(memory_space=pl.ANY),
        input_output_aliases={0: 0},
        compiler_params=PARAMS,
        name="tie",
    )(value, *after)


def pack(which, ints, scales, slots, quarter, rows_each, after=()):
    slot_count, block = ints.shape[1], ints.shape[2]
    places = slots.shape[0]

    def kernel(slots, quarter, scales, ints, *refs):
        out = refs[-1]

        def place(index, _):
            slot = slots[index]
            out[index] = (ints[0, slot].astype(F32) * scales[slot]).astype(BF16)
            return _

        lax.fori_loop(0, places, place, 0, unroll=8)

    return pl.pallas_call(
        kernel,
        out_shape=jax.ShapeDtypeStruct((places, rows_each, block), BF16),
        grid_spec=pltpu.PrefetchScalarGridSpec(
            num_scalar_prefetch=3,
            grid=(1,),
            in_specs=[
                pl.BlockSpec(
                    (1, slot_count, rows_each, block), lambda g, s, q, c: (which, 0, q[0], 0)
                )
            ]
            + waiting(after),
            out_specs=whole((places, rows_each, block)),
        ),
        compiler_params=PARAMS,
        cost_estimate=COST,
        name="pack",
    )(slots, quarter, scales, ints, *after)


def forward(x, arrived, flat, rows, columns, row_blocks, after=()):
    places, rows_each, block = arrived.shape
    tokens, depth = x.shape
    keep = flat.shape[0] // columns
    quarters = block // rows_each

    def kernel(flat, rows, x, arrived, *refs):
        dense, out = refs[-2:]
        step = pl.program_id(0)
        dense[...] = jnp.zeros_like(dense)
        for half in range(2):
            base = (step * 2 + half) * keep
            lanes = slice(half * block, (half + 1) * block)

            def place(k, _):
                dense[rows[base + k], :, lanes] = arrived[flat[base + k]]
                return _

            lax.fori_loop(0, keep, place, 0, unroll=2)
        weights = dense[...].reshape(depth, 2 * block)
        result = jnp.dot(x[...], weights, preferred_element_type=F32)
        turned = jnp.transpose(result).astype(BF16)
        for half in range(2):
            for q in range(quarters):
                first = half * block + q * rows_each
                out[q, half] = turned[first : first + rows_each]

    return pl.pallas_call(
        kernel,
        out_shape=(
            jax.ShapeDtypeStruct((row_blocks, rows_each, columns * block), BF16),
            jax.ShapeDtypeStruct((quarters, columns, rows_each, tokens), BF16),
        ),
        grid_spec=pltpu.PrefetchScalarGridSpec(
            num_scalar_prefetch=2,
            grid=(columns // 2,),
            in_specs=[whole((tokens, depth)), whole((places, rows_each, block))] + waiting(after),
            out_specs=(
                pl.BlockSpec((row_blocks, rows_each, 2 * block), lambda g, f, r: (0, 0, g)),
                pl.BlockSpec((quarters, 2, rows_each, tokens), lambda g, f, r: (0, g, 0, 0)),
            ),
        ),
        compiler_params=PARAMS,
        cost_estimate=COST,
        name="forward",
    )(flat, rows, x, arrived, *after)


def forward_down(cotangents, arrived, flat, rows, quarter, first, columns, row_blocks):
    (near, far), _ = cotangents
    chips, tokens, width = near.shape
    planes = far.shape[1] + 1
    owners = 2 * chips
    places, rows_each, block = arrived.shape
    keep = flat.shape[0] // columns
    hidden = columns * rows_each
    per_owner = row_blocks // owners

    def kernel(flat, rows, quarter, first, near, far, near_other, far_other, arrived, out, dense):
        step = pl.program_id(0)

        @pl.when(step == 0)
        def _():
            dense[...] = jnp.zeros_like(dense)
            out[...] = jnp.zeros_like(out)
            for c in range(columns):

                def place(k, _):
                    row = rows[c * keep + k]
                    lane = pl.multiple_of((row % per_owner) * block, block)
                    dense[row // per_owner, c * rows_each : (c + 1) * rows_each, pl.ds(lane, block)] = (
                        arrived[flat[c * keep + k]]
                    )
                    return _

                lax.fori_loop(0, keep, place, 0, unroll=2)

        for core, (own, others) in enumerate(((near, far), (near_other, far_other))):
            weights = dense[2 * step + lax.rem(first[0] + core, 2)]
            for shift in range(planes):
                cotangent = own[0] if shift == 0 else others[0, shift - 1]
                plane = lax.rem(quarter[0] + planes - shift, planes)
                lanes = pl.ds(pl.multiple_of(plane * tokens, tokens), tokens)
                out[:, lanes] += lax.dot_general(
                    weights, cotangent, NT, preferred_element_type=F32
                )

    share = [
        pl.BlockSpec((1, tokens, width), lambda g, *_: (g, 0, 0)),
        pl.BlockSpec((1, planes - 1, tokens, width), lambda g, *_: (g, 0, 0, 0)),
    ]
    return pl.pallas_call(
        kernel,
        out_shape=jax.ShapeDtypeStruct((hidden, planes * tokens), F32),
        grid_spec=pltpu.PrefetchScalarGridSpec(
            num_scalar_prefetch=4,
            grid=(chips,),
            in_specs=share + share + [whole((places, rows_each, block))],
            out_specs=whole((hidden, planes * tokens)),
            scratch_shapes=[pltpu.VMEM((owners, hidden, width), BF16)],
        ),
        compiler_params=PARAMS,
        cost_estimate=COST,
        name="forward_down",
    )(flat, rows, quarter, first, *cotangents[0], *cotangents[1], arrived)


def weight_grad(x_turned, grad, flat, rows, places, row_blocks, factor, after=()):
    quarters, columns, rows_each, tokens = grad.shape
    depth = x_turned.shape[0]
    block = quarters * rows_each
    keep = flat.shape[0] // columns

    def kernel(flat, rows, x_turned, grad, *refs):
        out, natural, result = refs[-3:]
        step = pl.program_id(0)
        for half in range(2):
            for q in range(quarters):
                natural[half, q] = grad[q, half]
        right = natural[...].reshape(2 * block, tokens)
        product = lax.dot_general(x_turned[...], right, NT, preferred_element_type=F32)
        result[...] = (product * factor).astype(BF16).reshape(result.shape)
        for half in range(2):
            base = (step * 2 + half) * keep
            lanes = slice(half * block, (half + 1) * block)

            def place(k, _):
                out[flat[base + k]] = result[rows[base + k], :, lanes]
                return _

            lax.fori_loop(0, keep, place, 0, unroll=2)

    return pl.pallas_call(
        kernel,
        out_shape=(
            jax.ShapeDtypeStruct((places, rows_each, block), BF16),
            jax.ShapeDtypeStruct((columns, quarters, rows_each, tokens), BF16),
        ),
        grid_spec=pltpu.PrefetchScalarGridSpec(
            num_scalar_prefetch=2,
            grid=(columns // 2,),
            in_specs=[
                whole((depth, tokens)),
                pl.BlockSpec((quarters, 2, rows_each, tokens), lambda g, f, r: (0, g, 0, 0)),
            ]
            + waiting(after),
            out_specs=(
                whole((places, rows_each, block)),
                pl.BlockSpec((2, quarters, rows_each, tokens), lambda g, f, r: (g, 0, 0, 0)),
            ),
            scratch_shapes=[pltpu.VMEM((row_blocks, rows_each, 2 * block), BF16)],
        ),
        compiler_params=PARAMS,
        cost_estimate=COST,
        name="weight_grad",
    )(flat, rows, x_turned, grad, *after)


def weight_grad_down(
    value, cotangents, flat, rows, quarter, first, places, block, columns, row_blocks, factor
):
    (near, far), _ = cotangents
    chips, tokens, width = near.shape
    planes = far.shape[1] + 1
    owners = 2 * chips
    hidden = value.shape[0]
    rows_each = hidden // columns
    keep = flat.shape[0] // columns
    per_owner = row_blocks // owners

    def kernel(
        flat, rows, quarter, first, value, near, far, near_other, far_other, out, joined, result
    ):
        step = pl.program_id(0)
        for core, (own, others) in enumerate(((near, far), (near_other, far_other))):
            for shift in range(planes):
                cotangent = own[0] if shift == 0 else others[0, shift - 1]
                joined[lax.rem(quarter[0] + planes - shift, planes)] = cotangent
            right = joined[...].reshape(planes * tokens, width)
            product = jnp.dot(value[...], right, preferred_element_type=F32)
            result[2 * step + lax.rem(first[0] + core, 2)] = (product * factor).astype(BF16)

        @pl.when(step == chips - 1)
        def _():
            for c in range(columns):

                def place(k, _):
                    row = rows[c * keep + k]
                    lane = pl.multiple_of((row % per_owner) * block, block)
                    out[flat[c * keep + k]] = result[
                        row // per_owner, c * rows_each : (c + 1) * rows_each, pl.ds(lane, block)
                    ]
                    return _

                lax.fori_loop(0, keep, place, 0, unroll=2)

    share = [
        pl.BlockSpec((1, tokens, width), lambda g, *_: (g, 0, 0)),
        pl.BlockSpec((1, planes - 1, tokens, width), lambda g, *_: (g, 0, 0, 0)),
    ]
    return pl.pallas_call(
        kernel,
        out_shape=jax.ShapeDtypeStruct((places, rows_each, block), BF16),
        grid_spec=pltpu.PrefetchScalarGridSpec(
            num_scalar_prefetch=4,
            grid=(chips,),
            in_specs=[whole((hidden, planes * tokens))] + share + share,
            out_specs=whole((places, rows_each, block)),
            scratch_shapes=[
                pltpu.VMEM((planes, tokens, width), BF16),
                pltpu.VMEM((owners, hidden, width), BF16),
            ],
        ),
        compiler_params=PARAMS,
        cost_estimate=COST,
        name="weight_grad_down",
    )(flat, rows, quarter, first, value, *cotangents[0], *cotangents[1])


def input_part(weights, grad, first, chips, earlier=()):
    depth, units = weights.shape
    tokens = grad.shape[1]
    rows = depth // (2 * chips)

    def kernel(first, left, right, grad, *refs):
        earlier, outs = refs[:-2], refs[-2:]
        both = jnp.concatenate([left[...], right[...]], axis=0)
        product = jnp.dot(both, grad[...], preferred_element_type=F32)
        for core in range(2):
            part = product[core * rows : (core + 1) * rows]
            if earlier:
                part = earlier[core][0] + part
            outs[core][0] = part.astype(outs[core].dtype)

    share = pl.BlockSpec((1, rows, tokens), lambda g, f: (g, 0, 0))
    out = jax.ShapeDtypeStruct((chips, rows, tokens), BF16 if earlier else F32)
    return pl.pallas_call(
        kernel,
        out_shape=(out, out),
        grid_spec=pltpu.PrefetchScalarGridSpec(
            num_scalar_prefetch=1,
            grid=(chips,),
            in_specs=[
                pl.BlockSpec((rows, units), lambda g, f: (2 * g + f[0], 0)),
                pl.BlockSpec((rows, units), lambda g, f: (2 * g + 1 - f[0], 0)),
                whole((units, tokens)),
            ]
            + [share] * len(earlier),
            out_specs=(share, share),
        ),
        compiler_params=PARAMS,
        cost_estimate=COST,
        name="input_part",
    )(first, weights, weights, grad, *earlier)


def unpack(which, returned, source, total):
    places, rows_each, block = returned.shape
    slot_count = source.shape[0]

    def kernel(source, returned, *refs):
        out = refs[-1]

        def place(slot, _):
            out[0, slot] = returned[source[slot]]
            return _

        lax.fori_loop(0, slot_count, place, 0, unroll=8)

    shape = (3, slot_count, rows_each, block)
    extra = [] if total is None else [total]
    return pl.pallas_call(
        kernel,
        out_shape=jax.ShapeDtypeStruct(shape, BF16),
        grid_spec=pltpu.PrefetchScalarGridSpec(
            num_scalar_prefetch=1,
            grid=(1,),
            in_specs=[whole((places, rows_each, block))] + waiting(extra),
            out_specs=pl.BlockSpec((1,) + shape[1:], lambda g, s: (which, 0, 0, 0)),
        ),
        input_output_aliases={2: 0} if extra else {},
        compiler_params=PARAMS,
        cost_estimate=COST,
        name="unpack",
    )(source, returned, *extra)


def in_order(kept, quarter, after=()):
    count, shape = len(kept), kept[0].shape

    def kernel(quarter, *refs):
        for shift in range(count):
            refs[-1][lax.rem(quarter[0] + count - shift, count)] = refs[shift][...]

    return pl.pallas_call(
        kernel,
        out_shape=jax.ShapeDtypeStruct((count,) + shape, kept[0].dtype),
        grid_spec=pltpu.PrefetchScalarGridSpec(
            num_scalar_prefetch=1,
            grid=(1,),
            in_specs=[whole(shape)] * count + waiting(after),
            out_specs=whole((count,) + shape),
        ),
        compiler_params=PARAMS,
        cost_estimate=COST,
        name="in_order",
    )(quarter, *kept, *after)


def silu_parts(gate, up_value, grad_act):
    sigmoid_g = jax.nn.sigmoid(gate)
    activated = gate * sigmoid_g
    value = (activated * up_value).astype(BF16)
    grad_gate = (grad_act * up_value * sigmoid_g * (1.0 + gate * (1.0 - sigmoid_g))).astype(BF16)
    grad_up = (grad_act * activated).astype(BF16)
    return (value, grad_gate, grad_up)


def per_device(inputs, out_grad, int_values, scales, block_rows, holder, slot_index):
    own_count = lax.axis_size("own")
    data_count = lax.axis_size("dp")
    own_index = lax.axis_index("own")
    data_index = lax.axis_index("dp")
    local_tokens, local_width = inputs.shape
    tokens = local_tokens * data_count
    slot_count = int_values.shape[1]
    block = int_values.shape[2]
    keep = block_rows.shape[2]
    width = local_width * own_count
    row_blocks = width // block
    columns = block_rows.shape[1] // own_count
    group = columns * keep
    active = 3 * own_count // 4
    capacity = (group + active - 1) // active
    places = own_count * capacity
    rows_each = block // data_count
    depth = row_blocks * rows_each
    hidden = columns * rows_each
    factor = 1.0 / math.sqrt(tokens)

    holder_group = holder.reshape(3, own_count, group)
    slot_group = slot_index.reshape(3, own_count, group)
    mine = (holder_group == own_index).astype(jnp.int32)
    rank = jnp.cumsum(mine, axis=2) - 1
    spots = jnp.arange(capacity, dtype=jnp.int32)
    picked = (mine[..., None] == 1) & (rank[..., None] == spots)
    bucket_slot = jnp.sum(jnp.where(picked, slot_group[..., None], 0), axis=2)
    used = spots < jnp.sum(mine, axis=2)[..., None]
    hits = used[..., None] & (bucket_slot[..., None] == jnp.arange(slot_count, dtype=jnp.int32))
    bucket_index = jnp.arange(places, dtype=jnp.int32).reshape(own_count, capacity)
    source = jnp.sum(jnp.where(hits, bucket_index[None, :, :, None], 0), axis=(1, 2))
    bucket_slot = bucket_slot.reshape(3, places)
    own_holder = lax.dynamic_index_in_dim(holder_group, own_index, 1, keepdims=False)
    entries = jnp.arange(group, dtype=jnp.int32)
    earlier = (own_holder[:, :, None] == own_holder[:, None, :]) & (
        entries[None, :, None] < entries[None, None, :]
    )
    position = jnp.sum(earlier.astype(jnp.int32), axis=1)
    flat = own_holder * capacity + position
    rows = lax.dynamic_index_in_dim(
        block_rows.reshape(3, own_count, group), own_index, 1, keepdims=False
    )
    quarter = data_index.astype(jnp.int32).reshape(1)

    def exchange(parts):
        kept = [parts[0]]
        for s in range(1, data_count):
            turn = [(i, (i + s) % data_count) for i in range(data_count)]
            kept.append(lax.ppermute(parts[s], "dp", turn))
        return kept

    def send(which, after=()):
        sending = pack(
            which, int_values, scales[which], bucket_slot[which], quarter, rows_each, after
        )
        return sending.reshape(own_count, capacity, rows_each, block)

    def receive(sending):
        arrived = lax.all_to_all(sending, "own", split_axis=0, concat_axis=0, tiled=True)
        return arrived.reshape(places, rows_each, block)

    chips = own_count // 2
    likes = [[core + 2 * chip for chip in range(chips)] for core in range(2)]
    swap = [(i, i ^ 1) for i in range(own_count)]
    core = jnp.remainder(own_index, 2).astype(jnp.int32).reshape(1)

    near = lax.all_gather(out_grad, "own", axis=0, axis_index_groups=likes)

    local = inputs.reshape(local_tokens, row_blocks // own_count, data_count, rows_each)
    local = local.transpose(2, 0, 1, 3).reshape(data_count, local_tokens, depth // own_count)
    twice = jnp.concatenate([local, local])
    local = exchange(
        [lax.dynamic_index_in_dim(twice, data_index + s, 0, keepdims=False) for s in range(data_count)]
    )
    local = in_order(local, quarter, (mark(near),))
    gathered = lax.all_gather(local.reshape(tokens, depth // own_count), "own", axis=0)
    sending_gate, sending_up, sending_down = send(0), send(1, (mark(local),)), send(2, (mark(local),))
    arrived_gate = receive(sending_gate)

    far = tie(jnp.stack(exchange([out_grad] * data_count)[1:]), mark(arrived_gate))
    far = lax.all_gather(far, "own", axis=0, axis_index_groups=likes)

    x = gathered.transpose(1, 0, 2).reshape(tokens, depth)
    x_turned = gathered.transpose(0, 2, 1).reshape(depth, tokens)
    packed = (mark(sending_up), mark(sending_down))
    gate_weights, part = forward(x, arrived_gate, flat[0], rows[0], columns, row_blocks, packed)
    gate = lax.psum_scatter(part, "dp", scatter_dimension=0)
    arrived_up = receive(tie(sending_up, mark(gate_weights)))
    up_weights, part = forward(x, arrived_up, flat[1], rows[1], columns, row_blocks)
    up_value = lax.psum_scatter(part, "dp", scatter_dimension=0)
    far = tie(far, mark(up_weights))
    cotangents = ((near, far), (lax.ppermute(near, "own", swap), lax.ppermute(far, "own", swap)))
    arrived_down = receive(tie(sending_down, mark(up_weights)))
    grad_act = forward_down(
        cotangents, arrived_down, flat[2], rows[2], quarter, core, columns, row_blocks
    )
    value, grad_gate, grad_up = silu_parts(
        gate.reshape(hidden, tokens).astype(F32), up_value.reshape(hidden, tokens).astype(F32), grad_act
    )
    shape = (columns, rows_each, tokens)

    def give_back(leaving):
        leaving = leaving.reshape(own_count, capacity, rows_each, block)
        returned = lax.all_to_all(leaving, "own", split_axis=0, concat_axis=0, tiled=True)
        return returned.reshape(places, rows_each, block)

    def natural(grad):
        return grad.reshape(columns * block, tokens)

    all_up = lax.all_gather(grad_up.reshape(shape), "dp", axis=0)
    leaving = weight_grad_down(
        value, cotangents, flat[2], rows[2], quarter, core, places, block, columns, row_blocks, factor
    )
    all_gate = lax.all_gather(grad_gate.reshape(shape), "dp", axis=0)
    returned = give_back(leaving)
    leaving, whole_up = weight_grad(
        x_turned, all_up, flat[1], rows[1], places, row_blocks, factor, (mark(returned),)
    )
    total = unpack(2, returned, source[2], None)
    returned = give_back(leaving)
    up_weights = up_weights.reshape(depth, columns * block)
    back = input_part(up_weights, natural(whole_up), core, chips)
    leaving, whole_gate = weight_grad(
        x_turned,
        all_gate,
        flat[0],
        rows[0],
        places,
        row_blocks,
        factor,
        (mark(returned), mark(back[0]), mark(total)),
    )
    total = unpack(1, returned, source[1], total)
    returned = give_back(leaving)

    gate_weights = gate_weights.reshape(depth, columns * block)
    back = input_part(gate_weights, natural(whole_gate), core, chips, back)
    back = back[0].astype(F32) + lax.ppermute(back[1], "own", swap).astype(F32)
    back = lax.psum_scatter(
        back.astype(BF16), "own", scatter_dimension=0, axis_index_groups=likes
    )
    back = back.reshape(depth // own_count, data_count, local_tokens).transpose(1, 0, 2)
    back = lax.all_to_all(back, "dp", split_axis=0, concat_axis=0, tiled=True)
    back = back.reshape(data_count, row_blocks // own_count, rows_each, local_tokens)
    input_grad = back.transpose(3, 1, 0, 2).reshape(local_tokens, local_width)
    total = unpack(0, returned, source[0], total)
    return (input_grad, total)


def solution(mesh):
    placed = (
        P("dp", "own"),
        P("dp", "own"),
        P(None, "own", None, None),
        P(None, "own"),
        P(),
        P(),
        P(),
    )
    return jax.shard_map(
        per_device,
        mesh=mesh,
        in_specs=placed,
        out_specs=(P("dp", "own"), P(None, "own", "dp", None)),
        check_vma=False,
    )
```

```python
import functools
import math

import jax
import jax.numpy as jnp
from jax import lax
from jax.experimental import pallas as pl
from jax.experimental.pallas import tpu as pltpu
from jax.sharding import PartitionSpec as P

F32 = jnp.float32
BF16 = jnp.bfloat16
NT = (((1,), (1,)), ((), ()))
COST = pl.CostEstimate(flops=1024, bytes_accessed=1024, transcendentals=0)
PARAMS = pltpu.CompilerParams(vmem_limit_bytes=56 * 2**20)


def whole(shape):
    return pl.BlockSpec(shape, lambda *_: (0,) * len(shape))


def waiting(after):
    return [pl.BlockSpec(memory_space=pl.ANY)] * len(after)


def mark(value):
    return value.reshape((-1,) + value.shape[-2:])[0, :16, :128]


def tie(value, *after):
    def kernel(*refs):
        pass

    return pl.pallas_call(
        kernel,
        out_shape=jax.ShapeDtypeStruct(value.shape, value.dtype),
        in_specs=waiting((value,) + after),
        out_specs=pl.BlockSpec(memory_space=pl.ANY),
        input_output_aliases={0: 0},
        compiler_params=PARAMS,
        name="tie",
    )(value, *after)


def pack(which, ints, scales, slots, quarter, rows_each, after=()):
    slot_count, block = ints.shape[1], ints.shape[2]
    places = slots.shape[0]

    def kernel(slots, quarter, scales, ints, *refs):
        out = refs[-1]

        def place(index, _):
            slot = slots[index]
            out[index] = (ints[0, slot].astype(F32) * scales[slot]).astype(BF16)
            return _

        lax.fori_loop(0, places, place, 0, unroll=8)

    return pl.pallas_call(
        kernel,
        out_shape=jax.ShapeDtypeStruct((places, rows_each, block), BF16),
        grid_spec=pltpu.PrefetchScalarGridSpec(
            num_scalar_prefetch=3,
            grid=(1,),
            in_specs=[
                pl.BlockSpec(
                    (1, slot_count, rows_each, block), lambda g, s, q, c: (which, 0, q[0], 0)
                )
            ]
            + waiting(after),
            out_specs=whole((places, rows_each, block)),
        ),
        compiler_params=PARAMS,
        cost_estimate=COST,
        name="pack",
    )(slots, quarter, scales, ints, *after)


def forward(x, arrived, flat, rows, columns, row_blocks, after=()):
    places, rows_each, block = arrived.shape
    tokens, depth = x.shape
    keep = flat.shape[0] // columns
    quarters = block // rows_each

    def kernel(flat, rows, x, arrived, *refs):
        dense, out = refs[-2:]
        step = pl.program_id(0)
        dense[...] = jnp.zeros_like(dense)
        for half in range(2):
            base = (step * 2 + half) * keep
            lanes = slice(half * block, (half + 1) * block)

            def place(k, _):
                dense[rows[base + k], :, lanes] = arrived[flat[base + k]]
                return _

            lax.fori_loop(0, keep, place, 0, unroll=2)
        weights = dense[...].reshape(depth, 2 * block)
        result = jnp.dot(x[...], weights, preferred_element_type=F32)
        turned = jnp.transpose(result).astype(BF16)
        for half in range(2):
            for q in range(quarters):
                first = half * block + q * rows_each
                out[q, half] = turned[first : first + rows_each]

    return pl.pallas_call(
        kernel,
        out_shape=(
            jax.ShapeDtypeStruct((row_blocks, rows_each, columns * block), BF16),
            jax.ShapeDtypeStruct((quarters, columns, rows_each, tokens), BF16),
        ),
        grid_spec=pltpu.PrefetchScalarGridSpec(
            num_scalar_prefetch=2,
            grid=(columns // 2,),
            in_specs=[whole((tokens, depth)), whole((places, rows_each, block))] + waiting(after),
            out_specs=(
                pl.BlockSpec((row_blocks, rows_each, 2 * block), lambda g, f, r: (0, 0, g)),
                pl.BlockSpec((quarters, 2, rows_each, tokens), lambda g, f, r: (0, g, 0, 0)),
            ),
        ),
        compiler_params=PARAMS,
        cost_estimate=COST,
        name="forward",
    )(flat, rows, x, arrived, *after)


def forward_down(cotangents, arrived, flat, rows, quarter, order, columns, row_blocks):
    (near, far), _ = cotangents
    chips, tokens, width = near.shape
    planes = far.shape[1] + 1
    owners = 2 * chips
    places, rows_each, block = arrived.shape
    keep = flat.shape[0] // columns
    hidden = columns * rows_each
    per_owner = row_blocks // owners

    def kernel(flat, rows, quarter, order, near, far, near_other, far_other, arrived, out, dense):
        step = pl.program_id(0)

        @pl.when(step == 0)
        def _():
            dense[...] = jnp.zeros_like(dense)
            out[...] = jnp.zeros_like(out)
            for c in range(columns):

                def place(k, _):
                    row = rows[c * keep + k]
                    lane = pl.multiple_of((row % per_owner) * block, block)
                    dense[row // per_owner, c * rows_each : (c + 1) * rows_each, pl.ds(lane, block)] = (
                        arrived[flat[c * keep + k]]
                    )
                    return _

                lax.fori_loop(0, keep, place, 0, unroll=2)

        for core, (own, others) in enumerate(((near, far), (near_other, far_other))):
            weights = dense[order[2 * step + core]]
            for shift in range(planes):
                cotangent = own[0] if shift == 0 else others[0, shift - 1]
                plane = lax.rem(quarter[0] + planes - shift, planes)
                lanes = pl.ds(pl.multiple_of(plane * tokens, tokens), tokens)
                out[:, lanes] += lax.dot_general(
                    weights, cotangent, NT, preferred_element_type=F32
                )

    share = [
        pl.BlockSpec((1, tokens, width), lambda g, f, r, q, o: (o[2 * g] // 2, 0, 0)),
        pl.BlockSpec((1, planes - 1, tokens, width), lambda g, *_: (g, 0, 0, 0)),
    ]
    return pl.pallas_call(
        kernel,
        out_shape=jax.ShapeDtypeStruct((hidden, planes * tokens), F32),
        grid_spec=pltpu.PrefetchScalarGridSpec(
            num_scalar_prefetch=4,
            grid=(chips,),
            in_specs=share + share + [whole((places, rows_each, block))],
            out_specs=whole((hidden, planes * tokens)),
            scratch_shapes=[pltpu.VMEM((owners, hidden, width), BF16)],
        ),
        compiler_params=PARAMS,
        cost_estimate=COST,
        name="forward_down",
    )(flat, rows, quarter, order, *cotangents[0], *cotangents[1], arrived)


def weight_grad(x_turned, grad, flat, rows, places, row_blocks, factor, after=()):
    quarters, columns, rows_each, tokens = grad.shape
    depth = x_turned.shape[0]
    block = quarters * rows_each
    keep = flat.shape[0] // columns

    def kernel(flat, rows, x_turned, grad, *refs):
        out, result = refs[-2:]
        step = pl.program_id(0)
        right = jnp.concatenate(
            [grad[q, half] for half in range(2) for q in range(quarters)], axis=0
        )
        product = lax.dot_general(x_turned[...], right, NT, preferred_element_type=F32)
        result[...] = (product * factor).astype(BF16).reshape(result.shape)
        for half in range(2):
            base = (step * 2 + half) * keep
            lanes = slice(half * block, (half + 1) * block)

            def place(k, _):
                out[flat[base + k]] = result[rows[base + k], :, lanes]
                return _

            lax.fori_loop(0, keep, place, 0, unroll=2)

    return pl.pallas_call(
        kernel,
        out_shape=jax.ShapeDtypeStruct((places, rows_each, block), BF16),
        grid_spec=pltpu.PrefetchScalarGridSpec(
            num_scalar_prefetch=2,
            grid=(columns // 2,),
            in_specs=[
                whole((depth, tokens)),
                pl.BlockSpec((quarters, 2, rows_each, tokens), lambda g, f, r: (0, g, 0, 0)),
            ]
            + waiting(after),
            out_specs=whole((places, rows_each, block)),
            scratch_shapes=[pltpu.VMEM((row_blocks, rows_each, 2 * block), BF16)],
        ),
        compiler_params=PARAMS,
        cost_estimate=COST,
        name="weight_grad",
    )(flat, rows, x_turned, grad, *after)


def weight_grad_down(
    value, cotangents, flat, rows, quarter, order, places, block, columns, row_blocks, factor
):
    (near, far), _ = cotangents
    chips, tokens, width = near.shape
    planes = far.shape[1] + 1
    owners = 2 * chips
    hidden = value.shape[0]
    rows_each = hidden // columns
    keep = flat.shape[0] // columns
    per_owner = row_blocks // owners

    def kernel(
        flat, rows, quarter, order, value, near, far, near_other, far_other, out, joined, result
    ):
        step = pl.program_id(0)
        for core, (own, others) in enumerate(((near, far), (near_other, far_other))):
            for shift in range(planes):
                cotangent = own[0] if shift == 0 else others[0, shift - 1]
                joined[lax.rem(quarter[0] + planes - shift, planes)] = cotangent
            right = joined[...].reshape(planes * tokens, width)
            product = jnp.dot(value[...], right, preferred_element_type=F32)
            result[order[2 * step + core]] = (product * factor).astype(BF16)

        @pl.when(step == chips - 1)
        def _():
            for c in range(columns):

                def place(k, _):
                    row = rows[c * keep + k]
                    lane = pl.multiple_of((row % per_owner) * block, block)
                    out[flat[c * keep + k]] = result[
                        row // per_owner, c * rows_each : (c + 1) * rows_each, pl.ds(lane, block)
                    ]
                    return _

                lax.fori_loop(0, keep, place, 0, unroll=2)

    share = [
        pl.BlockSpec((1, tokens, width), lambda g, f, r, q, o: (o[2 * g] // 2, 0, 0)),
        pl.BlockSpec((1, planes - 1, tokens, width), lambda g, *_: (g, 0, 0, 0)),
    ]
    return pl.pallas_call(
        kernel,
        out_shape=jax.ShapeDtypeStruct((places, rows_each, block), BF16),
        grid_spec=pltpu.PrefetchScalarGridSpec(
            num_scalar_prefetch=4,
            grid=(chips,),
            in_specs=[whole((hidden, planes * tokens))] + share + share,
            out_specs=whole((places, rows_each, block)),
            scratch_shapes=[
                pltpu.VMEM((planes, tokens, width), BF16),
                pltpu.VMEM((owners, hidden, width), BF16),
            ],
        ),
        compiler_params=PARAMS,
        cost_estimate=COST,
        name="weight_grad_down",
    )(flat, rows, quarter, order, value, *cotangents[0], *cotangents[1])


def input_part(weights, grad, first, chips, earlier=(), after=()):
    depth, units = weights.shape
    quarters, columns, rows_each, tokens = grad.shape
    rows = depth // (2 * chips)

    def kernel(first, left, right, grad, *refs):
        earlier, (*outs, natural) = refs[: len(refs) - len(after) - 3], refs[-3:]

        @pl.when(pl.program_id(0) == 0)
        def _():
            for c in range(columns):
                for q in range(quarters):
                    natural[c, q] = grad[q, c]

        both = jnp.concatenate([left[...], right[...]], axis=0)
        product = jnp.dot(
            both, natural[...].reshape(units, tokens), preferred_element_type=F32
        )
        for core in range(2):
            part = product[core * rows : (core + 1) * rows]
            if earlier:
                part = earlier[core][0] + part
            outs[core][0] = part.astype(outs[core].dtype)

    share = pl.BlockSpec((1, rows, tokens), lambda g, f: (g, 0, 0))
    out = jax.ShapeDtypeStruct((chips, rows, tokens), BF16 if earlier else F32)
    return pl.pallas_call(
        kernel,
        out_shape=(out, out),
        grid_spec=pltpu.PrefetchScalarGridSpec(
            num_scalar_prefetch=1,
            grid=(chips,),
            in_specs=[
                pl.BlockSpec((rows, units), lambda g, f: (2 * g + f[0], 0)),
                pl.BlockSpec((rows, units), lambda g, f: (2 * g + 1 - f[0], 0)),
                whole(grad.shape),
            ]
            + [share] * len(earlier)
            + waiting(after),
            out_specs=(share, share),
            scratch_shapes=[pltpu.VMEM((columns, quarters, rows_each, tokens), BF16)],
        ),
        compiler_params=PARAMS,
        cost_estimate=COST,
        name="input_part",
    )(first, weights, weights, grad, *earlier, *after)


def unpack(which, returned, source, total):
    places, rows_each, block = returned.shape
    slot_count = source.shape[0]

    def kernel(source, returned, *refs):
        out = refs[-1]

        def place(slot, _):
            out[0, slot] = returned[source[slot]]
            return _

        lax.fori_loop(0, slot_count, place, 0, unroll=8)

    shape = (3, slot_count, rows_each, block)
    extra = [] if total is None else [total]
    return pl.pallas_call(
        kernel,
        out_shape=jax.ShapeDtypeStruct(shape, BF16),
        grid_spec=pltpu.PrefetchScalarGridSpec(
            num_scalar_prefetch=1,
            grid=(1,),
            in_specs=[whole((places, rows_each, block))] + waiting(extra),
            out_specs=pl.BlockSpec((1,) + shape[1:], lambda g, s: (which, 0, 0, 0)),
        ),
        input_output_aliases={2: 0} if extra else {},
        compiler_params=PARAMS,
        cost_estimate=COST,
        name="unpack",
    )(source, returned, *extra)


def in_order(kept, quarter, after=()):
    count, shape = len(kept), kept[0].shape

    def kernel(quarter, *refs):
        for shift in range(count):
            refs[-1][lax.rem(quarter[0] + count - shift, count)] = refs[shift][...]

    return pl.pallas_call(
        kernel,
        out_shape=jax.ShapeDtypeStruct((count,) + shape, kept[0].dtype),
        grid_spec=pltpu.PrefetchScalarGridSpec(
            num_scalar_prefetch=1,
            grid=(1,),
            in_specs=[whole(shape)] * count + waiting(after),
            out_specs=whole((count,) + shape),
        ),
        compiler_params=PARAMS,
        cost_estimate=COST,
        name="in_order",
    )(quarter, *kept, *after)


def silu_parts(gate, up_value, grad_act):
    sigmoid_g = jax.nn.sigmoid(gate)
    activated = gate * sigmoid_g
    value = (activated * up_value).astype(BF16)
    grad_gate = (grad_act * up_value * sigmoid_g * (1.0 + gate * (1.0 - sigmoid_g))).astype(BF16)
    grad_up = (grad_act * activated).astype(BF16)
    return (value, grad_gate, grad_up)


def per_device(inputs, out_grad, int_values, scales, block_rows, holder, slot_index):
    own_count = lax.axis_size("own")
    data_count = lax.axis_size("dp")
    own_index = lax.axis_index("own")
    data_index = lax.axis_index("dp")
    local_tokens, local_width = inputs.shape
    tokens = local_tokens * data_count
    slot_count = int_values.shape[1]
    block = int_values.shape[2]
    keep = block_rows.shape[2]
    width = local_width * own_count
    row_blocks = width // block
    columns = block_rows.shape[1] // own_count
    group = columns * keep
    active = 3 * own_count // 4
    capacity = (group + active - 1) // active
    places = own_count * capacity
    rows_each = block // data_count
    depth = row_blocks * rows_each
    hidden = columns * rows_each
    factor = 1.0 / math.sqrt(tokens)

    holder_group = holder.reshape(3, own_count, group)
    slot_group = slot_index.reshape(3, own_count, group)
    mine = (holder_group == own_index).astype(jnp.int32)
    rank = jnp.cumsum(mine, axis=2) - 1
    spots = jnp.arange(capacity, dtype=jnp.int32)
    picked = (mine[..., None] == 1) & (rank[..., None] == spots)
    bucket_slot = jnp.sum(jnp.where(picked, slot_group[..., None], 0), axis=2)
    used = spots < jnp.sum(mine, axis=2)[..., None]
    hits = used[..., None] & (bucket_slot[..., None] == jnp.arange(slot_count, dtype=jnp.int32))
    bucket_index = jnp.arange(places, dtype=jnp.int32).reshape(own_count, capacity)
    source = jnp.sum(jnp.where(hits, bucket_index[None, :, :, None], 0), axis=(1, 2))
    bucket_slot = bucket_slot.reshape(3, places)
    own_holder = lax.dynamic_index_in_dim(holder_group, own_index, 1, keepdims=False)
    entries = jnp.arange(group, dtype=jnp.int32)
    earlier = (own_holder[:, :, None] == own_holder[:, None, :]) & (
        entries[None, :, None] < entries[None, None, :]
    )
    position = jnp.sum(earlier.astype(jnp.int32), axis=1)
    flat = own_holder * capacity + position
    rows = lax.dynamic_index_in_dim(
        block_rows.reshape(3, own_count, group), own_index, 1, keepdims=False
    )
    quarter = data_index.astype(jnp.int32).reshape(1)

    def exchange(parts):
        kept = [parts[0]]
        for s in range(1, data_count):
            turn = [(i, (i + s) % data_count) for i in range(data_count)]
            kept.append(lax.ppermute(parts[s], "dp", turn))
        return kept

    def send(which, after=()):
        sending = pack(
            which, int_values, scales[which], bucket_slot[which], quarter, rows_each, after
        )
        return sending.reshape(own_count, capacity, rows_each, block)

    def receive(sending):
        arrived = lax.all_to_all(sending, "own", split_axis=0, concat_axis=0, tiled=True)
        return arrived.reshape(places, rows_each, block)

    chips = own_count // 2
    likes = [[core + 2 * chip for chip in range(chips)] for core in range(2)]
    swap = [(i, i ^ 1) for i in range(own_count)]
    core = jnp.remainder(own_index, 2).astype(jnp.int32).reshape(1)
    turns = own_index ^ (2 * jnp.arange(chips, dtype=jnp.int32))
    order = jnp.stack([turns, turns ^ 1], axis=1).reshape(own_count)

    near = lax.all_gather(out_grad, "own", axis=0, axis_index_groups=likes)
    far = jnp.stack(exchange([out_grad] * data_count)[1:])

    local = inputs.reshape(local_tokens, row_blocks // own_count, data_count, rows_each)
    local = local.transpose(2, 0, 1, 3).reshape(data_count, local_tokens, depth // own_count)
    twice = jnp.concatenate([local, local])
    local = exchange(
        [lax.dynamic_index_in_dim(twice, data_index + s, 0, keepdims=False) for s in range(data_count)]
    )
    sending_gate = send(0)
    local = in_order(local, quarter, (mark(sending_gate), mark(far)))
    gathered = lax.all_gather(local.reshape(tokens, depth // own_count), "own", axis=0)
    sending_up, sending_down = send(1, (mark(local),)), send(2, (mark(local),))
    arrived_gate = receive(sending_gate)

    far = [tie(far, mark(arrived_gate))]
    for turn in range(1, chips):
        far.append(lax.ppermute(far[0], "own", [(i, i ^ (2 * turn)) for i in range(own_count)]))

    x = gathered.transpose(1, 0, 2).reshape(tokens, depth)
    x_turned = gathered.transpose(0, 2, 1).reshape(depth, tokens)
    packed = (mark(sending_up), mark(sending_down), mark(near))
    gate_weights, part = forward(x, arrived_gate, flat[0], rows[0], columns, row_blocks, packed)
    gate = lax.psum_scatter(part, "dp", scatter_dimension=0)
    arrived_up = receive(tie(sending_up, mark(gate_weights)))
    up_weights, part = forward(
        x, arrived_up, flat[1], rows[1], columns, row_blocks, (mark(gate),)
    )
    up_value = lax.psum_scatter(part, "dp", scatter_dimension=0)
    far = jnp.stack([tie(part, mark(up_weights)) for part in far])
    cotangents = ((near, far), (lax.ppermute(near, "own", swap), lax.ppermute(far, "own", swap)))
    arrived_down = receive(tie(sending_down, mark(arrived_up)))
    grad_act = forward_down(
        cotangents, arrived_down, flat[2], rows[2], quarter, order, columns, row_blocks
    )
    value, grad_gate, grad_up = silu_parts(
        gate.reshape(hidden, tokens).astype(F32), up_value.reshape(hidden, tokens).astype(F32), grad_act
    )
    shape = (columns, rows_each, tokens)

    def give_back(leaving):
        leaving = leaving.reshape(own_count, capacity, rows_each, block)
        returned = lax.all_to_all(leaving, "own", split_axis=0, concat_axis=0, tiled=True)
        return returned.reshape(places, rows_each, block)

    all_up = lax.all_gather(grad_up.reshape(shape), "dp", axis=0)
    leaving = weight_grad_down(
        value, cotangents, flat[2], rows[2], quarter, order, places, block, columns, row_blocks, factor
    )
    all_gate = lax.all_gather(grad_gate.reshape(shape), "dp", axis=0)
    returned = give_back(leaving)
    leaving = weight_grad(
        x_turned, all_up, flat[1], rows[1], places, row_blocks, factor, (mark(returned),)
    )
    total = unpack(2, returned, source[2], None)
    returned = give_back(leaving)

    up_weights = up_weights.reshape(depth, columns * block)
    gate_weights = gate_weights.reshape(depth, columns * block)
    back = input_part(up_weights, all_up, core, chips, after=(mark(leaving),))
    back = input_part(gate_weights, all_gate, core, chips, back, (mark(returned), mark(total)))
    leaving = weight_grad(
        x_turned, all_gate, flat[0], rows[0], places, row_blocks, factor, (mark(back[0]),)
    )
    total = unpack(1, returned, source[1], total)
    returned = give_back(leaving)

    back = back[0].astype(F32) + lax.ppermute(back[1], "own", swap).astype(F32)
    back = lax.psum_scatter(
        back.astype(BF16), "own", scatter_dimension=0, axis_index_groups=likes
    )
    back = back.reshape(depth // own_count, data_count, local_tokens).transpose(1, 0, 2)
    back = tie(back, mark(total))
    back = lax.all_to_all(back, "dp", split_axis=0, concat_axis=0, tiled=True)
    back = back.reshape(data_count, row_blocks // own_count, rows_each, local_tokens)
    input_grad = back.transpose(3, 1, 0, 2).reshape(local_tokens, local_width)
    total = unpack(0, returned, source[0], total)
    return (input_grad, total)


def solution(mesh):
    placed = (
        P("dp", "own"),
        P("dp", "own"),
        P(None, "own", None, None),
        P(None, "own"),
        P(),
        P(),
        P(),
    )
    return jax.shard_map(
        per_device,
        mesh=mesh,
        in_specs=placed,
        out_specs=(P("dp", "own"), P(None, "own", "dp", None)),
        check_vma=False,
    )
```

```python
import functools
import math

import jax
import jax.numpy as jnp
from jax import lax
from jax.experimental import pallas as pl
from jax.experimental.pallas import tpu as pltpu
from jax.sharding import PartitionSpec as P

F32 = jnp.float32
BF16 = jnp.bfloat16
NT = (((1,), (1,)), ((), ()))
COST = pl.CostEstimate(flops=1024, bytes_accessed=1024, transcendentals=0)
PARAMS = pltpu.CompilerParams(vmem_limit_bytes=56 * 2**20)


def whole(shape):
    return pl.BlockSpec(shape, lambda *_: (0,) * len(shape))


def waiting(after):
    return [pl.BlockSpec(memory_space=pl.ANY)] * len(after)


def mark(value):
    return value.reshape((-1,) + value.shape[-2:])[0, :16, :128]


def tie(value, *after):
    def kernel(*refs):
        pass

    return pl.pallas_call(
        kernel,
        out_shape=jax.ShapeDtypeStruct(value.shape, value.dtype),
        in_specs=waiting((value,) + after),
        out_specs=pl.BlockSpec(memory_space=pl.ANY),
        input_output_aliases={0: 0},
        compiler_params=PARAMS,
        name="tie",
    )(value, *after)


def pack(which, ints, scales, slots, quarter, rows_each, after=()):
    slot_count, block = ints.shape[1], ints.shape[2]
    places = slots.shape[0]

    def kernel(slots, quarter, scales, ints, *refs):
        out = refs[-1]

        def place(index, _):
            slot = slots[index]
            out[index] = (ints[0, slot].astype(F32) * scales[slot]).astype(BF16)
            return _

        lax.fori_loop(0, places, place, 0, unroll=8)

    return pl.pallas_call(
        kernel,
        out_shape=jax.ShapeDtypeStruct((places, rows_each, block), BF16),
        grid_spec=pltpu.PrefetchScalarGridSpec(
            num_scalar_prefetch=3,
            grid=(1,),
            in_specs=[
                pl.BlockSpec(
                    (1, slot_count, rows_each, block), lambda g, s, q, c: (which, 0, q[0], 0)
                )
            ]
            + waiting(after),
            out_specs=whole((places, rows_each, block)),
        ),
        compiler_params=PARAMS,
        cost_estimate=COST,
        name="pack",
    )(slots, quarter, scales, ints, *after)


def forward(x, arrived, flat, rows, columns, row_blocks, after=()):
    places, rows_each, block = arrived.shape
    tokens, depth = x.shape
    keep = flat.shape[0] // columns
    quarters = block // rows_each

    def kernel(flat, rows, x, arrived, *refs):
        dense, out = refs[-2:]
        step = pl.program_id(0)
        dense[...] = jnp.zeros_like(dense)
        for half in range(2):
            base = (step * 2 + half) * keep
            lanes = slice(half * block, (half + 1) * block)

            def place(k, _):
                dense[rows[base + k], :, lanes] = arrived[flat[base + k]]
                return _

            lax.fori_loop(0, keep, place, 0, unroll=2)
        weights = dense[...].reshape(depth, 2 * block)
        result = jnp.dot(x[...], weights, preferred_element_type=F32)
        turned = jnp.transpose(result).astype(BF16)
        for half in range(2):
            for q in range(quarters):
                first = half * block + q * rows_each
                out[q, half] = turned[first : first + rows_each]

    return pl.pallas_call(
        kernel,
        out_shape=(
            jax.ShapeDtypeStruct((row_blocks, rows_each, columns * block), BF16),
            jax.ShapeDtypeStruct((quarters, columns, rows_each, tokens), BF16),
        ),
        grid_spec=pltpu.PrefetchScalarGridSpec(
            num_scalar_prefetch=2,
            grid=(columns // 2,),
            in_specs=[whole((tokens, depth)), whole((places, rows_each, block))] + waiting(after),
            out_specs=(
                pl.BlockSpec((row_blocks, rows_each, 2 * block), lambda g, f, r: (0, 0, g)),
                pl.BlockSpec((quarters, 2, rows_each, tokens), lambda g, f, r: (0, g, 0, 0)),
            ),
        ),
        compiler_params=PARAMS,
        cost_estimate=COST,
        name="forward",
    )(flat, rows, x, arrived, *after)


def forward_down(cotangents, arrived, flat, rows, quarter, order, columns, row_blocks):
    (near, far), _ = cotangents
    chips, tokens, width = near.shape
    planes = far.shape[1] + 1
    owners = 2 * chips
    places, rows_each, block = arrived.shape
    keep = flat.shape[0] // columns
    hidden = columns * rows_each
    per_owner = row_blocks // owners

    def kernel(flat, rows, quarter, order, near, far, near_other, far_other, arrived, out, dense):
        step = pl.program_id(0)

        @pl.when(step == 0)
        def _():
            dense[...] = jnp.zeros_like(dense)
            out[...] = jnp.zeros_like(out)
            for c in range(columns):

                def place(k, _):
                    row = rows[c * keep + k]
                    lane = pl.multiple_of((row % per_owner) * block, block)
                    dense[row // per_owner, c * rows_each : (c + 1) * rows_each, pl.ds(lane, block)] = (
                        arrived[flat[c * keep + k]]
                    )
                    return _

                lax.fori_loop(0, keep, place, 0, unroll=2)

        for core, (own, others) in enumerate(((near, far), (near_other, far_other))):
            weights = dense[order[2 * step + core]]
            for shift in range(planes):
                cotangent = own[0] if shift == 0 else others[0, shift - 1]
                plane = lax.rem(quarter[0] + planes - shift, planes)
                lanes = pl.ds(pl.multiple_of(plane * tokens, tokens), tokens)
                out[:, lanes] += lax.dot_general(
                    weights, cotangent, NT, preferred_element_type=F32
                )

    share = [
        pl.BlockSpec((1, tokens, width), lambda g, f, r, q, o: (o[2 * g] // 2, 0, 0)),
        pl.BlockSpec((1, planes - 1, tokens, width), lambda g, *_: (g, 0, 0, 0)),
    ]
    return pl.pallas_call(
        kernel,
        out_shape=jax.ShapeDtypeStruct((hidden, planes * tokens), F32),
        grid_spec=pltpu.PrefetchScalarGridSpec(
            num_scalar_prefetch=4,
            grid=(chips,),
            in_specs=share + share + [whole((places, rows_each, block))],
            out_specs=whole((hidden, planes * tokens)),
            scratch_shapes=[pltpu.VMEM((owners, hidden, width), BF16)],
        ),
        compiler_params=PARAMS,
        cost_estimate=COST,
        name="forward_down",
    )(flat, rows, quarter, order, *cotangents[0], *cotangents[1], arrived)


def weight_grad(x_turned, grad, flat, rows, places, row_blocks, factor, after=()):
    quarters, columns, rows_each, tokens = grad.shape
    depth = x_turned.shape[0]
    block = quarters * rows_each
    keep = flat.shape[0] // columns

    def kernel(flat, rows, x_turned, grad, *refs):
        out, result = refs[-2:]
        step = pl.program_id(0)
        right = jnp.concatenate(
            [grad[q, half] for half in range(2) for q in range(quarters)], axis=0
        )
        product = lax.dot_general(x_turned[...], right, NT, preferred_element_type=F32)
        result[...] = (product * factor).astype(BF16).reshape(result.shape)
        for half in range(2):
            base = (step * 2 + half) * keep
            lanes = slice(half * block, (half + 1) * block)

            def place(k, _):
                out[flat[base + k]] = result[rows[base + k], :, lanes]
                return _

            lax.fori_loop(0, keep, place, 0, unroll=2)

    return pl.pallas_call(
        kernel,
        out_shape=jax.ShapeDtypeStruct((places, rows_each, block), BF16),
        grid_spec=pltpu.PrefetchScalarGridSpec(
            num_scalar_prefetch=2,
            grid=(columns // 2,),
            in_specs=[
                whole((depth, tokens)),
                pl.BlockSpec((quarters, 2, rows_each, tokens), lambda g, f, r: (0, g, 0, 0)),
            ]
            + waiting(after),
            out_specs=whole((places, rows_each, block)),
            scratch_shapes=[pltpu.VMEM((row_blocks, rows_each, 2 * block), BF16)],
        ),
        compiler_params=PARAMS,
        cost_estimate=COST,
        name="weight_grad",
    )(flat, rows, x_turned, grad, *after)


def weight_grad_down(
    value, cotangents, flat, rows, quarter, order, places, block, columns, row_blocks, factor
):
    (near, far), _ = cotangents
    chips, tokens, width = near.shape
    planes = far.shape[1] + 1
    owners = 2 * chips
    hidden = value.shape[0]
    rows_each = hidden // columns
    keep = flat.shape[0] // columns
    per_owner = row_blocks // owners

    def kernel(
        flat, rows, quarter, order, value, near, far, near_other, far_other, out, joined, result
    ):
        step = pl.program_id(0)
        for core, (own, others) in enumerate(((near, far), (near_other, far_other))):
            for shift in range(planes):
                cotangent = own[0] if shift == 0 else others[0, shift - 1]
                joined[lax.rem(quarter[0] + planes - shift, planes)] = cotangent
            right = joined[...].reshape(planes * tokens, width)
            product = jnp.dot(value[...], right, preferred_element_type=F32)
            result[order[2 * step + core]] = (product * factor).astype(BF16)

        @pl.when(step == chips - 1)
        def _():
            for c in range(columns):

                def place(k, _):
                    row = rows[c * keep + k]
                    lane = pl.multiple_of((row % per_owner) * block, block)
                    out[flat[c * keep + k]] = result[
                        row // per_owner, c * rows_each : (c + 1) * rows_each, pl.ds(lane, block)
                    ]
                    return _

                lax.fori_loop(0, keep, place, 0, unroll=2)

    share = [
        pl.BlockSpec((1, tokens, width), lambda g, f, r, q, o: (o[2 * g] // 2, 0, 0)),
        pl.BlockSpec((1, planes - 1, tokens, width), lambda g, *_: (g, 0, 0, 0)),
    ]
    return pl.pallas_call(
        kernel,
        out_shape=jax.ShapeDtypeStruct((places, rows_each, block), BF16),
        grid_spec=pltpu.PrefetchScalarGridSpec(
            num_scalar_prefetch=4,
            grid=(chips,),
            in_specs=[whole((hidden, planes * tokens))] + share + share,
            out_specs=whole((places, rows_each, block)),
            scratch_shapes=[
                pltpu.VMEM((planes, tokens, width), BF16),
                pltpu.VMEM((owners, hidden, width), BF16),
            ],
        ),
        compiler_params=PARAMS,
        cost_estimate=COST,
        name="weight_grad_down",
    )(flat, rows, quarter, order, value, *cotangents[0], *cotangents[1])


def input_part(weights, grad, first, chips, earlier=(), after=()):
    depth, units = weights.shape
    quarters, columns, rows_each, tokens = grad.shape
    rows = depth // (2 * chips)

    def kernel(first, left, right, grad, *refs):
        earlier, (*outs, natural) = refs[: len(refs) - len(after) - 3], refs[-3:]

        @pl.when(pl.program_id(0) == 0)
        def _():
            for c in range(columns):
                for q in range(quarters):
                    natural[c, q] = grad[q, c]

        both = jnp.concatenate([left[...], right[...]], axis=0)
        product = jnp.dot(
            both, natural[...].reshape(units, tokens), preferred_element_type=F32
        )
        for core in range(2):
            part = product[core * rows : (core + 1) * rows]
            if earlier:
                part = earlier[core][0] + part
            outs[core][0] = part.astype(outs[core].dtype)

    share = pl.BlockSpec((1, rows, tokens), lambda g, f: (g, 0, 0))
    out = jax.ShapeDtypeStruct((chips, rows, tokens), BF16 if earlier else F32)
    return pl.pallas_call(
        kernel,
        out_shape=(out, out),
        grid_spec=pltpu.PrefetchScalarGridSpec(
            num_scalar_prefetch=1,
            grid=(chips,),
            in_specs=[
                pl.BlockSpec((rows, units), lambda g, f: (2 * g + f[0], 0)),
                pl.BlockSpec((rows, units), lambda g, f: (2 * g + 1 - f[0], 0)),
                whole(grad.shape),
            ]
            + [share] * len(earlier)
            + waiting(after),
            out_specs=(share, share),
            scratch_shapes=[pltpu.VMEM((columns, quarters, rows_each, tokens), BF16)],
        ),
        compiler_params=PARAMS,
        cost_estimate=COST,
        name="input_part",
    )(first, weights, weights, grad, *earlier, *after)


def unpack(which, returned, source, total):
    places, rows_each, block = returned.shape
    slot_count = source.shape[0]

    def kernel(source, returned, *refs):
        out = refs[-1]

        def place(slot, _):
            out[0, slot] = returned[source[slot]]
            return _

        lax.fori_loop(0, slot_count, place, 0, unroll=8)

    shape = (3, slot_count, rows_each, block)
    extra = [] if total is None else [total]
    return pl.pallas_call(
        kernel,
        out_shape=jax.ShapeDtypeStruct(shape, BF16),
        grid_spec=pltpu.PrefetchScalarGridSpec(
            num_scalar_prefetch=1,
            grid=(1,),
            in_specs=[whole((places, rows_each, block))] + waiting(extra),
            out_specs=pl.BlockSpec((1,) + shape[1:], lambda g, s: (which, 0, 0, 0)),
        ),
        input_output_aliases={2: 0} if extra else {},
        compiler_params=PARAMS,
        cost_estimate=COST,
        name="unpack",
    )(source, returned, *extra)


def in_order(kept, quarter, after=()):
    count, shape = len(kept), kept[0].shape

    def kernel(quarter, *refs):
        for shift in range(count):
            refs[-1][lax.rem(quarter[0] + count - shift, count)] = refs[shift][...]

    return pl.pallas_call(
        kernel,
        out_shape=jax.ShapeDtypeStruct((count,) + shape, kept[0].dtype),
        grid_spec=pltpu.PrefetchScalarGridSpec(
            num_scalar_prefetch=1,
            grid=(1,),
            in_specs=[whole(shape)] * count + waiting(after),
            out_specs=whole((count,) + shape),
        ),
        compiler_params=PARAMS,
        cost_estimate=COST,
        name="in_order",
    )(quarter, *kept, *after)


def silu_parts(gate, up_value, grad_act):
    sigmoid_g = jax.nn.sigmoid(gate)
    activated = gate * sigmoid_g
    value = (activated * up_value).astype(BF16)
    grad_gate = (grad_act * up_value * sigmoid_g * (1.0 + gate * (1.0 - sigmoid_g))).astype(BF16)
    grad_up = (grad_act * activated).astype(BF16)
    return (value, grad_gate, grad_up)


def per_device(inputs, out_grad, int_values, scales, block_rows, holder, slot_index):
    own_count = lax.axis_size("own")
    data_count = lax.axis_size("dp")
    own_index = lax.axis_index("own")
    data_index = lax.axis_index("dp")
    local_tokens, local_width = inputs.shape
    tokens = local_tokens * data_count
    slot_count = int_values.shape[1]
    block = int_values.shape[2]
    keep = block_rows.shape[2]
    width = local_width * own_count
    row_blocks = width // block
    columns = block_rows.shape[1] // own_count
    group = columns * keep
    active = 3 * own_count // 4
    capacity = (group + active - 1) // active
    places = own_count * capacity
    rows_each = block // data_count
    depth = row_blocks * rows_each
    hidden = columns * rows_each
    factor = 1.0 / math.sqrt(tokens)

    holder_group = holder.reshape(3, own_count, group)
    slot_group = slot_index.reshape(3, own_count, group)
    mine = (holder_group == own_index).astype(jnp.int32)
    rank = jnp.cumsum(mine, axis=2) - 1
    spots = jnp.arange(capacity, dtype=jnp.int32)
    picked = (mine[..., None] == 1) & (rank[..., None] == spots)
    bucket_slot = jnp.sum(jnp.where(picked, slot_group[..., None], 0), axis=2)
    used = spots < jnp.sum(mine, axis=2)[..., None]
    hits = used[..., None] & (bucket_slot[..., None] == jnp.arange(slot_count, dtype=jnp.int32))
    bucket_index = jnp.arange(places, dtype=jnp.int32).reshape(own_count, capacity)
    source = jnp.sum(jnp.where(hits, bucket_index[None, :, :, None], 0), axis=(1, 2))
    bucket_slot = bucket_slot.reshape(3, places)
    own_holder = lax.dynamic_index_in_dim(holder_group, own_index, 1, keepdims=False)
    entries = jnp.arange(group, dtype=jnp.int32)
    earlier = (own_holder[:, :, None] == own_holder[:, None, :]) & (
        entries[None, :, None] < entries[None, None, :]
    )
    position = jnp.sum(earlier.astype(jnp.int32), axis=1)
    flat = own_holder * capacity + position
    rows = lax.dynamic_index_in_dim(
        block_rows.reshape(3, own_count, group), own_index, 1, keepdims=False
    )
    quarter = data_index.astype(jnp.int32).reshape(1)

    def exchange(parts):
        kept = [parts[0]]
        for s in range(1, data_count):
            turn = [(i, (i + s) % data_count) for i in range(data_count)]
            kept.append(lax.ppermute(parts[s], "dp", turn))
        return kept

    def to_planes(parts):
        twice = jnp.concatenate([parts, parts])
        return [
            lax.dynamic_index_in_dim(twice, data_index + s, 0, keepdims=False)
            for s in range(data_count)
        ]

    def send(which, after=()):
        sending = pack(
            which, int_values, scales[which], bucket_slot[which], quarter, rows_each, after
        )
        return sending.reshape(own_count, capacity, rows_each, block)

    def receive(sending):
        arrived = lax.all_to_all(sending, "own", split_axis=0, concat_axis=0, tiled=True)
        return arrived.reshape(places, rows_each, block)

    chips = own_count // 2
    likes = [[core + 2 * chip for chip in range(chips)] for core in range(2)]
    swap = [(i, i ^ 1) for i in range(own_count)]
    core = jnp.remainder(own_index, 2).astype(jnp.int32).reshape(1)
    turns = own_index ^ (2 * jnp.arange(chips, dtype=jnp.int32))
    order = jnp.stack([turns, turns ^ 1], axis=1).reshape(own_count)

    near = lax.all_gather(out_grad, "own", axis=0, axis_index_groups=likes)
    far = exchange([out_grad] * data_count)[1:]
    passed = tuple(mark(part) for part in far)
    far = jnp.stack(far)

    local = inputs.reshape(local_tokens, row_blocks // own_count, data_count, rows_each)
    local = local.transpose(2, 0, 1, 3).reshape(data_count, local_tokens, depth // own_count)
    local = exchange(to_planes(local))
    sending_gate = send(0)
    local = in_order(local, quarter, (mark(sending_gate),) + passed)
    gathered = lax.all_gather(local.reshape(tokens, depth // own_count), "own", axis=0)
    sending_up, sending_down = send(1, (mark(local),)), send(2, (mark(local),))
    arrived_gate = receive(sending_gate)

    far = [tie(far, mark(arrived_gate))]
    for turn in range(1, chips):
        far.append(lax.ppermute(far[0], "own", [(i, i ^ (2 * turn)) for i in range(own_count)]))

    x = gathered.transpose(1, 0, 2).reshape(tokens, depth)
    x_turned = gathered.transpose(0, 2, 1).reshape(depth, tokens)
    packed = (mark(sending_up), mark(sending_down), mark(near))
    gate_weights, part = forward(x, arrived_gate, flat[0], rows[0], columns, row_blocks, packed)
    gate = lax.psum_scatter(part, "dp", scatter_dimension=0)
    arrived_up = receive(tie(sending_up, mark(gate_weights)))
    up_weights, part = forward(
        x, arrived_up, flat[1], rows[1], columns, row_blocks, (mark(gate),)
    )
    up_value = lax.psum_scatter(part, "dp", scatter_dimension=0)
    far = jnp.stack([tie(part, mark(up_weights)) for part in far])
    cotangents = ((near, far), (lax.ppermute(near, "own", swap), lax.ppermute(far, "own", swap)))
    arrived_down = receive(tie(sending_down, mark(arrived_up)))
    grad_act = forward_down(
        cotangents, arrived_down, flat[2], rows[2], quarter, order, columns, row_blocks
    )
    value, grad_gate, grad_up = silu_parts(
        gate.reshape(hidden, tokens).astype(F32), up_value.reshape(hidden, tokens).astype(F32), grad_act
    )
    shape = (columns, rows_each, tokens)

    def give_back(leaving):
        leaving = leaving.reshape(own_count, capacity, rows_each, block)
        returned = lax.all_to_all(leaving, "own", split_axis=0, concat_axis=0, tiled=True)
        return returned.reshape(places, rows_each, block)

    all_up = lax.all_gather(grad_up.reshape(shape), "dp", axis=0)
    leaving = weight_grad_down(
        value, cotangents, flat[2], rows[2], quarter, order, places, block, columns, row_blocks, factor
    )
    all_gate = lax.all_gather(grad_gate.reshape(shape), "dp", axis=0)
    returned = give_back(leaving)
    leaving = weight_grad(
        x_turned, all_up, flat[1], rows[1], places, row_blocks, factor, (mark(returned),)
    )
    total = unpack(2, returned, source[2], None)
    returned = give_back(leaving)

    up_weights = up_weights.reshape(depth, columns * block)
    gate_weights = gate_weights.reshape(depth, columns * block)
    back = input_part(up_weights, all_up, core, chips, after=(mark(leaving),))
    back = input_part(gate_weights, all_gate, core, chips, back, (mark(returned), mark(total)))
    leaving = weight_grad(
        x_turned, all_gate, flat[0], rows[0], places, row_blocks, factor, (mark(back[0]),)
    )
    total = unpack(1, returned, source[1], total)
    returned = give_back(leaving)

    back = back[0].astype(F32) + lax.ppermute(back[1], "own", swap).astype(F32)
    back = lax.psum_scatter(
        back.astype(BF16), "own", scatter_dimension=0, axis_index_groups=likes
    )
    back = back.reshape(depth // own_count, data_count, local_tokens).transpose(1, 0, 2)
    back = tie(back, mark(total))
    back = lax.all_to_all(back, "dp", split_axis=0, concat_axis=0, tiled=True)
    back = back.reshape(data_count, row_blocks // own_count, rows_each, local_tokens)
    input_grad = back.transpose(3, 1, 0, 2).reshape(local_tokens, local_width)
    total = unpack(0, returned, source[0], total)
    return (input_grad, total)


def solution(mesh):
    placed = (
        P("dp", "own"),
        P("dp", "own"),
        P(None, "own", None, None),
        P(None, "own"),
        P(),
        P(),
        P(),
    )
    return jax.shard_map(
        per_device,
        mesh=mesh,
        in_specs=placed,
        out_specs=(P("dp", "own"), P(None, "own", "dp", None)),
        check_vma=False,
    )
```

```python
import functools
import math

import jax
import jax.numpy as jnp
from jax import lax
from jax.experimental import pallas as pl
from jax.experimental.pallas import tpu as pltpu
from jax.sharding import PartitionSpec as P

F32 = jnp.float32
BF16 = jnp.bfloat16
NT = (((1,), (1,)), ((), ()))
COST = pl.CostEstimate(flops=1024, bytes_accessed=1024, transcendentals=0)
PARAMS = pltpu.CompilerParams(vmem_limit_bytes=56 * 2**20)


def whole(shape):
    return pl.BlockSpec(shape, lambda *_: (0,) * len(shape))


def waiting(after):
    return [pl.BlockSpec(memory_space=pl.ANY)] * len(after)


def mark(value):
    return value.reshape((-1,) + value.shape[-2:])[0, :16, :128]


def tie(value, *after):
    def kernel(*refs):
        pass

    return pl.pallas_call(
        kernel,
        out_shape=jax.ShapeDtypeStruct(value.shape, value.dtype),
        in_specs=waiting((value,) + after),
        out_specs=pl.BlockSpec(memory_space=pl.ANY),
        input_output_aliases={0: 0},
        compiler_params=PARAMS,
        name="tie",
    )(value, *after)


def pack(which, ints, scales, slots, quarter, rows_each, after=()):
    slot_count, block = ints.shape[1], ints.shape[2]
    places = slots.shape[0]

    def kernel(slots, quarter, scales, ints, *refs):
        out = refs[-1]

        def place(index, _):
            slot = slots[index]
            out[index] = (ints[0, slot].astype(F32) * scales[slot]).astype(BF16)
            return _

        lax.fori_loop(0, places, place, 0, unroll=8)

    return pl.pallas_call(
        kernel,
        out_shape=jax.ShapeDtypeStruct((places, rows_each, block), BF16),
        grid_spec=pltpu.PrefetchScalarGridSpec(
            num_scalar_prefetch=3,
            grid=(1,),
            in_specs=[
                pl.BlockSpec(
                    (1, slot_count, rows_each, block), lambda g, s, q, c: (which, 0, q[0], 0)
                )
            ]
            + waiting(after),
            out_specs=whole((places, rows_each, block)),
        ),
        compiler_params=PARAMS,
        cost_estimate=COST,
        name="pack",
    )(slots, quarter, scales, ints, *after)


def forward(x, arrived, flat, rows, columns, row_blocks, after=()):
    places, rows_each, block = arrived.shape
    tokens, depth = x.shape
    keep = flat.shape[0] // columns
    quarters = block // rows_each

    def kernel(flat, rows, x, arrived, *refs):
        dense, out = refs[-2:]
        step = pl.program_id(0)
        dense[...] = jnp.zeros_like(dense)
        for half in range(2):
            base = (step * 2 + half) * keep
            lanes = slice(half * block, (half + 1) * block)

            def place(k, _):
                dense[rows[base + k], :, lanes] = arrived[flat[base + k]]
                return _

            lax.fori_loop(0, keep, place, 0, unroll=2)
        weights = dense[...].reshape(depth, 2 * block)
        result = jnp.dot(x[...], weights, preferred_element_type=F32)
        turned = jnp.transpose(result).astype(BF16)
        for half in range(2):
            for q in range(quarters):
                first = half * block + q * rows_each
                out[q, half] = turned[first : first + rows_each]

    return pl.pallas_call(
        kernel,
        out_shape=(
            jax.ShapeDtypeStruct((row_blocks, rows_each, columns * block), BF16),
            jax.ShapeDtypeStruct((quarters, columns, rows_each, tokens), BF16),
        ),
        grid_spec=pltpu.PrefetchScalarGridSpec(
            num_scalar_prefetch=2,
            grid=(columns // 2,),
            in_specs=[whole((tokens, depth)), whole((places, rows_each, block))] + waiting(after),
            out_specs=(
                pl.BlockSpec((row_blocks, rows_each, 2 * block), lambda g, f, r: (0, 0, g)),
                pl.BlockSpec((quarters, 2, rows_each, tokens), lambda g, f, r: (0, g, 0, 0)),
            ),
        ),
        compiler_params=PARAMS,
        cost_estimate=COST,
        name="forward",
    )(flat, rows, x, arrived, *after)


def share_specs(cotangents):
    near, early, late = cotangents
    _, tokens, width = near.shape
    others, _, half, _ = early.shape
    return [
        pl.BlockSpec((1, tokens, width), lambda g, f, r, q, o: (o[2 * g] // 2, 0, 0)),
        pl.BlockSpec((others, 1, half, width), lambda g, f, r, q, o: (0, o[2 * g] // 2, 0, 0)),
        pl.BlockSpec((1, others, half, width), lambda g, *_: (g, 0, 0, 0)),
    ]


def join(joined, quarter, near, early, late):
    planes, _, width = joined.shape
    half = early.shape[2]
    joined[quarter] = near[0]
    for shift in range(1, planes):
        plane = lax.rem(quarter + planes - shift, planes)
        joined[plane, :half] = early[shift - 1, 0]
        joined[plane, half:] = late[0, shift - 1]
    return joined[...].reshape(-1, width)


def forward_down(cotangents, arrived, flat, rows, quarter, order, columns, row_blocks):
    chips, tokens, width = cotangents[0][0].shape
    planes = cotangents[0][1].shape[0] + 1
    owners = 2 * chips
    places, rows_each, block = arrived.shape
    keep = flat.shape[0] // columns
    hidden = columns * rows_each
    per_owner = row_blocks // owners

    def kernel(flat, rows, quarter, order, *refs):
        shares, (arrived, out, joined, dense) = (refs[:3], refs[3:6]), refs[6:]
        step = pl.program_id(0)

        @pl.when(step == 0)
        def _():
            dense[...] = jnp.zeros_like(dense)
            out[...] = jnp.zeros_like(out)
            for c in range(columns):

                def place(k, _):
                    row = rows[c * keep + k]
                    lane = pl.multiple_of((row % per_owner) * block, block)
                    dense[row // per_owner, c * rows_each : (c + 1) * rows_each, pl.ds(lane, block)] = (
                        arrived[flat[c * keep + k]]
                    )
                    return _

                lax.fori_loop(0, keep, place, 0, unroll=2)

        for core in range(2):
            out[...] += lax.dot_general(
                dense[order[2 * step + core]],
                join(joined, quarter[0], *shares[core]),
                NT,
                preferred_element_type=F32,
            )

    share = share_specs(cotangents[0])
    return pl.pallas_call(
        kernel,
        out_shape=jax.ShapeDtypeStruct((hidden, planes * tokens), F32),
        grid_spec=pltpu.PrefetchScalarGridSpec(
            num_scalar_prefetch=4,
            grid=(chips,),
            in_specs=share + share + [whole((places, rows_each, block))],
            out_specs=whole((hidden, planes * tokens)),
            scratch_shapes=[
                pltpu.VMEM((planes, tokens, width), BF16),
                pltpu.VMEM((owners, hidden, width), BF16),
            ],
        ),
        compiler_params=PARAMS,
        cost_estimate=COST,
        name="forward_down",
    )(flat, rows, quarter, order, *cotangents[0], *cotangents[1], arrived)


def weight_grad(x_turned, grad, flat, rows, places, row_blocks, factor, after=()):
    quarters, columns, rows_each, tokens = grad.shape
    depth = x_turned.shape[0]
    block = quarters * rows_each
    keep = flat.shape[0] // columns

    def kernel(flat, rows, x_turned, grad, *refs):
        out, result = refs[-2:]
        step = pl.program_id(0)
        right = jnp.concatenate(
            [grad[q, half] for half in range(2) for q in range(quarters)], axis=0
        )
        product = lax.dot_general(x_turned[...], right, NT, preferred_element_type=F32)
        result[...] = (product * factor).astype(BF16).reshape(result.shape)
        for half in range(2):
            base = (step * 2 + half) * keep
            lanes = slice(half * block, (half + 1) * block)

            def place(k, _):
                out[flat[base + k]] = result[rows[base + k], :, lanes]
                return _

            lax.fori_loop(0, keep, place, 0, unroll=2)

    return pl.pallas_call(
        kernel,
        out_shape=jax.ShapeDtypeStruct((places, rows_each, block), BF16),
        grid_spec=pltpu.PrefetchScalarGridSpec(
            num_scalar_prefetch=2,
            grid=(columns // 2,),
            in_specs=[
                whole((depth, tokens)),
                pl.BlockSpec((quarters, 2, rows_each, tokens), lambda g, f, r: (0, g, 0, 0)),
            ]
            + waiting(after),
            out_specs=whole((places, rows_each, block)),
            scratch_shapes=[pltpu.VMEM((row_blocks, rows_each, 2 * block), BF16)],
        ),
        compiler_params=PARAMS,
        cost_estimate=COST,
        name="weight_grad",
    )(flat, rows, x_turned, grad, *after)


def weight_grad_down(
    value, cotangents, flat, rows, quarter, order, places, block, columns, row_blocks, factor
):
    chips, tokens, width = cotangents[0][0].shape
    planes = cotangents[0][1].shape[0] + 1
    owners = 2 * chips
    hidden = value.shape[0]
    rows_each = hidden // columns
    keep = flat.shape[0] // columns
    per_owner = row_blocks // owners

    def kernel(flat, rows, quarter, order, value, *refs):
        shares, (out, joined, result) = (refs[:3], refs[3:6]), refs[6:]
        step = pl.program_id(0)
        for core in range(2):
            right = join(joined, quarter[0], *shares[core])
            product = jnp.dot(value[...], right, preferred_element_type=F32)
            result[order[2 * step + core]] = (product * factor).astype(BF16)

        @pl.when(step == chips - 1)
        def _():
            for c in range(columns):

                def place(k, _):
                    row = rows[c * keep + k]
                    lane = pl.multiple_of((row % per_owner) * block, block)
                    out[flat[c * keep + k]] = result[
                        row // per_owner, c * rows_each : (c + 1) * rows_each, pl.ds(lane, block)
                    ]
                    return _

                lax.fori_loop(0, keep, place, 0, unroll=2)

    share = share_specs(cotangents[0])
    return pl.pallas_call(
        kernel,
        out_shape=jax.ShapeDtypeStruct((places, rows_each, block), BF16),
        grid_spec=pltpu.PrefetchScalarGridSpec(
            num_scalar_prefetch=4,
            grid=(chips,),
            in_specs=[whole((hidden, planes * tokens))] + share + share,
            out_specs=whole((places, rows_each, block)),
            scratch_shapes=[
                pltpu.VMEM((planes, tokens, width), BF16),
                pltpu.VMEM((owners, hidden, width), BF16),
            ],
        ),
        compiler_params=PARAMS,
        cost_estimate=COST,
        name="weight_grad_down",
    )(flat, rows, quarter, order, value, *cotangents[0], *cotangents[1])


def input_part(weights, grad, first, chips, earlier=(), after=()):
    depth, units = weights.shape
    quarters, columns, rows_each, tokens = grad.shape
    rows = depth // (2 * chips)

    def kernel(first, left, right, grad, *refs):
        earlier, (*outs, natural) = refs[: len(refs) - len(after) - 3], refs[-3:]

        @pl.when(pl.program_id(0) == 0)
        def _():
            for c in range(columns):
                for q in range(quarters):
                    natural[c, q] = grad[q, c]

        both = jnp.concatenate([left[...], right[...]], axis=0)
        product = jnp.dot(
            both, natural[...].reshape(units, tokens), preferred_element_type=F32
        )
        for core in range(2):
            part = product[core * rows : (core + 1) * rows]
            if earlier:
                part = earlier[core][0] + part
            outs[core][0] = part.astype(outs[core].dtype)

    share = pl.BlockSpec((1, rows, tokens), lambda g, f: (g, 0, 0))
    out = jax.ShapeDtypeStruct((chips, rows, tokens), BF16 if earlier else F32)
    return pl.pallas_call(
        kernel,
        out_shape=(out, out),
        grid_spec=pltpu.PrefetchScalarGridSpec(
            num_scalar_prefetch=1,
            grid=(chips,),
            in_specs=[
                pl.BlockSpec((rows, units), lambda g, f: (2 * g + f[0], 0)),
                pl.BlockSpec((rows, units), lambda g, f: (2 * g + 1 - f[0], 0)),
                whole(grad.shape),
            ]
            + [share] * len(earlier)
            + waiting(after),
            out_specs=(share, share),
            scratch_shapes=[pltpu.VMEM((columns, quarters, rows_each, tokens), BF16)],
        ),
        compiler_params=PARAMS,
        cost_estimate=COST,
        name="input_part",
    )(first, weights, weights, grad, *earlier, *after)


def unpack(which, returned, source, total):
    places, rows_each, block = returned.shape
    slot_count = source.shape[0]

    def kernel(source, returned, *refs):
        out = refs[-1]

        def place(slot, _):
            out[0, slot] = returned[source[slot]]
            return _

        lax.fori_loop(0, slot_count, place, 0, unroll=8)

    shape = (3, slot_count, rows_each, block)
    extra = [] if total is None else [total]
    return pl.pallas_call(
        kernel,
        out_shape=jax.ShapeDtypeStruct(shape, BF16),
        grid_spec=pltpu.PrefetchScalarGridSpec(
            num_scalar_prefetch=1,
            grid=(1,),
            in_specs=[whole((places, rows_each, block))] + waiting(extra),
            out_specs=pl.BlockSpec((1,) + shape[1:], lambda g, s: (which, 0, 0, 0)),
        ),
        input_output_aliases={2: 0} if extra else {},
        compiler_params=PARAMS,
        cost_estimate=COST,
        name="unpack",
    )(source, returned, *extra)


def in_order(kept, quarter, after=()):
    count, shape = len(kept), kept[0].shape

    def kernel(quarter, *refs):
        for shift in range(count):
            refs[-1][lax.rem(quarter[0] + count - shift, count)] = refs[shift][...]

    return pl.pallas_call(
        kernel,
        out_shape=jax.ShapeDtypeStruct((count,) + shape, kept[0].dtype),
        grid_spec=pltpu.PrefetchScalarGridSpec(
            num_scalar_prefetch=1,
            grid=(1,),
            in_specs=[whole(shape)] * count + waiting(after),
            out_specs=whole((count,) + shape),
        ),
        compiler_params=PARAMS,
        cost_estimate=COST,
        name="in_order",
    )(quarter, *kept, *after)


def silu_parts(gate, up_value, grad_act):
    sigmoid_g = jax.nn.sigmoid(gate)
    activated = gate * sigmoid_g
    value = (activated * up_value).astype(BF16)
    grad_gate = (grad_act * up_value * sigmoid_g * (1.0 + gate * (1.0 - sigmoid_g))).astype(BF16)
    grad_up = (grad_act * activated).astype(BF16)
    return (value, grad_gate, grad_up)


def per_device(inputs, out_grad, int_values, scales, block_rows, holder, slot_index):
    own_count = lax.axis_size("own")
    data_count = lax.axis_size("dp")
    own_index = lax.axis_index("own")
    data_index = lax.axis_index("dp")
    local_tokens, local_width = inputs.shape
    tokens = local_tokens * data_count
    slot_count = int_values.shape[1]
    block = int_values.shape[2]
    keep = block_rows.shape[2]
    width = local_width * own_count
    row_blocks = width // block
    columns = block_rows.shape[1] // own_count
    group = columns * keep
    active = 3 * own_count // 4
    capacity = (group + active - 1) // active
    places = own_count * capacity
    rows_each = block // data_count
    depth = row_blocks * rows_each
    hidden = columns * rows_each
    factor = 1.0 / math.sqrt(tokens)

    holder_group = holder.reshape(3, own_count, group)
    slot_group = slot_index.reshape(3, own_count, group)
    mine = (holder_group == own_index).astype(jnp.int32)
    rank = jnp.cumsum(mine, axis=2) - 1
    spots = jnp.arange(capacity, dtype=jnp.int32)
    picked = (mine[..., None] == 1) & (rank[..., None] == spots)
    bucket_slot = jnp.sum(jnp.where(picked, slot_group[..., None], 0), axis=2)
    used = spots < jnp.sum(mine, axis=2)[..., None]
    hits = used[..., None] & (bucket_slot[..., None] == jnp.arange(slot_count, dtype=jnp.int32))
    bucket_index = jnp.arange(places, dtype=jnp.int32).reshape(own_count, capacity)
    source = jnp.sum(jnp.where(hits, bucket_index[None, :, :, None], 0), axis=(1, 2))
    bucket_slot = bucket_slot.reshape(3, places)
    own_holder = lax.dynamic_index_in_dim(holder_group, own_index, 1, keepdims=False)
    entries = jnp.arange(group, dtype=jnp.int32)
    earlier = (own_holder[:, :, None] == own_holder[:, None, :]) & (
        entries[None, :, None] < entries[None, None, :]
    )
    position = jnp.sum(earlier.astype(jnp.int32), axis=1)
    flat = own_holder * capacity + position
    rows = lax.dynamic_index_in_dim(
        block_rows.reshape(3, own_count, group), own_index, 1, keepdims=False
    )
    quarter = data_index.astype(jnp.int32).reshape(1)

    def exchange(parts):
        kept = [parts[0]]
        for s in range(1, data_count):
            turn = [(i, (i + s) % data_count) for i in range(data_count)]
            kept.append(lax.ppermute(parts[s], "dp", turn))
        return kept

    def to_planes(parts):
        twice = jnp.concatenate([parts, parts])
        return [
            lax.dynamic_index_in_dim(twice, data_index + s, 0, keepdims=False)
            for s in range(data_count)
        ]

    def send(which, after=()):
        sending = pack(
            which, int_values, scales[which], bucket_slot[which], quarter, rows_each, after
        )
        return sending.reshape(own_count, capacity, rows_each, block)

    def receive(sending):
        arrived = lax.all_to_all(sending, "own", split_axis=0, concat_axis=0, tiled=True)
        return arrived.reshape(places, rows_each, block)

    chips = own_count // 2
    likes = [[core + 2 * chip for chip in range(chips)] for core in range(2)]
    swap = [(i, i ^ 1) for i in range(own_count)]
    core = jnp.remainder(own_index, 2).astype(jnp.int32).reshape(1)
    turns = own_index ^ (2 * jnp.arange(chips, dtype=jnp.int32))
    order = jnp.stack([turns, turns ^ 1], axis=1).reshape(own_count)

    near = lax.all_gather(out_grad, "own", axis=0, axis_index_groups=likes)
    half = local_tokens // 2
    early = exchange([near[:, :half]] * data_count)[1:]

    late = exchange([out_grad[half:]] * data_count)[1:]
    passed = tuple(mark(part) for part in late)

    local = inputs.reshape(local_tokens, row_blocks // own_count, data_count, rows_each)
    local = local.transpose(2, 0, 1, 3).reshape(data_count, local_tokens, depth // own_count)
    local = exchange(to_planes(local))
    sending_gate = send(0)
    local = in_order(local, quarter, (mark(sending_gate),))
    gathered = lax.all_gather(local.reshape(tokens, depth // own_count), "own", axis=0)
    sending_up, sending_down = send(1, (mark(local),)), send(2, (mark(local),) + passed)
    arrived_gate = receive(sending_gate)

    late = [tie(jnp.stack(late), mark(arrived_gate))]
    for turn in range(1, chips):
        late.append(lax.ppermute(late[0], "own", [(i, i ^ (2 * turn)) for i in range(own_count)]))

    x = gathered.transpose(1, 0, 2).reshape(tokens, depth)
    x_turned = gathered.transpose(0, 2, 1).reshape(depth, tokens)
    packed = (mark(sending_up), mark(sending_down)) + tuple(mark(part) for part in early)
    gate_weights, part = forward(x, arrived_gate, flat[0], rows[0], columns, row_blocks, packed)
    gate = lax.psum_scatter(part, "dp", scatter_dimension=0)
    arrived_up = receive(tie(sending_up, mark(gate_weights)))
    up_weights, part = forward(
        x, arrived_up, flat[1], rows[1], columns, row_blocks, (mark(gate),)
    )
    up_value = lax.psum_scatter(part, "dp", scatter_dimension=0)
    late = jnp.stack([tie(part, mark(up_weights)) for part in late])
    cotangents = (near, jnp.stack(early), late)
    cotangents = (cotangents, [lax.ppermute(part, "own", swap) for part in cotangents])
    arrived_down = receive(tie(sending_down, mark(arrived_up)))
    grad_act = forward_down(
        cotangents, arrived_down, flat[2], rows[2], quarter, order, columns, row_blocks
    )
    value, grad_gate, grad_up = silu_parts(
        gate.reshape(hidden, tokens).astype(F32), up_value.reshape(hidden, tokens).astype(F32), grad_act
    )
    shape = (columns, rows_each, tokens)

    def give_back(leaving):
        leaving = leaving.reshape(own_count, capacity, rows_each, block)
        returned = lax.all_to_all(leaving, "own", split_axis=0, concat_axis=0, tiled=True)
        return returned.reshape(places, rows_each, block)

    all_up = lax.all_gather(grad_up.reshape(shape), "dp", axis=0)
    leaving = weight_grad_down(
        value, cotangents, flat[2], rows[2], quarter, order, places, block, columns, row_blocks, factor
    )
    all_gate = lax.all_gather(grad_gate.reshape(shape), "dp", axis=0)
    returned = give_back(leaving)
    leaving = weight_grad(
        x_turned, all_up, flat[1], rows[1], places, row_blocks, factor, (mark(returned),)
    )
    total = unpack(2, returned, source[2], None)
    returned = give_back(leaving)

    up_weights = up_weights.reshape(depth, columns * block)
    gate_weights = gate_weights.reshape(depth, columns * block)
    back = input_part(up_weights, all_up, core, chips, after=(mark(leaving),))
    back = input_part(gate_weights, all_gate, core, chips, back, (mark(returned), mark(total)))
    leaving = weight_grad(
        x_turned, all_gate, flat[0], rows[0], places, row_blocks, factor, (mark(back[0]),)
    )
    total = unpack(1, returned, source[1], total)
    returned = give_back(leaving)

    back = back[0].astype(F32) + lax.ppermute(back[1], "own", swap).astype(F32)
    back = lax.psum_scatter(
        back.astype(BF16), "own", scatter_dimension=0, axis_index_groups=likes
    )
    back = back.reshape(depth // own_count, data_count, local_tokens).transpose(1, 0, 2)
    back = tie(back, mark(total))
    back = lax.all_to_all(back, "dp", split_axis=0, concat_axis=0, tiled=True)
    back = back.reshape(data_count, row_blocks // own_count, rows_each, local_tokens)
    input_grad = back.transpose(3, 1, 0, 2).reshape(local_tokens, local_width)
    total = unpack(0, returned, source[0], total)
    return (input_grad, total)


def solution(mesh):
    placed = (
        P("dp", "own"),
        P("dp", "own"),
        P(None, "own", None, None),
        P(None, "own"),
        P(),
        P(),
        P(),
    )
    return jax.shard_map(
        per_device,
        mesh=mesh,
        in_specs=placed,
        out_specs=(P("dp", "own"), P(None, "own", "dp", None)),
        check_vma=False,
    )
```

```python
import functools
import math

import jax
import jax.numpy as jnp
from jax import lax
from jax.experimental import pallas as pl
from jax.experimental.pallas import tpu as pltpu
from jax.sharding import PartitionSpec as P

F32 = jnp.float32
BF16 = jnp.bfloat16
NT = (((1,), (1,)), ((), ()))
COST = pl.CostEstimate(flops=1024, bytes_accessed=1024, transcendentals=0)
PARAMS = pltpu.CompilerParams(vmem_limit_bytes=56 * 2**20)


def whole(shape):
    return pl.BlockSpec(shape, lambda *_: (0,) * len(shape))


def waiting(after):
    return [pl.BlockSpec(memory_space=pl.ANY)] * len(after)


def mark(value):
    return value.reshape((-1,) + value.shape[-2:])[0, :16, :128]


def tie(value, *after):
    def kernel(*refs):
        pass

    return pl.pallas_call(
        kernel,
        out_shape=jax.ShapeDtypeStruct(value.shape, value.dtype),
        in_specs=waiting((value,) + after),
        out_specs=pl.BlockSpec(memory_space=pl.ANY),
        input_output_aliases={0: 0},
        compiler_params=PARAMS,
        name="tie",
    )(value, *after)


def pack(which, ints, scales, slots, quarter, rows_each, after=()):
    slot_count, block = ints.shape[1], ints.shape[2]
    places = slots.shape[0]

    def kernel(slots, quarter, scales, ints, *refs):
        out = refs[-1]

        def place(index, _):
            slot = slots[index]
            out[index] = (ints[0, slot].astype(F32) * scales[slot]).astype(BF16)
            return _

        lax.fori_loop(0, places, place, 0, unroll=8)

    return pl.pallas_call(
        kernel,
        out_shape=jax.ShapeDtypeStruct((places, rows_each, block), BF16),
        grid_spec=pltpu.PrefetchScalarGridSpec(
            num_scalar_prefetch=3,
            grid=(1,),
            in_specs=[
                pl.BlockSpec(
                    (1, slot_count, rows_each, block), lambda g, s, q, c: (which, 0, q[0], 0)
                )
            ]
            + waiting(after),
            out_specs=whole((places, rows_each, block)),
        ),
        compiler_params=PARAMS,
        cost_estimate=COST,
        name="pack",
    )(slots, quarter, scales, ints, *after)


def forward(x, arrived, flat, rows, columns, row_blocks, after=()):
    places, rows_each, block = arrived.shape
    tokens, depth = x.shape
    keep = flat.shape[0] // columns
    quarters = block // rows_each

    def kernel(flat, rows, x, arrived, *refs):
        dense, out = refs[-2:]
        step = pl.program_id(0)
        dense[...] = jnp.zeros_like(dense)
        for half in range(2):
            base = (step * 2 + half) * keep
            lanes = slice(half * block, (half + 1) * block)

            def place(k, _):
                dense[rows[base + k], :, lanes] = arrived[flat[base + k]]
                return _

            lax.fori_loop(0, keep, place, 0, unroll=2)
        weights = dense[...].reshape(depth, 2 * block)
        result = jnp.dot(x[...], weights, preferred_element_type=F32)
        turned = jnp.transpose(result).astype(BF16)
        for half in range(2):
            for q in range(quarters):
                first = half * block + q * rows_each
                out[q, half] = turned[first : first + rows_each]

    return pl.pallas_call(
        kernel,
        out_shape=(
            jax.ShapeDtypeStruct((row_blocks, rows_each, columns * block), BF16),
            jax.ShapeDtypeStruct((quarters, columns, rows_each, tokens), BF16),
        ),
        grid_spec=pltpu.PrefetchScalarGridSpec(
            num_scalar_prefetch=2,
            grid=(columns // 2,),
            in_specs=[whole((tokens, depth)), whole((places, rows_each, block))] + waiting(after),
            out_specs=(
                pl.BlockSpec((row_blocks, rows_each, 2 * block), lambda g, f, r: (0, 0, g)),
                pl.BlockSpec((quarters, 2, rows_each, tokens), lambda g, f, r: (0, g, 0, 0)),
            ),
        ),
        compiler_params=PARAMS,
        cost_estimate=COST,
        name="forward",
    )(flat, rows, x, arrived, *after)


def share_specs(cotangents):
    near, early, late = cotangents
    _, tokens, width = near.shape
    others, _, first, _ = early.shape
    return [
        pl.BlockSpec((1, tokens, width), lambda g, *_: (g, 0, 0)),
        pl.BlockSpec((others, 1, first, width), lambda g, *_: (0, g, 0, 0)),
        pl.BlockSpec((1, others, tokens - first, width), lambda g, *_: (g, 0, 0, 0)),
    ]


def join(joined, quarter, near, early, late):
    planes, _, width = joined.shape
    first = early.shape[2]
    joined[quarter] = near[0]
    for shift in range(1, planes):
        plane = lax.rem(quarter + planes - shift, planes)
        joined[plane, :first] = early[shift - 1, 0]
        joined[plane, first:] = late[0, shift - 1]
    return joined[...].reshape(-1, width)


def forward_down(cotangents, arrived, flat, rows, quarter, order, columns, row_blocks):
    chips, tokens, width = cotangents[0][0].shape
    planes = cotangents[0][1].shape[0] + 1
    owners = 2 * chips
    places, rows_each, block = arrived.shape
    keep = flat.shape[0] // columns
    hidden = columns * rows_each
    per_owner = row_blocks // owners

    def kernel(flat, rows, quarter, order, *refs):
        shares, (arrived, out, joined, dense) = (refs[:3], refs[3:6]), refs[6:]
        step = pl.program_id(0)

        @pl.when(step == 0)
        def _():
            dense[...] = jnp.zeros_like(dense)
            out[...] = jnp.zeros_like(out)
            for c in range(columns):

                def place(k, _):
                    row = rows[c * keep + k]
                    lane = pl.multiple_of((row % per_owner) * block, block)
                    dense[row // per_owner, c * rows_each : (c + 1) * rows_each, pl.ds(lane, block)] = (
                        arrived[flat[c * keep + k]]
                    )
                    return _

                lax.fori_loop(0, keep, place, 0, unroll=2)

        for core in range(2):
            out[...] += lax.dot_general(
                dense[order[2 * step + core]],
                join(joined, quarter[0], *shares[core]),
                NT,
                preferred_element_type=F32,
            )

    share = share_specs(cotangents[0])
    return pl.pallas_call(
        kernel,
        out_shape=jax.ShapeDtypeStruct((hidden, planes * tokens), F32),
        grid_spec=pltpu.PrefetchScalarGridSpec(
            num_scalar_prefetch=4,
            grid=(chips,),
            in_specs=share + share + [whole((places, rows_each, block))],
            out_specs=whole((hidden, planes * tokens)),
            scratch_shapes=[
                pltpu.VMEM((planes, tokens, width), BF16),
                pltpu.VMEM((owners, hidden, width), BF16),
            ],
        ),
        compiler_params=PARAMS,
        cost_estimate=COST,
        name="forward_down",
    )(flat, rows, quarter, order, *cotangents[0], *cotangents[1], arrived)


def weight_grad(x_turned, grad, flat, rows, places, row_blocks, factor, after=()):
    quarters, columns, rows_each, tokens = grad.shape
    depth = x_turned.shape[0]
    block = quarters * rows_each
    keep = flat.shape[0] // columns

    def kernel(flat, rows, x_turned, grad, *refs):
        out, result = refs[-2:]
        step = pl.program_id(0)
        right = jnp.concatenate(
            [grad[q, half] for half in range(2) for q in range(quarters)], axis=0
        )
        product = lax.dot_general(x_turned[...], right, NT, preferred_element_type=F32)
        result[...] = (product * factor).astype(BF16).reshape(result.shape)
        for half in range(2):
            base = (step * 2 + half) * keep
            lanes = slice(half * block, (half + 1) * block)

            def place(k, _):
                out[flat[base + k]] = result[rows[base + k], :, lanes]
                return _

            lax.fori_loop(0, keep, place, 0, unroll=2)

    return pl.pallas_call(
        kernel,
        out_shape=jax.ShapeDtypeStruct((places, rows_each, block), BF16),
        grid_spec=pltpu.PrefetchScalarGridSpec(
            num_scalar_prefetch=2,
            grid=(columns // 2,),
            in_specs=[
                whole((depth, tokens)),
                pl.BlockSpec((quarters, 2, rows_each, tokens), lambda g, f, r: (0, g, 0, 0)),
            ]
            + waiting(after),
            out_specs=whole((places, rows_each, block)),
            scratch_shapes=[pltpu.VMEM((row_blocks, rows_each, 2 * block), BF16)],
        ),
        compiler_params=PARAMS,
        cost_estimate=COST,
        name="weight_grad",
    )(flat, rows, x_turned, grad, *after)


def weight_grad_down(
    value, cotangents, flat, rows, quarter, order, places, block, columns, row_blocks, factor
):
    chips, tokens, width = cotangents[0][0].shape
    planes = cotangents[0][1].shape[0] + 1
    owners = 2 * chips
    hidden = value.shape[0]
    rows_each = hidden // columns
    keep = flat.shape[0] // columns
    per_owner = row_blocks // owners

    def kernel(flat, rows, quarter, order, value, *refs):
        shares, (out, joined, result) = (refs[:3], refs[3:6]), refs[6:]
        step = pl.program_id(0)
        for core in range(2):
            right = join(joined, quarter[0], *shares[core])
            product = jnp.dot(value[...], right, preferred_element_type=F32)
            result[order[2 * step + core]] = (product * factor).astype(BF16)

        @pl.when(step == chips - 1)
        def _():
            for c in range(columns):

                def place(k, _):
                    row = rows[c * keep + k]
                    lane = pl.multiple_of((row % per_owner) * block, block)
                    out[flat[c * keep + k]] = result[
                        row // per_owner, c * rows_each : (c + 1) * rows_each, pl.ds(lane, block)
                    ]
                    return _

                lax.fori_loop(0, keep, place, 0, unroll=2)

    share = share_specs(cotangents[0])
    return pl.pallas_call(
        kernel,
        out_shape=jax.ShapeDtypeStruct((places, rows_each, block), BF16),
        grid_spec=pltpu.PrefetchScalarGridSpec(
            num_scalar_prefetch=4,
            grid=(chips,),
            in_specs=[whole((hidden, planes * tokens))] + share + share,
            out_specs=whole((places, rows_each, block)),
            scratch_shapes=[
                pltpu.VMEM((planes, tokens, width), BF16),
                pltpu.VMEM((owners, hidden, width), BF16),
            ],
        ),
        compiler_params=PARAMS,
        cost_estimate=COST,
        name="weight_grad_down",
    )(flat, rows, quarter, order, value, *cotangents[0], *cotangents[1])


def input_part(weights, grad, first, chips, earlier=(), after=()):
    depth, units = weights.shape
    quarters, columns, rows_each, tokens = grad.shape
    rows = depth // (2 * chips)

    def kernel(first, left, right, grad, *refs):
        earlier, (*outs, natural) = refs[: len(refs) - len(after) - 3], refs[-3:]

        @pl.when(pl.program_id(0) == 0)
        def _():
            for c in range(columns):
                for q in range(quarters):
                    natural[c, q] = grad[q, c]

        both = jnp.concatenate([left[...], right[...]], axis=0)
        product = jnp.dot(
            both, natural[...].reshape(units, tokens), preferred_element_type=F32
        )
        for core in range(2):
            part = product[core * rows : (core + 1) * rows]
            if earlier:
                part = earlier[core][0] + part
            outs[core][0] = part.astype(outs[core].dtype)

    share = pl.BlockSpec((1, rows, tokens), lambda g, f: (g, 0, 0))
    out = jax.ShapeDtypeStruct((chips, rows, tokens), BF16 if earlier else F32)
    return pl.pallas_call(
        kernel,
        out_shape=(out, out),
        grid_spec=pltpu.PrefetchScalarGridSpec(
            num_scalar_prefetch=1,
            grid=(chips,),
            in_specs=[
                pl.BlockSpec((rows, units), lambda g, f: (2 * g + f[0], 0)),
                pl.BlockSpec((rows, units), lambda g, f: (2 * g + 1 - f[0], 0)),
                whole(grad.shape),
            ]
            + [share] * len(earlier)
            + waiting(after),
            out_specs=(share, share),
            scratch_shapes=[pltpu.VMEM((columns, quarters, rows_each, tokens), BF16)],
        ),
        compiler_params=PARAMS,
        cost_estimate=COST,
        name="input_part",
    )(first, weights, weights, grad, *earlier, *after)


def unpack(which, returned, source, total):
    places, rows_each, block = returned.shape
    slot_count = source.shape[0]

    def kernel(source, returned, *refs):
        out = refs[-1]

        def place(slot, _):
            out[0, slot] = returned[source[slot]]
            return _

        lax.fori_loop(0, slot_count, place, 0, unroll=8)

    shape = (3, slot_count, rows_each, block)
    extra = [] if total is None else [total]
    return pl.pallas_call(
        kernel,
        out_shape=jax.ShapeDtypeStruct(shape, BF16),
        grid_spec=pltpu.PrefetchScalarGridSpec(
            num_scalar_prefetch=1,
            grid=(1,),
            in_specs=[whole((places, rows_each, block))] + waiting(extra),
            out_specs=pl.BlockSpec((1,) + shape[1:], lambda g, s: (which, 0, 0, 0)),
        ),
        input_output_aliases={2: 0} if extra else {},
        compiler_params=PARAMS,
        cost_estimate=COST,
        name="unpack",
    )(source, returned, *extra)


def in_order(kept, quarter, after=()):
    count, shape = len(kept), kept[0].shape

    def kernel(quarter, *refs):
        for shift in range(count):
            refs[-1][lax.rem(quarter[0] + count - shift, count)] = refs[shift][...]

    return pl.pallas_call(
        kernel,
        out_shape=jax.ShapeDtypeStruct((count,) + shape, kept[0].dtype),
        grid_spec=pltpu.PrefetchScalarGridSpec(
            num_scalar_prefetch=1,
            grid=(1,),
            in_specs=[whole(shape)] * count + waiting(after),
            out_specs=whole((count,) + shape),
        ),
        compiler_params=PARAMS,
        cost_estimate=COST,
        name="in_order",
    )(quarter, *kept, *after)


def silu_parts(gate, up_value, grad_act):
    sigmoid_g = jax.nn.sigmoid(gate)
    activated = gate * sigmoid_g
    value = (activated * up_value).astype(BF16)
    grad_gate = (grad_act * up_value * sigmoid_g * (1.0 + gate * (1.0 - sigmoid_g))).astype(BF16)
    grad_up = (grad_act * activated).astype(BF16)
    return (value, grad_gate, grad_up)


def per_device(inputs, out_grad, int_values, scales, block_rows, holder, slot_index):
    own_count = lax.axis_size("own")
    data_count = lax.axis_size("dp")
    own_index = lax.axis_index("own")
    data_index = lax.axis_index("dp")
    local_tokens, local_width = inputs.shape
    tokens = local_tokens * data_count
    slot_count = int_values.shape[1]
    block = int_values.shape[2]
    keep = block_rows.shape[2]
    width = local_width * own_count
    row_blocks = width // block
    columns = block_rows.shape[1] // own_count
    group = columns * keep
    active = 3 * own_count // 4
    capacity = (group + active - 1) // active
    places = own_count * capacity
    rows_each = block // data_count
    depth = row_blocks * rows_each
    hidden = columns * rows_each
    factor = 1.0 / math.sqrt(tokens)

    holder_group = holder.reshape(3, own_count, group)
    slot_group = slot_index.reshape(3, own_count, group)
    mine = (holder_group == own_index).astype(jnp.int32)
    rank = jnp.cumsum(mine, axis=2) - 1
    spots = jnp.arange(capacity, dtype=jnp.int32)
    picked = (mine[..., None] == 1) & (rank[..., None] == spots)
    bucket_slot = jnp.sum(jnp.where(picked, slot_group[..., None], 0), axis=2)
    used = spots < jnp.sum(mine, axis=2)[..., None]
    hits = used[..., None] & (bucket_slot[..., None] == jnp.arange(slot_count, dtype=jnp.int32))
    bucket_index = jnp.arange(places, dtype=jnp.int32).reshape(own_count, capacity)
    source = jnp.sum(jnp.where(hits, bucket_index[None, :, :, None], 0), axis=(1, 2))
    bucket_slot = bucket_slot.reshape(3, places)
    own_holder = lax.dynamic_index_in_dim(holder_group, own_index, 1, keepdims=False)
    entries = jnp.arange(group, dtype=jnp.int32)
    earlier = (own_holder[:, :, None] == own_holder[:, None, :]) & (
        entries[None, :, None] < entries[None, None, :]
    )
    position = jnp.sum(earlier.astype(jnp.int32), axis=1)
    flat = own_holder * capacity + position
    rows = lax.dynamic_index_in_dim(
        block_rows.reshape(3, own_count, group), own_index, 1, keepdims=False
    )
    quarter = data_index.astype(jnp.int32).reshape(1)

    def exchange(parts):
        kept = [parts[0]]
        for s in range(1, data_count):
            turn = [(i, (i + s) % data_count) for i in range(data_count)]
            kept.append(lax.ppermute(parts[s], "dp", turn))
        return kept

    def to_planes(parts):
        twice = jnp.concatenate([parts, parts])
        return [
            lax.dynamic_index_in_dim(twice, data_index + s, 0, keepdims=False)
            for s in range(data_count)
        ]

    def send(which, after=()):
        sending = pack(
            which, int_values, scales[which], bucket_slot[which], quarter, rows_each, after
        )
        return sending.reshape(own_count, capacity, rows_each, block)

    def receive(sending):
        arrived = lax.all_to_all(sending, "own", split_axis=0, concat_axis=0, tiled=True)
        return arrived.reshape(places, rows_each, block)

    chips = own_count // 2
    likes = [[core + 2 * chip for chip in range(chips)] for core in range(2)]
    swap = [(i, i ^ 1) for i in range(own_count)]
    core = jnp.remainder(own_index, 2).astype(jnp.int32).reshape(1)
    turns = own_index ^ (2 * jnp.arange(chips, dtype=jnp.int32))
    order = jnp.stack([turns, turns ^ 1], axis=1).reshape(own_count)

    def over_chips(value):
        turns = [[(i, i ^ (2 * turn)) for i in range(own_count)] for turn in range(1, chips)]
        return [value] + [lax.ppermute(value, "own", turn) for turn in turns]

    near = over_chips(out_grad)
    gone = tuple(mark(part) for part in near[1:])
    near = jnp.stack(near)
    cut = local_tokens * 3 // 8
    early = exchange([near[:, :cut]] * data_count)[1:]

    late = exchange([out_grad[cut:]] * data_count)[1:]
    passed = tuple(mark(part) for part in late)

    local = inputs.reshape(local_tokens, row_blocks // own_count, data_count, rows_each)
    local = local.transpose(2, 0, 1, 3).reshape(data_count, local_tokens, depth // own_count)
    local = exchange(to_planes(local))
    sending_gate = send(0)
    local = in_order(local, quarter, (mark(sending_gate),) + gone)
    gathered = lax.all_gather(local.reshape(tokens, depth // own_count), "own", axis=0)
    sending_up, sending_down = send(1, (mark(local),)), send(2, (mark(local),) + passed)
    arrived_gate = receive(sending_gate)

    x = gathered.transpose(1, 0, 2).reshape(tokens, depth)
    x_turned = gathered.transpose(0, 2, 1).reshape(depth, tokens)
    packed = (mark(sending_up), mark(sending_down)) + tuple(mark(part) for part in early)
    gate_weights, part = forward(x, arrived_gate, flat[0], rows[0], columns, row_blocks, packed)
    gate = lax.psum_scatter(part, "dp", scatter_dimension=0)
    late = over_chips(tie(jnp.stack(late), mark(gate_weights)))
    arrived_up = receive(tie(sending_up, mark(gate_weights)))
    up_weights, part = forward(
        x,
        arrived_up,
        flat[1],
        rows[1],
        columns,
        row_blocks,
        (mark(gate),) + tuple(mark(part) for part in late[1:]),
    )
    up_value = lax.psum_scatter(part, "dp", scatter_dimension=0)
    cotangents = (near, jnp.stack(early), jnp.stack(late))
    cotangents = (cotangents, [lax.ppermute(part, "own", swap) for part in cotangents])
    arrived_down = receive(tie(sending_down, mark(arrived_up)))
    grad_act = forward_down(
        cotangents, arrived_down, flat[2], rows[2], quarter, order, columns, row_blocks
    )
    value, grad_gate, grad_up = silu_parts(
        gate.reshape(hidden, tokens).astype(F32), up_value.reshape(hidden, tokens).astype(F32), grad_act
    )
    shape = (columns, rows_each, tokens)

    def give_back(leaving):
        leaving = leaving.reshape(own_count, capacity, rows_each, block)
        returned = lax.all_to_all(leaving, "own", split_axis=0, concat_axis=0, tiled=True)
        return returned.reshape(places, rows_each, block)

    all_up = lax.all_gather(grad_up.reshape(shape), "dp", axis=0)
    leaving = weight_grad_down(
        value, cotangents, flat[2], rows[2], quarter, order, places, block, columns, row_blocks, factor
    )
    all_gate = lax.all_gather(grad_gate.reshape(shape), "dp", axis=0)
    returned = give_back(leaving)
    leaving = weight_grad(
        x_turned, all_up, flat[1], rows[1], places, row_blocks, factor, (mark(returned),)
    )
    total = unpack(2, returned, source[2], None)
    returned = give_back(leaving)

    up_weights = up_weights.reshape(depth, columns * block)
    gate_weights = gate_weights.reshape(depth, columns * block)
    back = input_part(up_weights, all_up, core, chips, after=(mark(leaving),))
    back = input_part(gate_weights, all_gate, core, chips, back, (mark(returned), mark(total)))
    leaving = weight_grad(
        x_turned, all_gate, flat[0], rows[0], places, row_blocks, factor, (mark(back[0]),)
    )
    total = unpack(1, returned, source[1], total)
    returned = give_back(leaving)

    back = back[0].astype(F32) + lax.ppermute(back[1], "own", swap).astype(F32)
    back = lax.psum_scatter(
        back.astype(BF16), "own", scatter_dimension=0, axis_index_groups=likes
    )
    back = back.reshape(depth // own_count, data_count, local_tokens).transpose(1, 0, 2)
    back = tie(back, mark(total))
    back = lax.all_to_all(back, "dp", split_axis=0, concat_axis=0, tiled=True)
    back = back.reshape(data_count, row_blocks // own_count, rows_each, local_tokens)
    input_grad = back.transpose(3, 1, 0, 2).reshape(local_tokens, local_width)
    total = unpack(0, returned, source[0], total)
    return (input_grad, total)


def solution(mesh):
    placed = (
        P("dp", "own"),
        P("dp", "own"),
        P(None, "own", None, None),
        P(None, "own"),
        P(),
        P(),
        P(),
    )
    return jax.shard_map(
        per_device,
        mesh=mesh,
        in_specs=placed,
        out_specs=(P("dp", "own"), P(None, "own", "dp", None)),
        check_vma=False,
    )
```

```python
import functools
import math

import jax
import jax.numpy as jnp
from jax import lax
from jax.experimental import pallas as pl
from jax.experimental.pallas import tpu as pltpu
from jax.sharding import PartitionSpec as P

F32 = jnp.float32
BF16 = jnp.bfloat16
NT = (((1,), (1,)), ((), ()))
COST = pl.CostEstimate(flops=1024, bytes_accessed=1024, transcendentals=0)
PARAMS = pltpu.CompilerParams(vmem_limit_bytes=56 * 2**20)


def whole(shape):
    return pl.BlockSpec(shape, lambda *_: (0,) * len(shape))


def waiting(after):
    return [pl.BlockSpec(memory_space=pl.ANY)] * len(after)


def mark(value):
    return value.reshape((-1,) + value.shape[-2:])[0, :16, :128]


def tie(value, *after):
    def kernel(*refs):
        pass

    return pl.pallas_call(
        kernel,
        out_shape=jax.ShapeDtypeStruct(value.shape, value.dtype),
        in_specs=waiting((value,) + after),
        out_specs=pl.BlockSpec(memory_space=pl.ANY),
        input_output_aliases={0: 0},
        compiler_params=PARAMS,
        name="tie",
    )(value, *after)


def pack(which, ints, scales, slots, quarter, rows_each, after=()):
    slot_count, block = ints.shape[1], ints.shape[2]
    places = slots.shape[0]

    def kernel(slots, quarter, scales, ints, *refs):
        out = refs[-1]

        def place(index, _):
            slot = slots[index]
            out[index] = (ints[0, slot].astype(F32) * scales[slot]).astype(BF16)
            return _

        lax.fori_loop(0, places, place, 0, unroll=8)

    return pl.pallas_call(
        kernel,
        out_shape=jax.ShapeDtypeStruct((places, rows_each, block), BF16),
        grid_spec=pltpu.PrefetchScalarGridSpec(
            num_scalar_prefetch=3,
            grid=(1,),
            in_specs=[
                pl.BlockSpec(
                    (1, slot_count, rows_each, block), lambda g, s, q, c: (which, 0, q[0], 0)
                )
            ]
            + waiting(after),
            out_specs=whole((places, rows_each, block)),
        ),
        compiler_params=PARAMS,
        cost_estimate=COST,
        name="pack",
    )(slots, quarter, scales, ints, *after)


def forward(x, arrived, flat, rows, columns, row_blocks, after=()):
    places, rows_each, block = arrived.shape
    tokens, depth = x.shape
    keep = flat.shape[0] // columns
    quarters = block // rows_each

    def kernel(flat, rows, x, arrived, *refs):
        dense, out = refs[-2:]
        step = pl.program_id(0)
        dense[...] = jnp.zeros_like(dense)
        for half in range(2):
            base = (step * 2 + half) * keep
            lanes = slice(half * block, (half + 1) * block)

            def place(k, _):
                dense[rows[base + k], :, lanes] = arrived[flat[base + k]]
                return _

            lax.fori_loop(0, keep, place, 0, unroll=13 if keep % 13 == 0 else 2)
        weights = dense[...].reshape(depth, 2 * block)
        result = jnp.dot(x[...], weights, preferred_element_type=F32)
        turned = jnp.transpose(result.astype(BF16))
        for half in range(2):
            for q in range(quarters):
                first = half * block + q * rows_each
                out[q, half] = turned[first : first + rows_each]

    return pl.pallas_call(
        kernel,
        out_shape=(
            jax.ShapeDtypeStruct((row_blocks, rows_each, columns * block), BF16),
            jax.ShapeDtypeStruct((quarters, columns, rows_each, tokens), BF16),
        ),
        grid_spec=pltpu.PrefetchScalarGridSpec(
            num_scalar_prefetch=2,
            grid=(columns // 2,),
            in_specs=[whole((tokens, depth)), whole((places, rows_each, block))] + waiting(after),
            out_specs=(
                pl.BlockSpec((row_blocks, rows_each, 2 * block), lambda g, f, r: (0, 0, g)),
                pl.BlockSpec((quarters, 2, rows_each, tokens), lambda g, f, r: (0, g, 0, 0)),
            ),
        ),
        compiler_params=PARAMS,
        cost_estimate=COST,
        name="forward",
    )(flat, rows, x, arrived, *after)


def share_specs(cotangents):
    near, early, late = cotangents
    _, tokens, width = near.shape
    others, _, first, _ = early.shape
    return [
        pl.BlockSpec((1, tokens, width), lambda g, *_: (g, 0, 0)),
        pl.BlockSpec((others, 1, first, width), lambda g, *_: (0, g, 0, 0)),
        pl.BlockSpec((1, others, tokens - first, width), lambda g, *_: (g, 0, 0, 0)),
    ]


def join(joined, quarter, near, early, late):
    planes, _, width = joined.shape
    first = early.shape[2]
    joined[quarter] = near[0]
    for shift in range(1, planes):
        plane = lax.rem(quarter + planes - shift, planes)
        joined[plane, :first] = early[shift - 1, 0]
        joined[plane, first:] = late[0, shift - 1]
    return joined[...].reshape(-1, width)


def forward_down(cotangents, arrived, flat, rows, quarter, order, columns, row_blocks):
    chips, tokens, width = cotangents[0][0].shape
    planes = cotangents[0][1].shape[0] + 1
    owners = 2 * chips
    places, rows_each, block = arrived.shape
    keep = flat.shape[0] // columns
    hidden = columns * rows_each
    per_owner = row_blocks // owners

    def kernel(flat, rows, quarter, order, *refs):
        shares, (arrived, out, joined, dense) = (refs[:3], refs[3:6]), refs[6:]
        step = pl.program_id(0)

        @pl.when(step == 0)
        def _():
            dense[...] = jnp.zeros_like(dense)
            out[...] = jnp.zeros_like(out)
            for c in range(columns):

                def place(k, _):
                    row = rows[c * keep + k]
                    lane = pl.multiple_of((row % per_owner) * block, block)
                    dense[row // per_owner, c * rows_each : (c + 1) * rows_each, pl.ds(lane, block)] = (
                        arrived[flat[c * keep + k]]
                    )
                    return _

                lax.fori_loop(0, keep, place, 0, unroll=13 if keep % 13 == 0 else 2)

        for core in range(2):
            out[...] += lax.dot_general(
                dense[order[2 * step + core]],
                join(joined, quarter[0], *shares[core]),
                NT,
                preferred_element_type=F32,
            )

    share = share_specs(cotangents[0])
    return pl.pallas_call(
        kernel,
        out_shape=jax.ShapeDtypeStruct((hidden, planes * tokens), F32),
        grid_spec=pltpu.PrefetchScalarGridSpec(
            num_scalar_prefetch=4,
            grid=(chips,),
            in_specs=share + share + [whole((places, rows_each, block))],
            out_specs=whole((hidden, planes * tokens)),
            scratch_shapes=[
                pltpu.VMEM((planes, tokens, width), BF16),
                pltpu.VMEM((owners, hidden, width), BF16),
            ],
        ),
        compiler_params=PARAMS,
        cost_estimate=COST,
        name="forward_down",
    )(flat, rows, quarter, order, *cotangents[0], *cotangents[1], arrived)


def weight_grad(x_turned, grad, flat, rows, places, row_blocks, factor, after=()):
    quarters, columns, rows_each, tokens = grad.shape
    depth = x_turned.shape[0]
    block = quarters * rows_each
    keep = flat.shape[0] // columns

    def kernel(flat, rows, x_turned, grad, *refs):
        out, result = refs[-2:]
        step = pl.program_id(0)
        right = jnp.concatenate(
            [grad[q, half] for half in range(2) for q in range(quarters)], axis=0
        )
        product = lax.dot_general(x_turned[...], right, NT, preferred_element_type=F32)
        result[...] = (product * factor).astype(BF16).reshape(result.shape)
        for half in range(2):
            base = (step * 2 + half) * keep
            lanes = slice(half * block, (half + 1) * block)

            def place(k, _):
                out[flat[base + k]] = result[rows[base + k], :, lanes]
                return _

            lax.fori_loop(0, keep, place, 0, unroll=13 if keep % 13 == 0 else 2)

    return pl.pallas_call(
        kernel,
        out_shape=jax.ShapeDtypeStruct((places, rows_each, block), BF16),
        grid_spec=pltpu.PrefetchScalarGridSpec(
            num_scalar_prefetch=2,
            grid=(columns // 2,),
            in_specs=[
                whole((depth, tokens)),
                pl.BlockSpec((quarters, 2, rows_each, tokens), lambda g, f, r: (0, g, 0, 0)),
            ]
            + waiting(after),
            out_specs=whole((places, rows_each, block)),
            scratch_shapes=[pltpu.VMEM((row_blocks, rows_each, 2 * block), BF16)],
        ),
        compiler_params=PARAMS,
        cost_estimate=COST,
        name="weight_grad",
    )(flat, rows, x_turned, grad, *after)


def weight_grad_down(
    value, cotangents, flat, rows, quarter, order, places, block, columns, row_blocks, factor
):
    chips, tokens, width = cotangents[0][0].shape
    planes = cotangents[0][1].shape[0] + 1
    owners = 2 * chips
    hidden = value.shape[0]
    rows_each = hidden // columns
    keep = flat.shape[0] // columns
    per_owner = row_blocks // owners

    def kernel(flat, rows, quarter, order, value, *refs):
        shares, (out, joined, result) = (refs[:3], refs[3:6]), refs[6:]
        step = pl.program_id(0)
        for core in range(2):
            right = join(joined, quarter[0], *shares[core])
            product = jnp.dot(value[...], right, preferred_element_type=F32)
            result[order[2 * step + core]] = (product * factor).astype(BF16)

        @pl.when(step == chips - 1)
        def _():
            for c in range(columns):

                def place(k, _):
                    row = rows[c * keep + k]
                    lane = pl.multiple_of((row % per_owner) * block, block)
                    out[flat[c * keep + k]] = result[
                        row // per_owner, c * rows_each : (c + 1) * rows_each, pl.ds(lane, block)
                    ]
                    return _

                lax.fori_loop(0, keep, place, 0, unroll=13 if keep % 13 == 0 else 2)

    share = share_specs(cotangents[0])
    return pl.pallas_call(
        kernel,
        out_shape=jax.ShapeDtypeStruct((places, rows_each, block), BF16),
        grid_spec=pltpu.PrefetchScalarGridSpec(
            num_scalar_prefetch=4,
            grid=(chips,),
            in_specs=[whole((hidden, planes * tokens))] + share + share,
            out_specs=whole((places, rows_each, block)),
            scratch_shapes=[
                pltpu.VMEM((planes, tokens, width), BF16),
                pltpu.VMEM((owners, hidden, width), BF16),
            ],
        ),
        compiler_params=PARAMS,
        cost_estimate=COST,
        name="weight_grad_down",
    )(flat, rows, quarter, order, value, *cotangents[0], *cotangents[1])


def input_part(weights, grad, first, chips, earlier=(), after=()):
    depth, units = weights.shape
    quarters, columns, rows_each, tokens = grad.shape
    rows = depth // (2 * chips)

    def kernel(first, left, right, grad, *refs):
        earlier, (*outs, natural) = refs[: len(refs) - len(after) - 3], refs[-3:]

        @pl.when(pl.program_id(0) == 0)
        def _():
            for c in range(columns):
                for q in range(quarters):
                    natural[c, q] = grad[q, c]

        both = jnp.concatenate([left[...], right[...]], axis=0)
        product = jnp.dot(
            both, natural[...].reshape(units, tokens), preferred_element_type=F32
        )
        for core in range(2):
            part = product[core * rows : (core + 1) * rows]
            if earlier:
                part = earlier[core][0] + part
            outs[core][0] = part.astype(outs[core].dtype)

    share = pl.BlockSpec((1, rows, tokens), lambda g, f: (g, 0, 0))
    out = jax.ShapeDtypeStruct((chips, rows, tokens), BF16 if earlier else F32)
    return pl.pallas_call(
        kernel,
        out_shape=(out, out),
        grid_spec=pltpu.PrefetchScalarGridSpec(
            num_scalar_prefetch=1,
            grid=(chips,),
            in_specs=[
                pl.BlockSpec((rows, units), lambda g, f: (2 * g + f[0], 0)),
                pl.BlockSpec((rows, units), lambda g, f: (2 * g + 1 - f[0], 0)),
                whole(grad.shape),
            ]
            + [share] * len(earlier)
            + waiting(after),
            out_specs=(share, share),
            scratch_shapes=[pltpu.VMEM((columns, quarters, rows_each, tokens), BF16)],
        ),
        compiler_params=PARAMS,
        cost_estimate=COST,
        name="input_part",
    )(first, weights, weights, grad, *earlier, *after)


def unpack(which, returned, source, total):
    places, rows_each, block = returned.shape
    slot_count = source.shape[0]

    def kernel(source, returned, *refs):
        out = refs[-1]

        def place(slot, _):
            out[0, slot] = returned[source[slot]]
            return _

        lax.fori_loop(0, slot_count, place, 0, unroll=8)

    shape = (3, slot_count, rows_each, block)
    extra = [] if total is None else [total]
    return pl.pallas_call(
        kernel,
        out_shape=jax.ShapeDtypeStruct(shape, BF16),
        grid_spec=pltpu.PrefetchScalarGridSpec(
            num_scalar_prefetch=1,
            grid=(1,),
            in_specs=[whole((places, rows_each, block))] + waiting(extra),
            out_specs=pl.BlockSpec((1,) + shape[1:], lambda g, s: (which, 0, 0, 0)),
        ),
        input_output_aliases={2: 0} if extra else {},
        compiler_params=PARAMS,
        cost_estimate=COST,
        name="unpack",
    )(source, returned, *extra)


def in_order(kept, quarter, after=()):
    count, shape = len(kept), kept[0].shape

    def kernel(quarter, *refs):
        for shift in range(count):
            refs[-1][lax.rem(quarter[0] + count - shift, count)] = refs[shift][...]

    return pl.pallas_call(
        kernel,
        out_shape=jax.ShapeDtypeStruct((count,) + shape, kept[0].dtype),
        grid_spec=pltpu.PrefetchScalarGridSpec(
            num_scalar_prefetch=1,
            grid=(1,),
            in_specs=[whole(shape)] * count + waiting(after),
            out_specs=whole((count,) + shape),
        ),
        compiler_params=PARAMS,
        cost_estimate=COST,
        name="in_order",
    )(quarter, *kept, *after)


def silu_parts(gate, up_value, grad_act):
    sigmoid_g = jax.nn.sigmoid(gate)
    activated = gate * sigmoid_g
    value = (activated * up_value).astype(BF16)
    grad_gate = (grad_act * up_value * sigmoid_g * (1.0 + gate * (1.0 - sigmoid_g))).astype(BF16)
    grad_up = (grad_act * activated).astype(BF16)
    return (value, grad_gate, grad_up)


def per_device(inputs, out_grad, int_values, scales, block_rows, holder, slot_index):
    own_count = lax.axis_size("own")
    data_count = lax.axis_size("dp")
    own_index = lax.axis_index("own")
    data_index = lax.axis_index("dp")
    local_tokens, local_width = inputs.shape
    tokens = local_tokens * data_count
    slot_count = int_values.shape[1]
    block = int_values.shape[2]
    keep = block_rows.shape[2]
    width = local_width * own_count
    row_blocks = width // block
    columns = block_rows.shape[1] // own_count
    group = columns * keep
    active = 3 * own_count // 4
    capacity = (group + active - 1) // active
    places = own_count * capacity
    rows_each = block // data_count
    depth = row_blocks * rows_each
    hidden = columns * rows_each
    factor = 1.0 / math.sqrt(tokens)

    holder_group = holder.reshape(3, own_count, group)
    slot_group = slot_index.reshape(3, own_count, group)
    mine = (holder_group == own_index).astype(jnp.int32)
    rank = jnp.cumsum(mine, axis=2) - 1
    spots = jnp.arange(capacity, dtype=jnp.int32)
    picked = (mine[..., None] == 1) & (rank[..., None] == spots)
    bucket_slot = jnp.sum(jnp.where(picked, slot_group[..., None], 0), axis=2)
    used = spots < jnp.sum(mine, axis=2)[..., None]
    hits = used[..., None] & (bucket_slot[..., None] == jnp.arange(slot_count, dtype=jnp.int32))
    bucket_index = jnp.arange(places, dtype=jnp.int32).reshape(own_count, capacity)
    source = jnp.sum(jnp.where(hits, bucket_index[None, :, :, None], 0), axis=(1, 2))
    bucket_slot = bucket_slot.reshape(3, places)
    own_holder = lax.dynamic_index_in_dim(holder_group, own_index, 1, keepdims=False)
    entries = jnp.arange(group, dtype=jnp.int32)
    earlier = (own_holder[:, :, None] == own_holder[:, None, :]) & (
        entries[None, :, None] < entries[None, None, :]
    )
    position = jnp.sum(earlier.astype(jnp.int32), axis=1)
    flat = own_holder * capacity + position
    rows = lax.dynamic_index_in_dim(
        block_rows.reshape(3, own_count, group), own_index, 1, keepdims=False
    )
    quarter = data_index.astype(jnp.int32).reshape(1)

    def exchange(parts):
        kept = [parts[0]]
        for s in range(1, data_count):
            turn = [(i, (i + s) % data_count) for i in range(data_count)]
            kept.append(lax.ppermute(parts[s], "dp", turn))
        return kept

    def to_planes(parts):
        twice = jnp.concatenate([parts, parts])
        return [
            lax.dynamic_index_in_dim(twice, data_index + s, 0, keepdims=False)
            for s in range(data_count)
        ]

    def send(which, after=()):
        sending = pack(
            which, int_values, scales[which], bucket_slot[which], quarter, rows_each, after
        )
        return sending.reshape(own_count, capacity, rows_each, block)

    def receive(sending):
        arrived = lax.all_to_all(sending, "own", split_axis=0, concat_axis=0, tiled=True)
        return arrived.reshape(places, rows_each, block)

    chips = own_count // 2
    likes = [[core + 2 * chip for chip in range(chips)] for core in range(2)]
    swap = [(i, i ^ 1) for i in range(own_count)]
    core = jnp.remainder(own_index, 2).astype(jnp.int32).reshape(1)
    turns = own_index ^ (2 * jnp.arange(chips, dtype=jnp.int32))
    order = jnp.stack([turns, turns ^ 1], axis=1).reshape(own_count)

    def over_chips(value):
        turns = [[(i, i ^ (2 * turn)) for i in range(own_count)] for turn in range(1, chips)]
        return [value] + [lax.ppermute(value, "own", turn) for turn in turns]

    near = over_chips(out_grad)
    gone = tuple(mark(part) for part in near[1:])
    near = jnp.stack(near)
    cut = local_tokens // 4
    early = exchange([near[:, :cut]] * data_count)[1:]

    late = exchange([out_grad[cut:]] * data_count)[1:]
    passed = tuple(mark(part) for part in late)

    local = inputs.reshape(local_tokens, row_blocks // own_count, data_count, rows_each)
    local = local.transpose(2, 0, 1, 3).reshape(data_count, local_tokens, depth // own_count)
    local = exchange(to_planes(local))
    sending_gate = send(0)
    local = in_order(local, quarter, (mark(sending_gate),) + gone)
    gathered = lax.all_gather(local.reshape(tokens, depth // own_count), "own", axis=0)
    sending_up, sending_down = send(1, (mark(local),)), send(2, (mark(local),) + passed)
    arrived_gate = receive(sending_gate)

    x = gathered.transpose(1, 0, 2).reshape(tokens, depth)
    x_turned = gathered.transpose(0, 2, 1).reshape(depth, tokens)
    packed = (mark(sending_up), mark(sending_down)) + tuple(mark(part) for part in early)
    gate_weights, part = forward(x, arrived_gate, flat[0], rows[0], columns, row_blocks, packed)
    gate = lax.psum_scatter(part, "dp", scatter_dimension=0)
    late = over_chips(tie(jnp.stack(late), mark(gate_weights)))
    arrived_up = receive(tie(sending_up, mark(gate_weights)))
    up_weights, part = forward(
        x,
        arrived_up,
        flat[1],
        rows[1],
        columns,
        row_blocks,
        (mark(gate),) + tuple(mark(part) for part in late[1:3]),
    )
    up_value = lax.psum_scatter(part, "dp", scatter_dimension=0)
    late = late[:3] + [tie(part, mark(up_weights)) for part in late[3:]]
    cotangents = (near, jnp.stack(early), jnp.stack(late))
    cotangents = (cotangents, [lax.ppermute(part, "own", swap) for part in cotangents])
    arrived_down = receive(tie(sending_down, mark(arrived_up)))
    grad_act = forward_down(
        cotangents, arrived_down, flat[2], rows[2], quarter, order, columns, row_blocks
    )
    value, grad_gate, grad_up = silu_parts(
        gate.reshape(hidden, tokens).astype(F32), up_value.reshape(hidden, tokens).astype(F32), grad_act
    )
    shape = (columns, rows_each, tokens)

    def give_back(leaving):
        leaving = leaving.reshape(own_count, capacity, rows_each, block)
        returned = lax.all_to_all(leaving, "own", split_axis=0, concat_axis=0, tiled=True)
        return returned.reshape(places, rows_each, block)

    all_up = lax.all_gather(grad_up.reshape(shape), "dp", axis=0)
    leaving = weight_grad_down(
        value, cotangents, flat[2], rows[2], quarter, order, places, block, columns, row_blocks, factor
    )
    all_gate = lax.all_gather(grad_gate.reshape(shape), "dp", axis=0)
    returned = give_back(leaving)
    leaving = weight_grad(
        x_turned, all_up, flat[1], rows[1], places, row_blocks, factor, (mark(returned),)
    )
    total = unpack(2, returned, source[2], None)
    returned = give_back(leaving)

    up_weights = up_weights.reshape(depth, columns * block)
    gate_weights = gate_weights.reshape(depth, columns * block)
    back = input_part(up_weights, all_up, core, chips, after=(mark(leaving),))
    back = input_part(gate_weights, all_gate, core, chips, back, (mark(returned), mark(total)))
    leaving = weight_grad(
        x_turned, all_gate, flat[0], rows[0], places, row_blocks, factor, (mark(back[0]),)
    )
    total = unpack(1, returned, source[1], total)
    returned = give_back(leaving)

    back = back[0].astype(F32) + lax.ppermute(back[1], "own", swap).astype(F32)
    back = lax.psum_scatter(
        back.astype(BF16), "own", scatter_dimension=0, axis_index_groups=likes
    )
    back = back.reshape(depth // own_count, data_count, local_tokens).transpose(1, 0, 2)
    back = tie(back, mark(total))
    back = lax.all_to_all(back, "dp", split_axis=0, concat_axis=0, tiled=True)
    back = back.reshape(data_count, row_blocks // own_count, rows_each, local_tokens)
    input_grad = back.transpose(3, 1, 0, 2).reshape(local_tokens, local_width)
    total = unpack(0, returned, source[0], total)
    return (input_grad, total)


def solution(mesh):
    placed = (
        P("dp", "own"),
        P("dp", "own"),
        P(None, "own", None, None),
        P(None, "own"),
        P(),
        P(),
        P(),
    )
    return jax.shard_map(
        per_device,
        mesh=mesh,
        in_specs=placed,
        out_specs=(P("dp", "own"), P(None, "own", "dp", None)),
        check_vma=False,
    )
```

```python
import functools
import math

import jax
import jax.numpy as jnp
from jax import lax
from jax.experimental import pallas as pl
from jax.experimental.pallas import tpu as pltpu
from jax.sharding import PartitionSpec as P

F32 = jnp.float32
BF16 = jnp.bfloat16
NT = (((1,), (1,)), ((), ()))
COST = pl.CostEstimate(flops=1024, bytes_accessed=1024, transcendentals=0)
PARAMS = pltpu.CompilerParams(vmem_limit_bytes=56 * 2**20)


def whole(shape):
    return pl.BlockSpec(shape, lambda *_: (0,) * len(shape))


def waiting(after):
    return [pl.BlockSpec(memory_space=pl.ANY)] * len(after)


def mark(value):
    return value.reshape((-1,) + value.shape[-2:])[0, :16, :128]


def tie(value, *after):
    def kernel(*refs):
        pass

    return pl.pallas_call(
        kernel,
        out_shape=jax.ShapeDtypeStruct(value.shape, value.dtype),
        in_specs=waiting((value,) + after),
        out_specs=pl.BlockSpec(memory_space=pl.ANY),
        input_output_aliases={0: 0},
        compiler_params=PARAMS,
        name="tie",
    )(value, *after)


def pack(which, ints, scales, slots, quarter, rows_each, after=()):
    slot_count, block = ints.shape[1], ints.shape[2]
    places = slots.shape[0]

    def kernel(slots, quarter, scales, ints, *refs):
        out = refs[-1]

        def place(index, _):
            slot = slots[index]
            out[index] = (ints[0, slot].astype(F32) * scales[slot]).astype(BF16)
            return _

        lax.fori_loop(0, places, place, 0, unroll=8)

    return pl.pallas_call(
        kernel,
        out_shape=jax.ShapeDtypeStruct((places, rows_each, block), BF16),
        grid_spec=pltpu.PrefetchScalarGridSpec(
            num_scalar_prefetch=3,
            grid=(1,),
            in_specs=[
                pl.BlockSpec(
                    (1, slot_count, rows_each, block), lambda g, s, q, c: (which, 0, q[0], 0)
                )
            ]
            + waiting(after),
            out_specs=whole((places, rows_each, block)),
        ),
        compiler_params=PARAMS,
        cost_estimate=COST,
        name="pack",
    )(slots, quarter, scales, ints, *after)


def forward(x, arrived, flat, rows, columns, row_blocks, after=()):
    places, rows_each, block = arrived.shape
    tokens, depth = x.shape
    keep = flat.shape[0] // columns
    quarters = block // rows_each

    def kernel(flat, rows, x, arrived, *refs):
        dense, out = refs[-2:]
        step = pl.program_id(0)
        dense[...] = jnp.zeros_like(dense)
        for half in range(2):
            base = (step * 2 + half) * keep
            lanes = slice(half * block, (half + 1) * block)

            def place(k, _):
                dense[rows[base + k], :, lanes] = arrived[flat[base + k]]
                return _

            lax.fori_loop(0, keep, place, 0, unroll=13 if keep % 13 == 0 else 2)
        weights = dense[...].reshape(depth, 2 * block)
        result = jnp.dot(x[...], weights, preferred_element_type=F32)
        turned = jnp.transpose(result.astype(BF16))
        for half in range(2):
            for q in range(quarters):
                first = half * block + q * rows_each
                out[q, half] = turned[first : first + rows_each]

    return pl.pallas_call(
        kernel,
        out_shape=(
            jax.ShapeDtypeStruct((row_blocks, rows_each, columns * block), BF16),
            jax.ShapeDtypeStruct((quarters, columns, rows_each, tokens), BF16),
        ),
        grid_spec=pltpu.PrefetchScalarGridSpec(
            num_scalar_prefetch=2,
            grid=(columns // 2,),
            in_specs=[whole((tokens, depth)), whole((places, rows_each, block))] + waiting(after),
            out_specs=(
                pl.BlockSpec((row_blocks, rows_each, 2 * block), lambda g, f, r: (0, 0, g)),
                pl.BlockSpec((quarters, 2, rows_each, tokens), lambda g, f, r: (0, g, 0, 0)),
            ),
        ),
        compiler_params=PARAMS,
        cost_estimate=COST,
        name="forward",
    )(flat, rows, x, arrived, *after)


def share_specs(cotangents):
    near, early, late = cotangents
    _, tokens, width = near.shape
    others, _, first, _ = early.shape
    return [
        pl.BlockSpec((1, tokens, width), lambda g, *_: (g, 0, 0)),
        pl.BlockSpec((others, 1, first, width), lambda g, *_: (0, g, 0, 0)),
        pl.BlockSpec((1, others, tokens - first, width), lambda g, *_: (g, 0, 0, 0)),
    ]


def join(joined, quarter, near, early, late):
    planes, _, width = joined.shape
    first = early.shape[2]
    joined[quarter] = near[0]
    for shift in range(1, planes):
        plane = lax.rem(quarter + planes - shift, planes)
        joined[plane, :first] = early[shift - 1, 0]
        joined[plane, first:] = late[0, shift - 1]
    return joined[...].reshape(-1, width)


def build_down(arrived, flat, rows, columns, row_blocks, owners):
    places, rows_each, block = arrived.shape
    keep = flat.shape[0] // columns
    per_owner = row_blocks // owners
    shape = (owners, columns * rows_each, per_owner * block)

    def kernel(flat, rows, arrived, dense):
        dense[...] = jnp.zeros_like(dense)
        for c in range(columns):

            def place(k, _):
                row = rows[c * keep + k]
                lane = pl.multiple_of((row % per_owner) * block, block)
                dense[row // per_owner, c * rows_each : (c + 1) * rows_each, pl.ds(lane, block)] = (
                    arrived[flat[c * keep + k]]
                )
                return _

            lax.fori_loop(0, keep, place, 0, unroll=13 if keep % 13 == 0 else 2)

    return pl.pallas_call(
        kernel,
        out_shape=jax.ShapeDtypeStruct(shape, BF16),
        grid_spec=pltpu.PrefetchScalarGridSpec(
            num_scalar_prefetch=2,
            grid=(1,),
            in_specs=[whole((places, rows_each, block))],
            out_specs=whole(shape),
        ),
        compiler_params=PARAMS,
        cost_estimate=COST,
        name="build_down",
    )(flat, rows, arrived)


def forward_down(cotangents, dense, quarter, order):
    chips, tokens, width = cotangents[0][0].shape
    planes = cotangents[0][1].shape[0] + 1
    hidden = dense.shape[1]

    def kernel(quarter, order, *refs):
        shares, weights, (out, joined) = (refs[:3], refs[3:6]), refs[6:8], refs[8:]

        @pl.when(pl.program_id(0) == 0)
        def _():
            out[...] = jnp.zeros_like(out)

        for core in range(2):
            right = join(joined, quarter[0], *shares[core])
            out[...] += lax.dot_general(weights[core][0], right, NT, preferred_element_type=F32)

    share = share_specs(cotangents[0])
    return pl.pallas_call(
        kernel,
        out_shape=jax.ShapeDtypeStruct((hidden, planes * tokens), F32),
        grid_spec=pltpu.PrefetchScalarGridSpec(
            num_scalar_prefetch=2,
            grid=(chips,),
            in_specs=share
            + share
            + [
                pl.BlockSpec((1, hidden, width), lambda g, q, o: (o[2 * g], 0, 0)),
                pl.BlockSpec((1, hidden, width), lambda g, q, o: (o[2 * g + 1], 0, 0)),
            ],
            out_specs=whole((hidden, planes * tokens)),
            scratch_shapes=[pltpu.VMEM((planes, tokens, width), BF16)],
        ),
        compiler_params=PARAMS,
        cost_estimate=COST,
        name="forward_down",
    )(quarter, order, *cotangents[0], *cotangents[1], dense, dense)


def weight_grad(x_turned, grad, flat, rows, places, row_blocks, factor, after=()):
    quarters, columns, rows_each, tokens = grad.shape
    depth = x_turned.shape[0]
    block = quarters * rows_each
    keep = flat.shape[0] // columns

    def kernel(flat, rows, x_turned, grad, *refs):
        out, result = refs[-2:]
        step = pl.program_id(0)
        right = jnp.concatenate(
            [grad[q, half] for half in range(2) for q in range(quarters)], axis=0
        )
        product = lax.dot_general(x_turned[...], right, NT, preferred_element_type=F32)
        result[...] = (product * factor).astype(BF16).reshape(result.shape)
        for half in range(2):
            base = (step * 2 + half) * keep
            lanes = slice(half * block, (half + 1) * block)

            def place(k, _):
                out[flat[base + k]] = result[rows[base + k], :, lanes]
                return _

            lax.fori_loop(0, keep, place, 0, unroll=13 if keep % 13 == 0 else 2)

    return pl.pallas_call(
        kernel,
        out_shape=jax.ShapeDtypeStruct((places, rows_each, block), BF16),
        grid_spec=pltpu.PrefetchScalarGridSpec(
            num_scalar_prefetch=2,
            grid=(columns // 2,),
            in_specs=[
                whole((depth, tokens)),
                pl.BlockSpec((quarters, 2, rows_each, tokens), lambda g, f, r: (0, g, 0, 0)),
            ]
            + waiting(after),
            out_specs=whole((places, rows_each, block)),
            scratch_shapes=[pltpu.VMEM((row_blocks, rows_each, 2 * block), BF16)],
        ),
        compiler_params=PARAMS,
        cost_estimate=COST,
        name="weight_grad",
    )(flat, rows, x_turned, grad, *after)


def weight_grad_down(
    value, cotangents, flat, rows, quarter, order, places, block, columns, row_blocks, factor
):
    chips, tokens, width = cotangents[0][0].shape
    planes = cotangents[0][1].shape[0] + 1
    owners = 2 * chips
    hidden = value.shape[0]
    rows_each = hidden // columns
    keep = flat.shape[0] // columns
    per_owner = row_blocks // owners

    def kernel(flat, rows, quarter, order, value, *refs):
        shares, (out, joined, result) = (refs[:3], refs[3:6]), refs[6:]
        step = pl.program_id(0)
        for core in range(2):
            right = join(joined, quarter[0], *shares[core])
            product = jnp.dot(value[...], right, preferred_element_type=F32)
            result[order[2 * step + core]] = (product * factor).astype(BF16)

        @pl.when(step == chips - 1)
        def _():
            for c in range(columns):

                def place(k, _):
                    row = rows[c * keep + k]
                    lane = pl.multiple_of((row % per_owner) * block, block)
                    out[flat[c * keep + k]] = result[
                        row // per_owner, c * rows_each : (c + 1) * rows_each, pl.ds(lane, block)
                    ]
                    return _

                lax.fori_loop(0, keep, place, 0, unroll=13 if keep % 13 == 0 else 2)

    share = share_specs(cotangents[0])
    return pl.pallas_call(
        kernel,
        out_shape=jax.ShapeDtypeStruct((places, rows_each, block), BF16),
        grid_spec=pltpu.PrefetchScalarGridSpec(
            num_scalar_prefetch=4,
            grid=(chips,),
            in_specs=[whole((hidden, planes * tokens))] + share + share,
            out_specs=whole((places, rows_each, block)),
            scratch_shapes=[
                pltpu.VMEM((planes, tokens, width), BF16),
                pltpu.VMEM((owners, hidden, width), BF16),
            ],
        ),
        compiler_params=PARAMS,
        cost_estimate=COST,
        name="weight_grad_down",
    )(flat, rows, quarter, order, value, *cotangents[0], *cotangents[1])


def input_part(weights, grad, first, chips, earlier=(), after=()):
    depth, units = weights.shape
    quarters, columns, rows_each, tokens = grad.shape
    rows = depth // (2 * chips)

    def kernel(first, left, right, grad, *refs):
        earlier, (*outs, natural) = refs[: len(refs) - len(after) - 3], refs[-3:]

        @pl.when(pl.program_id(0) == 0)
        def _():
            for c in range(columns):
                for q in range(quarters):
                    natural[c, q] = grad[q, c]

        both = jnp.concatenate([left[...], right[...]], axis=0)
        product = jnp.dot(
            both, natural[...].reshape(units, tokens), preferred_element_type=F32
        )
        for core in range(2):
            part = product[core * rows : (core + 1) * rows]
            if earlier:
                part = earlier[core][0] + part
            outs[core][0] = part.astype(outs[core].dtype)

    share = pl.BlockSpec((1, rows, tokens), lambda g, f: (g, 0, 0))
    out = jax.ShapeDtypeStruct((chips, rows, tokens), BF16 if earlier else F32)
    return pl.pallas_call(
        kernel,
        out_shape=(out, out),
        grid_spec=pltpu.PrefetchScalarGridSpec(
            num_scalar_prefetch=1,
            grid=(chips,),
            in_specs=[
                pl.BlockSpec((rows, units), lambda g, f: (2 * g + f[0], 0)),
                pl.BlockSpec((rows, units), lambda g, f: (2 * g + 1 - f[0], 0)),
                whole(grad.shape),
            ]
            + [share] * len(earlier)
            + waiting(after),
            out_specs=(share, share),
            scratch_shapes=[pltpu.VMEM((columns, quarters, rows_each, tokens), BF16)],
        ),
        compiler_params=PARAMS,
        cost_estimate=COST,
        name="input_part",
    )(first, weights, weights, grad, *earlier, *after)


def unpack(which, returned, source, total):
    places, rows_each, block = returned.shape
    slot_count = source.shape[0]

    def kernel(source, returned, *refs):
        out = refs[-1]

        def place(slot, _):
            out[0, slot] = returned[source[slot]]
            return _

        lax.fori_loop(0, slot_count, place, 0, unroll=8)

    shape = (3, slot_count, rows_each, block)
    extra = [] if total is None else [total]
    return pl.pallas_call(
        kernel,
        out_shape=jax.ShapeDtypeStruct(shape, BF16),
        grid_spec=pltpu.PrefetchScalarGridSpec(
            num_scalar_prefetch=1,
            grid=(1,),
            in_specs=[whole((places, rows_each, block))] + waiting(extra),
            out_specs=pl.BlockSpec((1,) + shape[1:], lambda g, s: (which, 0, 0, 0)),
        ),
        input_output_aliases={2: 0} if extra else {},
        compiler_params=PARAMS,
        cost_estimate=COST,
        name="unpack",
    )(source, returned, *extra)


def bundle(local, cotangent, quarter):
    planes, tokens, share = local.shape
    rows = tokens // planes
    total, width = rows + cotangent.shape[0], cotangent.shape[1]

    def kernel(quarter, local, cotangent, *outs):
        for shift in range(1, planes):
            plane = lax.rem(quarter[0] + shift, planes)
            for part in range(planes):
                outs[shift - 1][:rows, part * share : (part + 1) * share] = local[
                    plane, part * rows : (part + 1) * rows
                ]
            outs[shift - 1][rows:] = cotangent[...]

    return pl.pallas_call(
        kernel,
        out_shape=[jax.ShapeDtypeStruct((total, width), BF16)] * (planes - 1),
        grid_spec=pltpu.PrefetchScalarGridSpec(
            num_scalar_prefetch=1,
            grid=(1,),
            in_specs=[whole(local.shape), whole(cotangent.shape)],
            out_specs=[whole((total, width))] * (planes - 1),
        ),
        compiler_params=PARAMS,
        cost_estimate=COST,
        name="bundle",
    )(quarter, local, cotangent)


def unbundle(local, bundles, quarter, after=()):
    planes, tokens, share = local.shape
    rows = tokens // planes

    def kernel(quarter, local, *refs):
        out = refs[-1]
        out[quarter[0]] = local[quarter[0]]
        for shift in range(1, planes):
            plane = lax.rem(quarter[0] + planes - shift, planes)
            for part in range(planes):
                out[plane, part * rows : (part + 1) * rows] = refs[shift - 1][
                    :rows, part * share : (part + 1) * share
                ]

    return pl.pallas_call(
        kernel,
        out_shape=jax.ShapeDtypeStruct(local.shape, BF16),
        grid_spec=pltpu.PrefetchScalarGridSpec(
            num_scalar_prefetch=1,
            grid=(1,),
            in_specs=[whole(local.shape)] + [whole(part.shape) for part in bundles] + waiting(after),
            out_specs=whole(local.shape),
        ),
        compiler_params=PARAMS,
        cost_estimate=COST,
        name="unbundle",
    )(quarter, local, *bundles, *after)


def silu_parts(gate, up_value, grad_act):
    sigmoid_g = jax.nn.sigmoid(gate)
    activated = gate * sigmoid_g
    value = (activated * up_value).astype(BF16)
    grad_gate = (grad_act * up_value * sigmoid_g * (1.0 + gate * (1.0 - sigmoid_g))).astype(BF16)
    grad_up = (grad_act * activated).astype(BF16)
    return (value, grad_gate, grad_up)


def per_device(inputs, out_grad, int_values, scales, block_rows, holder, slot_index):
    own_count = lax.axis_size("own")
    data_count = lax.axis_size("dp")
    own_index = lax.axis_index("own")
    data_index = lax.axis_index("dp")
    local_tokens, local_width = inputs.shape
    tokens = local_tokens * data_count
    slot_count = int_values.shape[1]
    block = int_values.shape[2]
    keep = block_rows.shape[2]
    width = local_width * own_count
    row_blocks = width // block
    columns = block_rows.shape[1] // own_count
    group = columns * keep
    active = 3 * own_count // 4
    capacity = (group + active - 1) // active
    places = own_count * capacity
    rows_each = block // data_count
    depth = row_blocks * rows_each
    hidden = columns * rows_each
    factor = 1.0 / math.sqrt(tokens)

    holder_group = holder.reshape(3, own_count, group)
    slot_group = slot_index.reshape(3, own_count, group)
    mine = (holder_group == own_index).astype(jnp.int32)
    rank = jnp.cumsum(mine, axis=2) - 1
    spots = jnp.arange(capacity, dtype=jnp.int32)
    picked = (mine[..., None] == 1) & (rank[..., None] == spots)
    bucket_slot = jnp.sum(jnp.where(picked, slot_group[..., None], 0), axis=2)
    used = spots < jnp.sum(mine, axis=2)[..., None]
    hits = used[..., None] & (bucket_slot[..., None] == jnp.arange(slot_count, dtype=jnp.int32))
    bucket_index = jnp.arange(places, dtype=jnp.int32).reshape(own_count, capacity)
    source = jnp.sum(jnp.where(hits, bucket_index[None, :, :, None], 0), axis=(1, 2))
    bucket_slot = bucket_slot.reshape(3, places)
    own_holder = lax.dynamic_index_in_dim(holder_group, own_index, 1, keepdims=False)
    entries = jnp.arange(group, dtype=jnp.int32)
    earlier = (own_holder[:, :, None] == own_holder[:, None, :]) & (
        entries[None, :, None] < entries[None, None, :]
    )
    position = jnp.sum(earlier.astype(jnp.int32), axis=1)
    flat = own_holder * capacity + position
    rows = lax.dynamic_index_in_dim(
        block_rows.reshape(3, own_count, group), own_index, 1, keepdims=False
    )
    quarter = data_index.astype(jnp.int32).reshape(1)

    def exchange(parts):
        return [
            lax.ppermute(part, "dp", [(i, (i + s) % data_count) for i in range(data_count)])
            for s, part in enumerate(parts, 1)
        ]

    def send(which, after=()):
        sending = pack(
            which, int_values, scales[which], bucket_slot[which], quarter, rows_each, after
        )
        return sending.reshape(own_count, capacity, rows_each, block)

    def receive(sending):
        arrived = lax.all_to_all(sending, "own", split_axis=0, concat_axis=0, tiled=True)
        return arrived.reshape(places, rows_each, block)

    chips = own_count // 2
    likes = [[core + 2 * chip for chip in range(chips)] for core in range(2)]
    swap = [(i, i ^ 1) for i in range(own_count)]
    core = jnp.remainder(own_index, 2).astype(jnp.int32).reshape(1)
    turns = own_index ^ (2 * jnp.arange(chips, dtype=jnp.int32))
    order = jnp.stack([turns, turns ^ 1], axis=1).reshape(own_count)

    def over_chips(value):
        turns = [[(i, i ^ (2 * turn)) for i in range(own_count)] for turn in range(1, chips)]
        return [value] + [lax.ppermute(value, "own", turn) for turn in turns]

    near = over_chips(out_grad)
    gone = tuple(mark(part) for part in near[1:])
    near = jnp.stack(near)
    cut = local_tokens // 4
    early = exchange([near[:, :cut]] * (data_count - 1))

    local = inputs.reshape(local_tokens, row_blocks // own_count, data_count, rows_each)
    local = local.transpose(2, 0, 1, 3).reshape(data_count, local_tokens, depth // own_count)
    bundles = exchange(bundle(local, out_grad[cut:], quarter))
    sending_gate = send(0)
    local = unbundle(local, bundles, quarter, (mark(sending_gate),) + gone)
    late = jnp.stack([part[local_tokens // data_count :] for part in bundles])
    gathered = lax.all_gather(local.reshape(tokens, depth // own_count), "own", axis=0)
    sending_up, sending_down = send(1, (mark(local),)), send(2, (mark(local),))
    arrived_gate = receive(sending_gate)

    x = gathered.transpose(1, 0, 2).reshape(tokens, depth)
    x_turned = gathered.transpose(0, 2, 1).reshape(depth, tokens)
    packed = (mark(sending_up), mark(sending_down)) + tuple(mark(part) for part in early)
    gate_weights, part = forward(x, arrived_gate, flat[0], rows[0], columns, row_blocks, packed)
    gate = lax.psum_scatter(part, "dp", scatter_dimension=0)
    late = over_chips(tie(late, mark(gate_weights)))
    arrived_up = receive(tie(sending_up, mark(gate_weights)))
    up_weights, part = forward(
        x,
        arrived_up,
        flat[1],
        rows[1],
        columns,
        row_blocks,
        (mark(gate),) + tuple(mark(part) for part in late[1:3]),
    )
    up_value = lax.psum_scatter(part, "dp", scatter_dimension=0)
    late = late[:3] + [tie(part, mark(up_weights)) for part in late[3:]]
    arrived_down = receive(tie(sending_down, mark(up_weights)))
    down_weights = build_down(arrived_down, flat[2], rows[2], columns, row_blocks, own_count)
    cotangents = (near, jnp.stack(early), tie(jnp.stack(late), mark(arrived_down)))
    cotangents = (cotangents, [lax.ppermute(part, "own", swap) for part in cotangents])
    grad_act = forward_down(cotangents, down_weights, quarter, order)
    value, grad_gate, grad_up = silu_parts(
        gate.reshape(hidden, tokens).astype(F32), up_value.reshape(hidden, tokens).astype(F32), grad_act
    )
    shape = (columns, rows_each, tokens)

    def give_back(leaving):
        leaving = leaving.reshape(own_count, capacity, rows_each, block)
        returned = lax.all_to_all(leaving, "own", split_axis=0, concat_axis=0, tiled=True)
        return returned.reshape(places, rows_each, block)

    all_up = lax.all_gather(grad_up.reshape(shape), "dp", axis=0)
    leaving = weight_grad_down(
        value, cotangents, flat[2], rows[2], quarter, order, places, block, columns, row_blocks, factor
    )
    all_gate = lax.all_gather(grad_gate.reshape(shape), "dp", axis=0)
    returned = give_back(leaving)
    leaving = weight_grad(
        x_turned, all_up, flat[1], rows[1], places, row_blocks, factor, (mark(returned),)
    )
    total = unpack(2, returned, source[2], None)
    returned = give_back(leaving)

    up_weights = up_weights.reshape(depth, columns * block)
    gate_weights = gate_weights.reshape(depth, columns * block)
    back = input_part(up_weights, all_up, core, chips, after=(mark(leaving),))
    done = (mark(returned), mark(total), mark(back[0]))
    leaving = weight_grad(
        x_turned, all_gate, flat[0], rows[0], places, row_blocks, factor, done
    )
    back = input_part(gate_weights, all_gate, core, chips, back, (mark(leaving),))
    total = unpack(1, returned, source[1], total)
    returned = give_back(leaving)

    back = back[0].astype(F32) + lax.ppermute(back[1], "own", swap).astype(F32)
    back = lax.psum_scatter(
        back.astype(BF16), "own", scatter_dimension=0, axis_index_groups=likes
    )
    back = back.reshape(depth // own_count, data_count, local_tokens).transpose(1, 0, 2)
    back = tie(back, mark(total))
    back = lax.all_to_all(back, "dp", split_axis=0, concat_axis=0, tiled=True)
    back = back.reshape(data_count, row_blocks // own_count, rows_each, local_tokens)
    input_grad = back.transpose(3, 1, 0, 2).reshape(local_tokens, local_width)
    total = unpack(0, returned, source[0], total)
    return (input_grad, total)


def solution(mesh):
    placed = (
        P("dp", "own"),
        P("dp", "own"),
        P(None, "own", None, None),
        P(None, "own"),
        P(),
        P(),
        P(),
    )
    return jax.shard_map(
        per_device,
        mesh=mesh,
        in_specs=placed,
        out_specs=(P("dp", "own"), P(None, "own", "dp", None)),
        check_vma=False,
    )
```

```python
import functools
import math

import jax
import jax.numpy as jnp
from jax import lax
from jax.experimental import pallas as pl
from jax.experimental.pallas import tpu as pltpu
from jax.sharding import PartitionSpec as P

F32 = jnp.float32
BF16 = jnp.bfloat16
NT = (((1,), (1,)), ((), ()))
COST = pl.CostEstimate(flops=1024, bytes_accessed=1024, transcendentals=0)
PARAMS = pltpu.CompilerParams(vmem_limit_bytes=56 * 2**20)


def whole(shape):
    return pl.BlockSpec(shape, lambda *_: (0,) * len(shape))


def waiting(after):
    return [pl.BlockSpec(memory_space=pl.ANY)] * len(after)


def mark(value):
    return value.reshape((-1,) + value.shape[-2:])[0, :16, :128]


def tie(value, *after):
    def kernel(*refs):
        pass

    return pl.pallas_call(
        kernel,
        out_shape=jax.ShapeDtypeStruct(value.shape, value.dtype),
        in_specs=waiting((value,) + after),
        out_specs=pl.BlockSpec(memory_space=pl.ANY),
        input_output_aliases={0: 0},
        compiler_params=PARAMS,
        name="tie",
    )(value, *after)


def pack(which, ints, scales, slots, quarter, rows_each, after=()):
    slot_count, block = ints.shape[1], ints.shape[2]
    places = slots.shape[0]

    def kernel(slots, quarter, scales, ints, *refs):
        out = refs[-1]

        def place(index, _):
            slot = slots[index]
            out[index] = (ints[0, slot].astype(F32) * scales[slot]).astype(BF16)
            return _

        lax.fori_loop(0, places, place, 0, unroll=8)

    return pl.pallas_call(
        kernel,
        out_shape=jax.ShapeDtypeStruct((places, rows_each, block), BF16),
        grid_spec=pltpu.PrefetchScalarGridSpec(
            num_scalar_prefetch=3,
            grid=(1,),
            in_specs=[
                pl.BlockSpec(
                    (1, slot_count, rows_each, block), lambda g, s, q, c: (which, 0, q[0], 0)
                )
            ]
            + waiting(after),
            out_specs=whole((places, rows_each, block)),
        ),
        compiler_params=PARAMS,
        cost_estimate=COST,
        name="pack",
    )(slots, quarter, scales, ints, *after)


def forward(x, arrived, flat, rows, columns, row_blocks, after=()):
    places, rows_each, block = arrived.shape
    tokens, depth = x.shape
    keep = flat.shape[0] // columns
    quarters = block // rows_each

    def kernel(flat, rows, x, arrived, *refs):
        dense, out = refs[-2:]
        step = pl.program_id(0)
        dense[...] = jnp.zeros_like(dense)
        for half in range(2):
            base = (step * 2 + half) * keep
            lanes = slice(half * block, (half + 1) * block)

            def place(k, _):
                dense[rows[base + k], :, lanes] = arrived[flat[base + k]]
                return _

            lax.fori_loop(0, keep, place, 0, unroll=13 if keep % 13 == 0 else 2)
        weights = dense[...].reshape(depth, 2 * block)
        result = jnp.dot(x[...], weights, preferred_element_type=F32)
        turned = jnp.transpose(result.astype(BF16))
        for half in range(2):
            for q in range(quarters):
                first = half * block + q * rows_each
                out[q, half] = turned[first : first + rows_each]

    return pl.pallas_call(
        kernel,
        out_shape=(
            jax.ShapeDtypeStruct((row_blocks, rows_each, columns * block), BF16),
            jax.ShapeDtypeStruct((quarters, columns, rows_each, tokens), BF16),
        ),
        grid_spec=pltpu.PrefetchScalarGridSpec(
            num_scalar_prefetch=2,
            grid=(columns // 2,),
            in_specs=[whole((tokens, depth)), whole((places, rows_each, block))] + waiting(after),
            out_specs=(
                pl.BlockSpec((row_blocks, rows_each, 2 * block), lambda g, f, r: (0, 0, g)),
                pl.BlockSpec((quarters, 2, rows_each, tokens), lambda g, f, r: (0, g, 0, 0)),
            ),
        ),
        compiler_params=PARAMS,
        cost_estimate=COST,
        name="forward",
    )(flat, rows, x, arrived, *after)


def share_specs(cotangents):
    near, early, late = cotangents
    _, tokens, width = near.shape
    others, _, first, _ = early.shape
    return [
        pl.BlockSpec((1, tokens, width), lambda g, *_: (g, 0, 0)),
        pl.BlockSpec((others, 1, first, width), lambda g, *_: (0, g, 0, 0)),
        pl.BlockSpec((1, others, tokens - first, width), lambda g, *_: (g, 0, 0, 0)),
    ]


def join(joined, quarter, near, early, late):
    planes, _, width = joined.shape
    first = early.shape[2]
    joined[quarter] = near[0]
    for shift in range(1, planes):
        plane = lax.rem(quarter + planes - shift, planes)
        joined[plane, :first] = early[shift - 1, 0]
        joined[plane, first:] = late[0, shift - 1]
    return joined[...].reshape(-1, width)


def forward_down(cotangents, arrived, flat, rows, quarter, order, columns, row_blocks):
    chips, tokens, width = cotangents[0][0].shape
    planes = cotangents[0][1].shape[0] + 1
    owners = 2 * chips
    places, rows_each, block = arrived.shape
    keep = flat.shape[0] // columns
    hidden = columns * rows_each
    per_owner = row_blocks // owners

    def kernel(flat, rows, quarter, order, *refs):
        shares, (arrived, out, joined, dense) = (refs[:3], refs[3:6]), refs[6:]
        step = pl.program_id(0)

        @pl.when(step == 0)
        def _():
            dense[...] = jnp.zeros_like(dense)
            out[...] = jnp.zeros_like(out)
            for c in range(columns):

                def place(k, _):
                    row = rows[c * keep + k]
                    lane = pl.multiple_of((row % per_owner) * block, block)
                    dense[row // per_owner, c * rows_each : (c + 1) * rows_each, pl.ds(lane, block)] = (
                        arrived[flat[c * keep + k]]
                    )
                    return _

                lax.fori_loop(0, keep, place, 0, unroll=13 if keep % 13 == 0 else 2)

        for core in range(2):
            out[...] += lax.dot_general(
                dense[order[2 * step + core]],
                join(joined, quarter[0], *shares[core]),
                NT,
                preferred_element_type=F32,
            )

    share = share_specs(cotangents[0])
    return pl.pallas_call(
        kernel,
        out_shape=jax.ShapeDtypeStruct((hidden, planes * tokens), F32),
        grid_spec=pltpu.PrefetchScalarGridSpec(
            num_scalar_prefetch=4,
            grid=(chips,),
            in_specs=share + share + [whole((places, rows_each, block))],
            out_specs=whole((hidden, planes * tokens)),
            scratch_shapes=[
                pltpu.VMEM((planes, tokens, width), BF16),
                pltpu.VMEM((owners, hidden, width), BF16),
            ],
        ),
        compiler_params=PARAMS,
        cost_estimate=COST,
        name="forward_down",
    )(flat, rows, quarter, order, *cotangents[0], *cotangents[1], arrived)


def weight_grad(x_turned, grad, flat, rows, places, row_blocks, factor, after=()):
    quarters, columns, rows_each, tokens = grad.shape
    depth = x_turned.shape[0]
    block = quarters * rows_each
    keep = flat.shape[0] // columns

    def kernel(flat, rows, x_turned, grad, *refs):
        out, result = refs[-2:]
        step = pl.program_id(0)
        right = jnp.concatenate(
            [grad[q, half] for half in range(2) for q in range(quarters)], axis=0
        )
        product = lax.dot_general(x_turned[...], right, NT, preferred_element_type=F32)
        result[...] = (product * factor).astype(BF16).reshape(result.shape)
        for half in range(2):
            base = (step * 2 + half) * keep
            lanes = slice(half * block, (half + 1) * block)

            def place(k, _):
                out[flat[base + k]] = result[rows[base + k], :, lanes]
                return _

            lax.fori_loop(0, keep, place, 0, unroll=13 if keep % 13 == 0 else 2)

    return pl.pallas_call(
        kernel,
        out_shape=jax.ShapeDtypeStruct((places, rows_each, block), BF16),
        grid_spec=pltpu.PrefetchScalarGridSpec(
            num_scalar_prefetch=2,
            grid=(columns // 2,),
            in_specs=[
                whole((depth, tokens)),
                pl.BlockSpec((quarters, 2, rows_each, tokens), lambda g, f, r: (0, g, 0, 0)),
            ]
            + waiting(after),
            out_specs=whole((places, rows_each, block)),
            scratch_shapes=[pltpu.VMEM((row_blocks, rows_each, 2 * block), BF16)],
        ),
        compiler_params=PARAMS,
        cost_estimate=COST,
        name="weight_grad",
    )(flat, rows, x_turned, grad, *after)


def weight_grad_down(
    value, cotangents, flat, rows, quarter, order, places, block, columns, row_blocks, factor
):
    chips, tokens, width = cotangents[0][0].shape
    planes = cotangents[0][1].shape[0] + 1
    owners = 2 * chips
    hidden = value.shape[0]
    rows_each = hidden // columns
    keep = flat.shape[0] // columns
    per_owner = row_blocks // owners

    def kernel(flat, rows, quarter, order, value, *refs):
        shares, (out, joined, result) = (refs[:3], refs[3:6]), refs[6:]
        step = pl.program_id(0)
        for core in range(2):
            right = join(joined, quarter[0], *shares[core])
            product = jnp.dot(value[...], right, preferred_element_type=F32)
            result[order[2 * step + core]] = (product * factor).astype(BF16)

        @pl.when(step == chips - 1)
        def _():
            for c in range(columns):

                def place(k, _):
                    row = rows[c * keep + k]
                    lane = pl.multiple_of((row % per_owner) * block, block)
                    out[flat[c * keep + k]] = result[
                        row // per_owner, c * rows_each : (c + 1) * rows_each, pl.ds(lane, block)
                    ]
                    return _

                lax.fori_loop(0, keep, place, 0, unroll=13 if keep % 13 == 0 else 2)

    share = share_specs(cotangents[0])
    return pl.pallas_call(
        kernel,
        out_shape=jax.ShapeDtypeStruct((places, rows_each, block), BF16),
        grid_spec=pltpu.PrefetchScalarGridSpec(
            num_scalar_prefetch=4,
            grid=(chips,),
            in_specs=[whole((hidden, planes * tokens))] + share + share,
            out_specs=whole((places, rows_each, block)),
            scratch_shapes=[
                pltpu.VMEM((planes, tokens, width), BF16),
                pltpu.VMEM((owners, hidden, width), BF16),
            ],
        ),
        compiler_params=PARAMS,
        cost_estimate=COST,
        name="weight_grad_down",
    )(flat, rows, quarter, order, value, *cotangents[0], *cotangents[1])


def input_part(weights, grad, first, chips, earlier=(), after=()):
    depth, units = weights.shape
    quarters, columns, rows_each, tokens = grad.shape
    rows = depth // (2 * chips)

    def kernel(first, left, right, grad, *refs):
        earlier, (*outs, natural) = refs[: len(refs) - len(after) - 3], refs[-3:]

        @pl.when(pl.program_id(0) == 0)
        def _():
            for c in range(columns):
                for q in range(quarters):
                    natural[c, q] = grad[q, c]

        both = jnp.concatenate([left[...], right[...]], axis=0)
        product = jnp.dot(
            both, natural[...].reshape(units, tokens), preferred_element_type=F32
        )
        for core in range(2):
            part = product[core * rows : (core + 1) * rows]
            if earlier:
                part = earlier[core][0] + part
            outs[core][0] = part.astype(outs[core].dtype)

    share = pl.BlockSpec((1, rows, tokens), lambda g, f: (g, 0, 0))
    out = jax.ShapeDtypeStruct((chips, rows, tokens), BF16 if earlier else F32)
    return pl.pallas_call(
        kernel,
        out_shape=(out, out),
        grid_spec=pltpu.PrefetchScalarGridSpec(
            num_scalar_prefetch=1,
            grid=(chips,),
            in_specs=[
                pl.BlockSpec((rows, units), lambda g, f: (2 * g + f[0], 0)),
                pl.BlockSpec((rows, units), lambda g, f: (2 * g + 1 - f[0], 0)),
                whole(grad.shape),
            ]
            + [share] * len(earlier)
            + waiting(after),
            out_specs=(share, share),
            scratch_shapes=[pltpu.VMEM((columns, quarters, rows_each, tokens), BF16)],
        ),
        compiler_params=PARAMS,
        cost_estimate=COST,
        name="input_part",
    )(first, weights, weights, grad, *earlier, *after)


def unpack(which, returned, source, total):
    places, rows_each, block = returned.shape
    slot_count = source.shape[0]

    def kernel(source, returned, *refs):
        out = refs[-1]

        def place(slot, _):
            out[0, slot] = returned[source[slot]]
            return _

        lax.fori_loop(0, slot_count, place, 0, unroll=8)

    shape = (3, slot_count, rows_each, block)
    extra = [] if total is None else [total]
    return pl.pallas_call(
        kernel,
        out_shape=jax.ShapeDtypeStruct(shape, BF16),
        grid_spec=pltpu.PrefetchScalarGridSpec(
            num_scalar_prefetch=1,
            grid=(1,),
            in_specs=[whole((places, rows_each, block))] + waiting(extra),
            out_specs=pl.BlockSpec((1,) + shape[1:], lambda g, s: (which, 0, 0, 0)),
        ),
        input_output_aliases={2: 0} if extra else {},
        compiler_params=PARAMS,
        cost_estimate=COST,
        name="unpack",
    )(source, returned, *extra)


def in_order(kept, quarter, after=()):
    count, shape = len(kept), kept[0].shape

    def kernel(quarter, *refs):
        for shift in range(count):
            refs[-1][lax.rem(quarter[0] + count - shift, count)] = refs[shift][...]

    return pl.pallas_call(
        kernel,
        out_shape=jax.ShapeDtypeStruct((count,) + shape, kept[0].dtype),
        grid_spec=pltpu.PrefetchScalarGridSpec(
            num_scalar_prefetch=1,
            grid=(1,),
            in_specs=[whole(shape)] * count + waiting(after),
            out_specs=whole((count,) + shape),
        ),
        compiler_params=PARAMS,
        cost_estimate=COST,
        name="in_order",
    )(quarter, *kept, *after)


def silu_parts(gate, up_value, grad_act):
    sigmoid_g = jax.nn.sigmoid(gate)
    activated = gate * sigmoid_g
    value = (activated * up_value).astype(BF16)
    grad_gate = (grad_act * up_value * sigmoid_g * (1.0 + gate * (1.0 - sigmoid_g))).astype(BF16)
    grad_up = (grad_act * activated).astype(BF16)
    return (value, grad_gate, grad_up)


def per_device(inputs, out_grad, int_values, scales, block_rows, holder, slot_index):
    own_count = lax.axis_size("own")
    data_count = lax.axis_size("dp")
    own_index = lax.axis_index("own")
    data_index = lax.axis_index("dp")
    local_tokens, local_width = inputs.shape
    tokens = local_tokens * data_count
    slot_count = int_values.shape[1]
    block = int_values.shape[2]
    keep = block_rows.shape[2]
    width = local_width * own_count
    row_blocks = width // block
    columns = block_rows.shape[1] // own_count
    group = columns * keep
    active = 3 * own_count // 4
    capacity = (group + active - 1) // active
    places = own_count * capacity
    rows_each = block // data_count
    depth = row_blocks * rows_each
    hidden = columns * rows_each
    factor = 1.0 / math.sqrt(tokens)

    holder_group = holder.reshape(3, own_count, group)
    slot_group = slot_index.reshape(3, own_count, group)
    mine = (holder_group == own_index).astype(jnp.int32)
    rank = jnp.cumsum(mine, axis=2) - 1
    spots = jnp.arange(capacity, dtype=jnp.int32)
    picked = (mine[..., None] == 1) & (rank[..., None] == spots)
    bucket_slot = jnp.sum(jnp.where(picked, slot_group[..., None], 0), axis=2)
    used = spots < jnp.sum(mine, axis=2)[..., None]
    hits = used[..., None] & (bucket_slot[..., None] == jnp.arange(slot_count, dtype=jnp.int32))
    bucket_index = jnp.arange(places, dtype=jnp.int32).reshape(own_count, capacity)
    source = jnp.sum(jnp.where(hits, bucket_index[None, :, :, None], 0), axis=(1, 2))
    bucket_slot = bucket_slot.reshape(3, places)
    own_holder = lax.dynamic_index_in_dim(holder_group, own_index, 1, keepdims=False)
    entries = jnp.arange(group, dtype=jnp.int32)
    earlier = (own_holder[:, :, None] == own_holder[:, None, :]) & (
        entries[None, :, None] < entries[None, None, :]
    )
    position = jnp.sum(earlier.astype(jnp.int32), axis=1)
    flat = own_holder * capacity + position
    rows = lax.dynamic_index_in_dim(
        block_rows.reshape(3, own_count, group), own_index, 1, keepdims=False
    )
    quarter = data_index.astype(jnp.int32).reshape(1)

    def exchange(parts):
        kept = [parts[0]]
        for s in range(1, data_count):
            turn = [(i, (i + s) % data_count) for i in range(data_count)]
            kept.append(lax.ppermute(parts[s], "dp", turn))
        return kept

    def to_planes(parts):
        twice = jnp.concatenate([parts, parts])
        return [
            lax.dynamic_index_in_dim(twice, data_index + s, 0, keepdims=False)
            for s in range(data_count)
        ]

    def send(which, after=()):
        sending = pack(
            which, int_values, scales[which], bucket_slot[which], quarter, rows_each, after
        )
        return sending.reshape(own_count, capacity, rows_each, block)

    def receive(sending):
        arrived = lax.all_to_all(sending, "own", split_axis=0, concat_axis=0, tiled=True)
        return arrived.reshape(places, rows_each, block)

    chips = own_count // 2
    likes = [[core + 2 * chip for chip in range(chips)] for core in range(2)]
    swap = [(i, i ^ 1) for i in range(own_count)]
    core = jnp.remainder(own_index, 2).astype(jnp.int32).reshape(1)
    turns = own_index ^ (2 * jnp.arange(chips, dtype=jnp.int32))
    order = jnp.stack([turns, turns ^ 1], axis=1).reshape(own_count)

    def over_chips(value):
        turns = [[(i, i ^ (2 * turn)) for i in range(own_count)] for turn in range(1, chips)]
        return [value] + [lax.ppermute(value, "own", turn) for turn in turns]

    near = over_chips(out_grad)
    gone = tuple(mark(part) for part in near[1:])
    near = jnp.stack(near)
    cut = local_tokens // 4
    bundle = jnp.concatenate([near[:, :cut].reshape(chips * cut, local_width), out_grad[cut:]])
    bundles = exchange([bundle] * data_count)[1:]

    early = [part[: chips * cut].reshape(chips, cut, local_width) for part in bundles]
    late = [part[chips * cut :] for part in bundles]

    local = inputs.reshape(local_tokens, row_blocks // own_count, data_count, rows_each)
    local = local.transpose(2, 0, 1, 3).reshape(data_count, local_tokens, depth // own_count)
    local = exchange(to_planes(local))
    sending_gate = send(0)
    local = in_order(local, quarter, (mark(sending_gate),) + gone)
    gathered = lax.all_gather(local.reshape(tokens, depth // own_count), "own", axis=0)
    sending_up, sending_down = send(1, (mark(local),)), send(2, (mark(local),))
    arrived_gate = receive(sending_gate)

    x = gathered.transpose(1, 0, 2).reshape(tokens, depth)
    x_turned = gathered.transpose(0, 2, 1).reshape(depth, tokens)
    packed = (mark(sending_up), mark(sending_down)) + tuple(mark(part) for part in bundles)
    gate_weights, part = forward(x, arrived_gate, flat[0], rows[0], columns, row_blocks, packed)
    gate = lax.psum_scatter(part, "dp", scatter_dimension=0)
    late = over_chips(tie(jnp.stack(late), mark(gate_weights)))
    arrived_up = receive(tie(sending_up, mark(gate_weights)))
    up_weights, part = forward(
        x,
        arrived_up,
        flat[1],
        rows[1],
        columns,
        row_blocks,
        (mark(gate),) + tuple(mark(part) for part in late[1:]),
    )
    up_value = lax.psum_scatter(part, "dp", scatter_dimension=0)
    cotangents = (near, jnp.stack(early), jnp.stack(late))
    cotangents = (cotangents, [lax.ppermute(part, "own", swap) for part in cotangents])
    arrived_down = receive(tie(sending_down, mark(arrived_up)))
    grad_act = forward_down(
        cotangents, arrived_down, flat[2], rows[2], quarter, order, columns, row_blocks
    )
    value, grad_gate, grad_up = silu_parts(
        gate.reshape(hidden, tokens).astype(F32), up_value.reshape(hidden, tokens).astype(F32), grad_act
    )
    shape = (columns, rows_each, tokens)

    def give_back(leaving):
        leaving = leaving.reshape(own_count, capacity, rows_each, block)
        returned = lax.all_to_all(leaving, "own", split_axis=0, concat_axis=0, tiled=True)
        return returned.reshape(places, rows_each, block)

    all_up = lax.all_gather(grad_up.reshape(shape), "dp", axis=0)
    leaving = weight_grad_down(
        value, cotangents, flat[2], rows[2], quarter, order, places, block, columns, row_blocks, factor
    )
    all_gate = lax.all_gather(grad_gate.reshape(shape), "dp", axis=0)
    returned = give_back(leaving)
    leaving = weight_grad(
        x_turned, all_up, flat[1], rows[1], places, row_blocks, factor, (mark(returned),)
    )
    total = unpack(2, returned, source[2], None)
    returned = give_back(leaving)

    up_weights = up_weights.reshape(depth, columns * block)
    gate_weights = gate_weights.reshape(depth, columns * block)
    back = input_part(up_weights, all_up, core, chips, after=(mark(leaving),))
    back = input_part(gate_weights, all_gate, core, chips, back, (mark(returned), mark(total)))
    leaving = weight_grad(
        x_turned, all_gate, flat[0], rows[0], places, row_blocks, factor, (mark(back[0]),)
    )
    total = unpack(1, returned, source[1], total)
    returned = give_back(leaving)

    back = back[0].astype(F32) + lax.ppermute(back[1], "own", swap).astype(F32)
    back = lax.psum_scatter(
        back.astype(BF16), "own", scatter_dimension=0, axis_index_groups=likes
    )
    back = back.reshape(depth // own_count, data_count, local_tokens).transpose(1, 0, 2)
    back = tie(back, mark(total))
    back = lax.all_to_all(back, "dp", split_axis=0, concat_axis=0, tiled=True)
    back = back.reshape(data_count, row_blocks // own_count, rows_each, local_tokens)
    input_grad = back.transpose(3, 1, 0, 2).reshape(local_tokens, local_width)
    total = unpack(0, returned, source[0], total)
    return (input_grad, total)


def solution(mesh):
    placed = (
        P("dp", "own"),
        P("dp", "own"),
        P(None, "own", None, None),
        P(None, "own"),
        P(),
        P(),
        P(),
    )
    return jax.shard_map(
        per_device,
        mesh=mesh,
        in_specs=placed,
        out_specs=(P("dp", "own"), P(None, "own", "dp", None)),
        check_vma=False,
    )
```

```python
import functools
import math

import jax
import jax.numpy as jnp
from jax import lax
from jax.experimental import pallas as pl
from jax.experimental.pallas import tpu as pltpu
from jax.sharding import PartitionSpec as P

F32 = jnp.float32
BF16 = jnp.bfloat16
NT = (((1,), (1,)), ((), ()))
COST = pl.CostEstimate(flops=1024, bytes_accessed=1024, transcendentals=0)
PARAMS = pltpu.CompilerParams(vmem_limit_bytes=56 * 2**20)


def whole(shape):
    return pl.BlockSpec(shape, lambda *_: (0,) * len(shape))


def waiting(after):
    return [pl.BlockSpec(memory_space=pl.ANY)] * len(after)


def mark(value):
    return value.reshape((-1,) + value.shape[-2:])[0, :16, :128]


def tie(value, *after):
    def kernel(*refs):
        pass

    return pl.pallas_call(
        kernel,
        out_shape=jax.ShapeDtypeStruct(value.shape, value.dtype),
        in_specs=waiting((value,) + after),
        out_specs=pl.BlockSpec(memory_space=pl.ANY),
        input_output_aliases={0: 0},
        compiler_params=PARAMS,
        name="tie",
    )(value, *after)


def pack(which, ints, scales, slots, quarter, rows_each, after=()):
    slot_count, block = ints.shape[1], ints.shape[2]
    places = slots.shape[0]

    def kernel(slots, quarter, scales, ints, *refs):
        out = refs[-1]

        def place(index, _):
            slot = slots[index]
            out[index] = (ints[0, slot].astype(F32) * scales[slot]).astype(BF16)
            return _

        lax.fori_loop(0, places, place, 0, unroll=8)

    return pl.pallas_call(
        kernel,
        out_shape=jax.ShapeDtypeStruct((places, rows_each, block), BF16),
        grid_spec=pltpu.PrefetchScalarGridSpec(
            num_scalar_prefetch=3,
            grid=(1,),
            in_specs=[
                pl.BlockSpec(
                    (1, slot_count, rows_each, block), lambda g, s, q, c: (which, 0, q[0], 0)
                )
            ]
            + waiting(after),
            out_specs=whole((places, rows_each, block)),
        ),
        compiler_params=PARAMS,
        cost_estimate=COST,
        name="pack",
    )(slots, quarter, scales, ints, *after)


def forward(x, arrived, flat, rows, columns, row_blocks, after=()):
    places, rows_each, block = arrived.shape
    tokens, depth = x.shape
    keep = flat.shape[0] // columns
    quarters = block // rows_each

    def kernel(flat, rows, x, arrived, *refs):
        dense, out = refs[-2:]
        step = pl.program_id(0)
        dense[...] = jnp.zeros_like(dense)
        for half in range(2):
            base = (step * 2 + half) * keep
            lanes = slice(half * block, (half + 1) * block)

            def place(k, _):
                dense[rows[base + k], :, lanes] = arrived[flat[base + k]]
                return _

            lax.fori_loop(0, keep, place, 0, unroll=13 if keep % 13 == 0 else 2)
        weights = dense[...].reshape(depth, 2 * block)
        result = jnp.dot(x[...], weights, preferred_element_type=F32)
        turned = jnp.transpose(result.astype(BF16))
        for half in range(2):
            for q in range(quarters):
                first = half * block + q * rows_each
                out[q, half] = turned[first : first + rows_each]

    return pl.pallas_call(
        kernel,
        out_shape=(
            jax.ShapeDtypeStruct((row_blocks, rows_each, columns * block), BF16),
            jax.ShapeDtypeStruct((quarters, columns, rows_each, tokens), BF16),
        ),
        grid_spec=pltpu.PrefetchScalarGridSpec(
            num_scalar_prefetch=2,
            grid=(columns // 2,),
            in_specs=[whole((tokens, depth)), whole((places, rows_each, block))] + waiting(after),
            out_specs=(
                pl.BlockSpec((row_blocks, rows_each, 2 * block), lambda g, f, r: (0, 0, g)),
                pl.BlockSpec((quarters, 2, rows_each, tokens), lambda g, f, r: (0, g, 0, 0)),
            ),
        ),
        compiler_params=PARAMS,
        cost_estimate=COST,
        name="forward",
    )(flat, rows, x, arrived, *after)


def share_specs(cotangents):
    near, early, late = cotangents
    _, tokens, width = near.shape
    others, _, first, _ = early.shape
    return [
        pl.BlockSpec((1, tokens, width), lambda g, *_: (g, 0, 0)),
        pl.BlockSpec((others, 1, first, width), lambda g, *_: (0, g, 0, 0)),
        pl.BlockSpec((1, others, tokens - first, width), lambda g, *_: (g, 0, 0, 0)),
    ]


def join(joined, quarter, near, early, late):
    planes, _, width = joined.shape
    first = early.shape[2]
    joined[quarter] = near[0]
    for shift in range(1, planes):
        plane = lax.rem(quarter + planes - shift, planes)
        joined[plane, :first] = early[shift - 1, 0]
        joined[plane, first:] = late[0, shift - 1]
    return joined[...].reshape(-1, width)


def forward_down(cotangents, arrived, flat, rows, quarter, order, columns, row_blocks):
    chips, tokens, width = cotangents[0][0].shape
    planes = cotangents[0][1].shape[0] + 1
    owners = 2 * chips
    places, rows_each, block = arrived.shape
    keep = flat.shape[0] // columns
    hidden = columns * rows_each
    per_owner = row_blocks // owners

    def kernel(flat, rows, quarter, order, *refs):
        shares, (arrived, out, joined, dense) = (refs[:3], refs[3:6]), refs[6:]
        step = pl.program_id(0)

        @pl.when(step == 0)
        def _():
            dense[...] = jnp.zeros_like(dense)
            out[...] = jnp.zeros_like(out)
            for c in range(columns):

                def place(k, _):
                    row = rows[c * keep + k]
                    lane = pl.multiple_of((row % per_owner) * block, block)
                    dense[row // per_owner, c * rows_each : (c + 1) * rows_each, pl.ds(lane, block)] = (
                        arrived[flat[c * keep + k]]
                    )
                    return _

                lax.fori_loop(0, keep, place, 0, unroll=13 if keep % 13 == 0 else 2)

        for core in range(2):
            out[...] += lax.dot_general(
                dense[order[2 * step + core]],
                join(joined, quarter[0], *shares[core]),
                NT,
                preferred_element_type=F32,
            )

    share = share_specs(cotangents[0])
    return pl.pallas_call(
        kernel,
        out_shape=jax.ShapeDtypeStruct((hidden, planes * tokens), F32),
        grid_spec=pltpu.PrefetchScalarGridSpec(
            num_scalar_prefetch=4,
            grid=(chips,),
            in_specs=share + share + [whole((places, rows_each, block))],
            out_specs=whole((hidden, planes * tokens)),
            scratch_shapes=[
                pltpu.VMEM((planes, tokens, width), BF16),
                pltpu.VMEM((owners, hidden, width), BF16),
            ],
        ),
        compiler_params=PARAMS,
        cost_estimate=COST,
        name="forward_down",
    )(flat, rows, quarter, order, *cotangents[0], *cotangents[1], arrived)


def weight_grad(x_turned, grad, flat, rows, places, row_blocks, factor, after=()):
    quarters, columns, rows_each, tokens = grad.shape
    depth = x_turned.shape[0]
    block = quarters * rows_each
    keep = flat.shape[0] // columns

    def kernel(flat, rows, x_turned, grad, *refs):
        out, result = refs[-2:]
        step = pl.program_id(0)
        right = jnp.concatenate(
            [grad[q, half] for half in range(2) for q in range(quarters)], axis=0
        )
        product = lax.dot_general(x_turned[...], right, NT, preferred_element_type=F32)
        result[...] = (product * factor).astype(BF16).reshape(result.shape)
        for half in range(2):
            base = (step * 2 + half) * keep
            lanes = slice(half * block, (half + 1) * block)

            def place(k, _):
                out[flat[base + k]] = result[rows[base + k], :, lanes]
                return _

            lax.fori_loop(0, keep, place, 0, unroll=13 if keep % 13 == 0 else 2)

    return pl.pallas_call(
        kernel,
        out_shape=jax.ShapeDtypeStruct((places, rows_each, block), BF16),
        grid_spec=pltpu.PrefetchScalarGridSpec(
            num_scalar_prefetch=2,
            grid=(columns // 2,),
            in_specs=[
                whole((depth, tokens)),
                pl.BlockSpec((quarters, 2, rows_each, tokens), lambda g, f, r: (0, g, 0, 0)),
            ]
            + waiting(after),
            out_specs=whole((places, rows_each, block)),
            scratch_shapes=[pltpu.VMEM((row_blocks, rows_each, 2 * block), BF16)],
        ),
        compiler_params=PARAMS,
        cost_estimate=COST,
        name="weight_grad",
    )(flat, rows, x_turned, grad, *after)


def weight_grad_down(
    value, cotangents, flat, rows, quarter, order, places, block, columns, row_blocks, factor
):
    chips, tokens, width = cotangents[0][0].shape
    planes = cotangents[0][1].shape[0] + 1
    owners = 2 * chips
    hidden = value.shape[0]
    rows_each = hidden // columns
    keep = flat.shape[0] // columns
    per_owner = row_blocks // owners

    def kernel(flat, rows, quarter, order, value, *refs):
        shares, (out, joined, result) = (refs[:3], refs[3:6]), refs[6:]
        step = pl.program_id(0)
        for core in range(2):
            right = join(joined, quarter[0], *shares[core])
            product = jnp.dot(value[...], right, preferred_element_type=F32)
            result[order[2 * step + core]] = (product * factor).astype(BF16)

        @pl.when(step == chips - 1)
        def _():
            for c in range(columns):

                def place(k, _):
                    row = rows[c * keep + k]
                    lane = pl.multiple_of((row % per_owner) * block, block)
                    out[flat[c * keep + k]] = result[
                        row // per_owner, c * rows_each : (c + 1) * rows_each, pl.ds(lane, block)
                    ]
                    return _

                lax.fori_loop(0, keep, place, 0, unroll=13 if keep % 13 == 0 else 2)

    share = share_specs(cotangents[0])
    return pl.pallas_call(
        kernel,
        out_shape=jax.ShapeDtypeStruct((places, rows_each, block), BF16),
        grid_spec=pltpu.PrefetchScalarGridSpec(
            num_scalar_prefetch=4,
            grid=(chips,),
            in_specs=[whole((hidden, planes * tokens))] + share + share,
            out_specs=whole((places, rows_each, block)),
            scratch_shapes=[
                pltpu.VMEM((planes, tokens, width), BF16),
                pltpu.VMEM((owners, hidden, width), BF16),
            ],
        ),
        compiler_params=PARAMS,
        cost_estimate=COST,
        name="weight_grad_down",
    )(flat, rows, quarter, order, value, *cotangents[0], *cotangents[1])


def input_part(weights, grad, first, chips, earlier=(), after=()):
    depth, units = weights.shape
    quarters, columns, rows_each, tokens = grad.shape
    rows = depth // (2 * chips)

    def kernel(first, left, right, grad, *refs):
        earlier, (*outs, natural) = refs[: len(refs) - len(after) - 3], refs[-3:]

        @pl.when(pl.program_id(0) == 0)
        def _():
            for c in range(columns):
                for q in range(quarters):
                    natural[c, q] = grad[q, c]

        both = jnp.concatenate([left[...], right[...]], axis=0)
        product = jnp.dot(
            both, natural[...].reshape(units, tokens), preferred_element_type=F32
        )
        for core in range(2):
            part = product[core * rows : (core + 1) * rows]
            if earlier:
                part = earlier[core][0] + part
            outs[core][0] = part.astype(outs[core].dtype)

    share = pl.BlockSpec((1, rows, tokens), lambda g, f: (g, 0, 0))
    out = jax.ShapeDtypeStruct((chips, rows, tokens), BF16 if earlier else F32)
    return pl.pallas_call(
        kernel,
        out_shape=(out, out),
        grid_spec=pltpu.PrefetchScalarGridSpec(
            num_scalar_prefetch=1,
            grid=(chips,),
            in_specs=[
                pl.BlockSpec((rows, units), lambda g, f: (2 * g + f[0], 0)),
                pl.BlockSpec((rows, units), lambda g, f: (2 * g + 1 - f[0], 0)),
                whole(grad.shape),
            ]
            + [share] * len(earlier)
            + waiting(after),
            out_specs=(share, share),
            scratch_shapes=[pltpu.VMEM((columns, quarters, rows_each, tokens), BF16)],
        ),
        compiler_params=PARAMS,
        cost_estimate=COST,
        name="input_part",
    )(first, weights, weights, grad, *earlier, *after)


def unpack(which, returned, source, total):
    places, rows_each, block = returned.shape
    slot_count = source.shape[0]

    def kernel(source, returned, *refs):
        out = refs[-1]

        def place(slot, _):
            out[0, slot] = returned[source[slot]]
            return _

        lax.fori_loop(0, slot_count, place, 0, unroll=8)

    shape = (3, slot_count, rows_each, block)
    extra = [] if total is None else [total]
    return pl.pallas_call(
        kernel,
        out_shape=jax.ShapeDtypeStruct(shape, BF16),
        grid_spec=pltpu.PrefetchScalarGridSpec(
            num_scalar_prefetch=1,
            grid=(1,),
            in_specs=[whole((places, rows_each, block))] + waiting(extra),
            out_specs=pl.BlockSpec((1,) + shape[1:], lambda g, s: (which, 0, 0, 0)),
        ),
        input_output_aliases={2: 0} if extra else {},
        compiler_params=PARAMS,
        cost_estimate=COST,
        name="unpack",
    )(source, returned, *extra)


def in_order(kept, quarter, after=()):
    count, shape = len(kept), kept[0].shape

    def kernel(quarter, *refs):
        for shift in range(count):
            refs[-1][lax.rem(quarter[0] + count - shift, count)] = refs[shift][...]

    return pl.pallas_call(
        kernel,
        out_shape=jax.ShapeDtypeStruct((count,) + shape, kept[0].dtype),
        grid_spec=pltpu.PrefetchScalarGridSpec(
            num_scalar_prefetch=1,
            grid=(1,),
            in_specs=[whole(shape)] * count + waiting(after),
            out_specs=whole((count,) + shape),
        ),
        compiler_params=PARAMS,
        cost_estimate=COST,
        name="in_order",
    )(quarter, *kept, *after)


def silu_parts(gate, up_value, grad_act):
    sigmoid_g = jax.nn.sigmoid(gate)
    activated = gate * sigmoid_g
    value = (activated * up_value).astype(BF16)
    grad_gate = (grad_act * up_value * sigmoid_g * (1.0 + gate * (1.0 - sigmoid_g))).astype(BF16)
    grad_up = (grad_act * activated).astype(BF16)
    return (value, grad_gate, grad_up)


def per_device(inputs, out_grad, int_values, scales, block_rows, holder, slot_index):
    own_count = lax.axis_size("own")
    data_count = lax.axis_size("dp")
    own_index = lax.axis_index("own")
    data_index = lax.axis_index("dp")
    local_tokens, local_width = inputs.shape
    tokens = local_tokens * data_count
    slot_count = int_values.shape[1]
    block = int_values.shape[2]
    keep = block_rows.shape[2]
    width = local_width * own_count
    row_blocks = width // block
    columns = block_rows.shape[1] // own_count
    group = columns * keep
    active = 3 * own_count // 4
    capacity = (group + active - 1) // active
    places = own_count * capacity
    rows_each = block // data_count
    depth = row_blocks * rows_each
    hidden = columns * rows_each
    factor = 1.0 / math.sqrt(tokens)

    holder_group = holder.reshape(3, own_count, group)
    slot_group = slot_index.reshape(3, own_count, group)
    mine = (holder_group == own_index).astype(jnp.int32)
    rank = jnp.cumsum(mine, axis=2) - 1
    spots = jnp.arange(capacity, dtype=jnp.int32)
    picked = (mine[..., None] == 1) & (rank[..., None] == spots)
    bucket_slot = jnp.sum(jnp.where(picked, slot_group[..., None], 0), axis=2)
    used = spots < jnp.sum(mine, axis=2)[..., None]
    hits = used[..., None] & (bucket_slot[..., None] == jnp.arange(slot_count, dtype=jnp.int32))
    bucket_index = jnp.arange(places, dtype=jnp.int32).reshape(own_count, capacity)
    source = jnp.sum(jnp.where(hits, bucket_index[None, :, :, None], 0), axis=(1, 2))
    bucket_slot = bucket_slot.reshape(3, places)
    own_holder = lax.dynamic_index_in_dim(holder_group, own_index, 1, keepdims=False)
    entries = jnp.arange(group, dtype=jnp.int32)
    earlier = (own_holder[:, :, None] == own_holder[:, None, :]) & (
        entries[None, :, None] < entries[None, None, :]
    )
    position = jnp.sum(earlier.astype(jnp.int32), axis=1)
    flat = own_holder * capacity + position
    rows = lax.dynamic_index_in_dim(
        block_rows.reshape(3, own_count, group), own_index, 1, keepdims=False
    )
    quarter = data_index.astype(jnp.int32).reshape(1)

    def exchange(parts):
        kept = [parts[0]]
        for s in range(1, data_count):
            turn = [(i, (i + s) % data_count) for i in range(data_count)]
            kept.append(lax.ppermute(parts[s], "dp", turn))
        return kept

    def to_planes(parts):
        twice = jnp.concatenate([parts, parts])
        return [
            lax.dynamic_index_in_dim(twice, data_index + s, 0, keepdims=False)
            for s in range(data_count)
        ]

    def send(which, after=()):
        sending = pack(
            which, int_values, scales[which], bucket_slot[which], quarter, rows_each, after
        )
        return sending.reshape(own_count, capacity, rows_each, block)

    def receive(sending):
        arrived = lax.all_to_all(sending, "own", split_axis=0, concat_axis=0, tiled=True)
        return arrived.reshape(places, rows_each, block)

    chips = own_count // 2
    likes = [[core + 2 * chip for chip in range(chips)] for core in range(2)]
    swap = [(i, i ^ 1) for i in range(own_count)]
    core = jnp.remainder(own_index, 2).astype(jnp.int32).reshape(1)
    turns = own_index ^ (2 * jnp.arange(chips, dtype=jnp.int32))
    order = jnp.stack([turns, turns ^ 1], axis=1).reshape(own_count)

    def over_chips(value):
        turns = [[(i, i ^ (2 * turn)) for i in range(own_count)] for turn in range(1, chips)]
        return [value] + [lax.ppermute(value, "own", turn) for turn in turns]

    near = over_chips(out_grad)
    gone = tuple(mark(part) for part in near[1:])
    near = jnp.stack(near)
    cut = local_tokens // 8
    bundle = jnp.concatenate([near[:, :cut].reshape(chips * cut, local_width), out_grad[cut:]])
    bundles = exchange([bundle] * data_count)[1:]

    early = [part[: chips * cut].reshape(chips, cut, local_width) for part in bundles]
    late = [part[chips * cut :] for part in bundles]

    local = inputs.reshape(local_tokens, row_blocks // own_count, data_count, rows_each)
    local = local.transpose(2, 0, 1, 3).reshape(data_count, local_tokens, depth // own_count)
    local = exchange(to_planes(local))
    sending_gate = send(0)
    local = in_order(local, quarter, (mark(sending_gate),) + gone)
    gathered = lax.all_gather(local.reshape(tokens, depth // own_count), "own", axis=0)
    sending_up, sending_down = send(1, (mark(local),)), send(2, (mark(local),))
    arrived_gate = receive(sending_gate)

    x = gathered.transpose(1, 0, 2).reshape(tokens, depth)
    x_turned = gathered.transpose(0, 2, 1).reshape(depth, tokens)
    packed = (mark(sending_up), mark(sending_down)) + tuple(mark(part) for part in bundles)
    gate_weights, part = forward(x, arrived_gate, flat[0], rows[0], columns, row_blocks, packed)
    gate = lax.psum_scatter(part, "dp", scatter_dimension=0)
    late = over_chips(tie(jnp.stack(late), mark(gate_weights)))
    arrived_up = receive(tie(sending_up, mark(gate_weights)))
    up_weights, part = forward(
        x,
        arrived_up,
        flat[1],
        rows[1],
        columns,
        row_blocks,
        (mark(gate),) + tuple(mark(part) for part in late[1:]),
    )
    up_value = lax.psum_scatter(part, "dp", scatter_dimension=0)
    cotangents = (near, jnp.stack(early), jnp.stack(late))
    cotangents = (cotangents, [lax.ppermute(part, "own", swap) for part in cotangents])
    arrived_down = receive(tie(sending_down, mark(arrived_up)))
    grad_act = forward_down(
        cotangents, arrived_down, flat[2], rows[2], quarter, order, columns, row_blocks
    )
    value, grad_gate, grad_up = silu_parts(
        gate.reshape(hidden, tokens).astype(F32), up_value.reshape(hidden, tokens).astype(F32), grad_act
    )
    shape = (columns, rows_each, tokens)

    def give_back(leaving):
        leaving = leaving.reshape(own_count, capacity, rows_each, block)
        returned = lax.all_to_all(leaving, "own", split_axis=0, concat_axis=0, tiled=True)
        return returned.reshape(places, rows_each, block)

    all_up = lax.all_gather(grad_up.reshape(shape), "dp", axis=0)
    leaving = weight_grad_down(
        value, cotangents, flat[2], rows[2], quarter, order, places, block, columns, row_blocks, factor
    )
    all_gate = lax.all_gather(grad_gate.reshape(shape), "dp", axis=0)
    returned = give_back(leaving)
    leaving = weight_grad(
        x_turned, all_up, flat[1], rows[1], places, row_blocks, factor, (mark(returned),)
    )
    total = unpack(2, returned, source[2], None)
    returned = give_back(leaving)

    up_weights = up_weights.reshape(depth, columns * block)
    gate_weights = gate_weights.reshape(depth, columns * block)
    back = input_part(up_weights, all_up, core, chips, after=(mark(leaving),))
    back = input_part(gate_weights, all_gate, core, chips, back, (mark(returned), mark(total)))
    leaving = weight_grad(
        x_turned, all_gate, flat[0], rows[0], places, row_blocks, factor, (mark(back[0]),)
    )
    total = unpack(1, returned, source[1], total)
    returned = give_back(leaving)

    back = back[0].astype(F32) + lax.ppermute(back[1], "own", swap).astype(F32)
    back = lax.psum_scatter(
        back.astype(BF16), "own", scatter_dimension=0, axis_index_groups=likes
    )
    back = back.reshape(depth // own_count, data_count, local_tokens).transpose(1, 0, 2)
    back = tie(back, mark(total))
    back = in_order(exchange(to_planes(back)), quarter)
    back = back.reshape(data_count, row_blocks // own_count, rows_each, local_tokens)
    input_grad = back.transpose(3, 1, 0, 2).reshape(local_tokens, local_width)
    total = unpack(0, returned, source[0], total)
    return (input_grad, total)


def solution(mesh):
    placed = (
        P("dp", "own"),
        P("dp", "own"),
        P(None, "own", None, None),
        P(None, "own"),
        P(),
        P(),
        P(),
    )
    return jax.shard_map(
        per_device,
        mesh=mesh,
        in_specs=placed,
        out_specs=(P("dp", "own"), P(None, "own", "dp", None)),
        check_vma=False,
    )
```

```python
import functools
import math

import jax
import jax.numpy as jnp
from jax import lax
from jax.experimental import pallas as pl
from jax.experimental.pallas import tpu as pltpu
from jax.sharding import PartitionSpec as P

F32 = jnp.float32
BF16 = jnp.bfloat16
NT = (((1,), (1,)), ((), ()))
COST = pl.CostEstimate(flops=1024, bytes_accessed=1024, transcendentals=0)
PARAMS = pltpu.CompilerParams(vmem_limit_bytes=56 * 2**20)


def whole(shape):
    return pl.BlockSpec(shape, lambda *_: (0,) * len(shape))


def waiting(after):
    return [pl.BlockSpec(memory_space=pl.ANY)] * len(after)


def mark(value):
    return value.reshape((-1,) + value.shape[-2:])[0, :16, :128]


def tie(value, *after):
    def kernel(*refs):
        pass

    return pl.pallas_call(
        kernel,
        out_shape=jax.ShapeDtypeStruct(value.shape, value.dtype),
        in_specs=waiting((value,) + after),
        out_specs=pl.BlockSpec(memory_space=pl.ANY),
        input_output_aliases={0: 0},
        compiler_params=PARAMS,
        name="tie",
    )(value, *after)


def pack(which, ints, scales, slots, quarter, rows_each, after=()):
    slot_count, block = ints.shape[1], ints.shape[2]
    places = slots.shape[0]

    def kernel(slots, quarter, scales, ints, *refs):
        out = refs[-1]

        def place(index, _):
            slot = slots[index]
            out[index] = (ints[0, slot].astype(F32) * scales[slot]).astype(BF16)
            return _

        lax.fori_loop(0, places, place, 0, unroll=8)

    return pl.pallas_call(
        kernel,
        out_shape=jax.ShapeDtypeStruct((places, rows_each, block), BF16),
        grid_spec=pltpu.PrefetchScalarGridSpec(
            num_scalar_prefetch=3,
            grid=(1,),
            in_specs=[
                pl.BlockSpec(
                    (1, slot_count, rows_each, block), lambda g, s, q, c: (which, 0, q[0], 0)
                )
            ]
            + waiting(after),
            out_specs=whole((places, rows_each, block)),
        ),
        compiler_params=PARAMS,
        cost_estimate=COST,
        name="pack",
    )(slots, quarter, scales, ints, *after)


def forward(x, arrived, flat, rows, columns, row_blocks, after=()):
    places, rows_each, block = arrived.shape
    tokens, depth = x.shape
    keep = flat.shape[0] // columns
    quarters = block // rows_each

    def kernel(flat, rows, x, arrived, *refs):
        dense, out = refs[-2:]
        step = pl.program_id(0)
        dense[...] = jnp.zeros_like(dense)
        for half in range(2):
            base = (step * 2 + half) * keep
            lanes = slice(half * block, (half + 1) * block)

            def place(k, _):
                dense[rows[base + k], :, lanes] = arrived[flat[base + k]]
                return _

            lax.fori_loop(0, keep, place, 0, unroll=13 if keep % 13 == 0 else 2)
        weights = dense[...].reshape(depth, 2 * block)
        result = jnp.dot(x[...], weights, preferred_element_type=F32)
        turned = jnp.transpose(result.astype(BF16))
        for half in range(2):
            for q in range(quarters):
                first = half * block + q * rows_each
                out[q, half] = turned[first : first + rows_each]

    return pl.pallas_call(
        kernel,
        out_shape=(
            jax.ShapeDtypeStruct((row_blocks, rows_each, columns * block), BF16),
            jax.ShapeDtypeStruct((quarters, columns, rows_each, tokens), BF16),
        ),
        grid_spec=pltpu.PrefetchScalarGridSpec(
            num_scalar_prefetch=2,
            grid=(columns // 2,),
            in_specs=[whole((tokens, depth)), whole((places, rows_each, block))] + waiting(after),
            out_specs=(
                pl.BlockSpec((row_blocks, rows_each, 2 * block), lambda g, f, r: (0, 0, g)),
                pl.BlockSpec((quarters, 2, rows_each, tokens), lambda g, f, r: (0, g, 0, 0)),
            ),
        ),
        compiler_params=PARAMS,
        cost_estimate=COST,
        name="forward",
    )(flat, rows, x, arrived, *after)


def share_specs(cotangents):
    near, early, late = cotangents
    _, tokens, width = near.shape
    others, _, first, _ = early.shape
    return [
        pl.BlockSpec((1, tokens, width), lambda g, *_: (g, 0, 0)),
        pl.BlockSpec((others, 1, first, width), lambda g, *_: (0, g, 0, 0)),
        pl.BlockSpec((1, others, tokens - first, width), lambda g, *_: (g, 0, 0, 0)),
    ]


def join(joined, quarter, near, early, late):
    planes, _, width = joined.shape
    first = early.shape[2]
    joined[quarter] = near[0]
    for shift in range(1, planes):
        plane = lax.rem(quarter + planes - shift, planes)
        joined[plane, :first] = early[shift - 1, 0]
        joined[plane, first:] = late[0, shift - 1]
    return joined[...].reshape(-1, width)


def forward_down(cotangents, arrived, flat, rows, quarter, order, columns, row_blocks):
    chips, tokens, width = cotangents[0][0].shape
    planes = cotangents[0][1].shape[0] + 1
    owners = 2 * chips
    places, rows_each, block = arrived.shape
    keep = flat.shape[0] // columns
    hidden = columns * rows_each
    per_owner = row_blocks // owners

    def kernel(flat, rows, quarter, order, *refs):
        shares, (arrived, out, joined, dense) = (refs[:3], refs[3:6]), refs[6:]
        step = pl.program_id(0)

        @pl.when(step == 0)
        def _():
            dense[...] = jnp.zeros_like(dense)
            out[...] = jnp.zeros_like(out)
            for c in range(columns):

                def place(k, _):
                    row = rows[c * keep + k]
                    lane = pl.multiple_of((row % per_owner) * block, block)
                    dense[row // per_owner, c * rows_each : (c + 1) * rows_each, pl.ds(lane, block)] = (
                        arrived[flat[c * keep + k]]
                    )
                    return _

                lax.fori_loop(0, keep, place, 0, unroll=13 if keep % 13 == 0 else 2)

        for core in range(2):
            out[...] += lax.dot_general(
                dense[order[2 * step + core]],
                join(joined, quarter[0], *shares[core]),
                NT,
                preferred_element_type=F32,
            )

    share = share_specs(cotangents[0])
    return pl.pallas_call(
        kernel,
        out_shape=jax.ShapeDtypeStruct((hidden, planes * tokens), F32),
        grid_spec=pltpu.PrefetchScalarGridSpec(
            num_scalar_prefetch=4,
            grid=(chips,),
            in_specs=share + share + [whole((places, rows_each, block))],
            out_specs=whole((hidden, planes * tokens)),
            scratch_shapes=[
                pltpu.VMEM((planes, tokens, width), BF16),
                pltpu.VMEM((owners, hidden, width), BF16),
            ],
        ),
        compiler_params=PARAMS,
        cost_estimate=COST,
        name="forward_down",
    )(flat, rows, quarter, order, *cotangents[0], *cotangents[1], arrived)


def weight_grad(x_turned, grad, flat, rows, places, row_blocks, factor, after=()):
    quarters, columns, rows_each, tokens = grad.shape
    depth = x_turned.shape[0]
    block = quarters * rows_each
    keep = flat.shape[0] // columns

    def kernel(flat, rows, x_turned, grad, *refs):
        out, result = refs[-2:]
        step = pl.program_id(0)
        right = jnp.concatenate(
            [grad[q, half] for half in range(2) for q in range(quarters)], axis=0
        )
        product = lax.dot_general(x_turned[...], right, NT, preferred_element_type=F32)
        result[...] = (product * factor).astype(BF16).reshape(result.shape)
        for half in range(2):
            base = (step * 2 + half) * keep
            lanes = slice(half * block, (half + 1) * block)

            def place(k, _):
                out[flat[base + k]] = result[rows[base + k], :, lanes]
                return _

            lax.fori_loop(0, keep, place, 0, unroll=13 if keep % 13 == 0 else 2)

    return pl.pallas_call(
        kernel,
        out_shape=jax.ShapeDtypeStruct((places, rows_each, block), BF16),
        grid_spec=pltpu.PrefetchScalarGridSpec(
            num_scalar_prefetch=2,
            grid=(columns // 2,),
            in_specs=[
                whole((depth, tokens)),
                pl.BlockSpec((quarters, 2, rows_each, tokens), lambda g, f, r: (0, g, 0, 0)),
            ]
            + waiting(after),
            out_specs=whole((places, rows_each, block)),
            scratch_shapes=[pltpu.VMEM((row_blocks, rows_each, 2 * block), BF16)],
        ),
        compiler_params=PARAMS,
        cost_estimate=COST,
        name="weight_grad",
    )(flat, rows, x_turned, grad, *after)


def weight_grad_down(
    value, cotangents, flat, rows, quarter, order, places, block, columns, row_blocks, factor
):
    chips, tokens, width = cotangents[0][0].shape
    planes = cotangents[0][1].shape[0] + 1
    owners = 2 * chips
    hidden = value.shape[0]
    rows_each = hidden // columns
    keep = flat.shape[0] // columns
    per_owner = row_blocks // owners

    def kernel(flat, rows, quarter, order, value, *refs):
        shares, (out, joined, result) = (refs[:3], refs[3:6]), refs[6:]
        step = pl.program_id(0)
        for core in range(2):
            right = join(joined, quarter[0], *shares[core])
            product = jnp.dot(value[...], right, preferred_element_type=F32)
            result[order[2 * step + core]] = (product * factor).astype(BF16)

        @pl.when(step == chips - 1)
        def _():
            for c in range(columns):

                def place(k, _):
                    row = rows[c * keep + k]
                    lane = pl.multiple_of((row % per_owner) * block, block)
                    out[flat[c * keep + k]] = result[
                        row // per_owner, c * rows_each : (c + 1) * rows_each, pl.ds(lane, block)
                    ]
                    return _

                lax.fori_loop(0, keep, place, 0, unroll=13 if keep % 13 == 0 else 2)

    share = share_specs(cotangents[0])
    return pl.pallas_call(
        kernel,
        out_shape=jax.ShapeDtypeStruct((places, rows_each, block), BF16),
        grid_spec=pltpu.PrefetchScalarGridSpec(
            num_scalar_prefetch=4,
            grid=(chips,),
            in_specs=[whole((hidden, planes * tokens))] + share + share,
            out_specs=whole((places, rows_each, block)),
            scratch_shapes=[
                pltpu.VMEM((planes, tokens, width), BF16),
                pltpu.VMEM((owners, hidden, width), BF16),
            ],
        ),
        compiler_params=PARAMS,
        cost_estimate=COST,
        name="weight_grad_down",
    )(flat, rows, quarter, order, value, *cotangents[0], *cotangents[1])


def input_part(weights, grad, first, chips, earlier=(), after=()):
    depth, units = weights.shape
    quarters, columns, rows_each, tokens = grad.shape
    rows = depth // (2 * chips)

    def kernel(first, left, right, grad, *refs):
        earlier, (*outs, natural) = refs[: len(refs) - len(after) - 3], refs[-3:]

        @pl.when(pl.program_id(0) == 0)
        def _():
            for c in range(columns):
                for q in range(quarters):
                    natural[c, q] = grad[q, c]

        both = jnp.concatenate([left[...], right[...]], axis=0)
        product = jnp.dot(
            both, natural[...].reshape(units, tokens), preferred_element_type=F32
        )
        for core in range(2):
            part = product[core * rows : (core + 1) * rows]
            if earlier:
                part = earlier[core][0] + part
            outs[core][0] = part.astype(outs[core].dtype)

    share = pl.BlockSpec((1, rows, tokens), lambda g, f: (g, 0, 0))
    out = jax.ShapeDtypeStruct((chips, rows, tokens), BF16 if earlier else F32)
    return pl.pallas_call(
        kernel,
        out_shape=(out, out),
        grid_spec=pltpu.PrefetchScalarGridSpec(
            num_scalar_prefetch=1,
            grid=(chips,),
            in_specs=[
                pl.BlockSpec((rows, units), lambda g, f: (2 * g + f[0], 0)),
                pl.BlockSpec((rows, units), lambda g, f: (2 * g + 1 - f[0], 0)),
                whole(grad.shape),
            ]
            + [share] * len(earlier)
            + waiting(after),
            out_specs=(share, share),
            scratch_shapes=[pltpu.VMEM((columns, quarters, rows_each, tokens), BF16)],
        ),
        compiler_params=PARAMS,
        cost_estimate=COST,
        name="input_part",
    )(first, weights, weights, grad, *earlier, *after)


def unpack(which, returned, source, total, after=()):
    places, rows_each, block = returned.shape
    slot_count = source.shape[0]

    def kernel(source, returned, *refs):
        out = refs[-1]

        def place(slot, _):
            out[0, slot] = returned[source[slot]]
            return _

        lax.fori_loop(0, slot_count, place, 0, unroll=8)

    shape = (3, slot_count, rows_each, block)
    extra = [] if total is None else [total]
    return pl.pallas_call(
        kernel,
        out_shape=jax.ShapeDtypeStruct(shape, BF16),
        grid_spec=pltpu.PrefetchScalarGridSpec(
            num_scalar_prefetch=1,
            grid=(1,),
            in_specs=[whole((places, rows_each, block))] + waiting(extra) + waiting(after),
            out_specs=pl.BlockSpec((1,) + shape[1:], lambda g, s: (which, 0, 0, 0)),
        ),
        input_output_aliases={2: 0} if extra else {},
        compiler_params=PARAMS,
        cost_estimate=COST,
        name="unpack",
    )(source, returned, *extra, *after)


def in_order(kept, quarter, after=()):
    count, shape = len(kept), kept[0].shape

    def kernel(quarter, *refs):
        for shift in range(count):
            refs[-1][lax.rem(quarter[0] + count - shift, count)] = refs[shift][...]

    return pl.pallas_call(
        kernel,
        out_shape=jax.ShapeDtypeStruct((count,) + shape, kept[0].dtype),
        grid_spec=pltpu.PrefetchScalarGridSpec(
            num_scalar_prefetch=1,
            grid=(1,),
            in_specs=[whole(shape)] * count + waiting(after),
            out_specs=whole((count,) + shape),
        ),
        compiler_params=PARAMS,
        cost_estimate=COST,
        name="in_order",
    )(quarter, *kept, *after)


def silu_parts(gate, up_value, grad_act):
    sigmoid_g = jax.nn.sigmoid(gate)
    activated = gate * sigmoid_g
    value = (activated * up_value).astype(BF16)
    grad_gate = (grad_act * up_value * sigmoid_g * (1.0 + gate * (1.0 - sigmoid_g))).astype(BF16)
    grad_up = (grad_act * activated).astype(BF16)
    return (value, grad_gate, grad_up)


def per_device(inputs, out_grad, int_values, scales, block_rows, holder, slot_index):
    own_count = lax.axis_size("own")
    data_count = lax.axis_size("dp")
    own_index = lax.axis_index("own")
    data_index = lax.axis_index("dp")
    local_tokens, local_width = inputs.shape
    tokens = local_tokens * data_count
    slot_count = int_values.shape[1]
    block = int_values.shape[2]
    keep = block_rows.shape[2]
    width = local_width * own_count
    row_blocks = width // block
    columns = block_rows.shape[1] // own_count
    group = columns * keep
    active = 3 * own_count // 4
    capacity = (group + active - 1) // active
    places = own_count * capacity
    rows_each = block // data_count
    depth = row_blocks * rows_each
    hidden = columns * rows_each
    factor = 1.0 / math.sqrt(tokens)

    holder_group = holder.reshape(3, own_count, group)
    slot_group = slot_index.reshape(3, own_count, group)
    mine = (holder_group == own_index).astype(jnp.int32)
    rank = jnp.cumsum(mine, axis=2) - 1
    spots = jnp.arange(capacity, dtype=jnp.int32)
    picked = (mine[..., None] == 1) & (rank[..., None] == spots)
    bucket_slot = jnp.sum(jnp.where(picked, slot_group[..., None], 0), axis=2)
    used = spots < jnp.sum(mine, axis=2)[..., None]
    hits = used[..., None] & (bucket_slot[..., None] == jnp.arange(slot_count, dtype=jnp.int32))
    bucket_index = jnp.arange(places, dtype=jnp.int32).reshape(own_count, capacity)
    source = jnp.sum(jnp.where(hits, bucket_index[None, :, :, None], 0), axis=(1, 2))
    bucket_slot = bucket_slot.reshape(3, places)
    own_holder = lax.dynamic_index_in_dim(holder_group, own_index, 1, keepdims=False)
    entries = jnp.arange(group, dtype=jnp.int32)
    earlier = (own_holder[:, :, None] == own_holder[:, None, :]) & (
        entries[None, :, None] < entries[None, None, :]
    )
    position = jnp.sum(earlier.astype(jnp.int32), axis=1)
    flat = own_holder * capacity + position
    rows = lax.dynamic_index_in_dim(
        block_rows.reshape(3, own_count, group), own_index, 1, keepdims=False
    )
    quarter = data_index.astype(jnp.int32).reshape(1)

    def exchange(parts):
        kept = [parts[0]]
        for s in range(1, data_count):
            turn = [(i, (i + s) % data_count) for i in range(data_count)]
            kept.append(lax.ppermute(parts[s], "dp", turn))
        return kept

    def to_planes(parts):
        twice = jnp.concatenate([parts, parts])
        return [
            lax.dynamic_index_in_dim(twice, data_index + s, 0, keepdims=False)
            for s in range(data_count)
        ]

    def send(which, after=()):
        sending = pack(
            which, int_values, scales[which], bucket_slot[which], quarter, rows_each, after
        )
        return sending.reshape(own_count, capacity, rows_each, block)

    def receive(sending):
        arrived = lax.all_to_all(sending, "own", split_axis=0, concat_axis=0, tiled=True)
        return arrived.reshape(places, rows_each, block)

    chips = own_count // 2
    likes = [[core + 2 * chip for chip in range(chips)] for core in range(2)]
    swap = [(i, i ^ 1) for i in range(own_count)]
    core = jnp.remainder(own_index, 2).astype(jnp.int32).reshape(1)
    turns = own_index ^ (2 * jnp.arange(chips, dtype=jnp.int32))
    order = jnp.stack([turns, turns ^ 1], axis=1).reshape(own_count)

    def over_chips(value):
        turns = [[(i, i ^ (2 * turn)) for i in range(own_count)] for turn in range(1, chips)]
        return [value] + [lax.ppermute(value, "own", turn) for turn in turns]

    near = over_chips(out_grad)
    gone = tuple(mark(part) for part in near[1:])
    near = jnp.stack(near)
    cut = local_tokens // 8
    bundle = jnp.concatenate([near[:, :cut].reshape(chips * cut, local_width), out_grad[cut:]])
    bundles = exchange([bundle] * data_count)[1:]

    early = [part[: chips * cut].reshape(chips, cut, local_width) for part in bundles]
    late = [part[chips * cut :] for part in bundles]

    local = inputs.reshape(local_tokens, row_blocks // own_count, data_count, rows_each)
    local = local.transpose(2, 0, 1, 3).reshape(data_count, local_tokens, depth // own_count)
    local = exchange(to_planes(local))
    sending_gate = send(0)
    local = in_order(local, quarter, (mark(sending_gate),) + gone)
    gathered = lax.all_gather(local.reshape(tokens, depth // own_count), "own", axis=0)
    sending_up, sending_down = send(1, (mark(local),)), send(2, (mark(local),))
    arrived_gate = receive(sending_gate)

    x = gathered.transpose(1, 0, 2).reshape(tokens, depth)
    x_turned = gathered.transpose(0, 2, 1).reshape(depth, tokens)
    packed = (mark(sending_up), mark(sending_down)) + tuple(mark(part) for part in bundles)
    gate_weights, part = forward(x, arrived_gate, flat[0], rows[0], columns, row_blocks, packed)
    gate = lax.psum_scatter(part, "dp", scatter_dimension=0)
    late = over_chips(tie(jnp.stack(late), mark(gate_weights)))
    arrived_up = receive(tie(sending_up, mark(gate_weights)))
    up_weights, part = forward(
        x,
        arrived_up,
        flat[1],
        rows[1],
        columns,
        row_blocks,
        (mark(gate),) + tuple(mark(part) for part in late[1:]),
    )
    up_value = lax.psum_scatter(part, "dp", scatter_dimension=0)
    cotangents = (near, jnp.stack(early), jnp.stack(late))
    cotangents = (cotangents, [lax.ppermute(part, "own", swap) for part in cotangents])
    arrived_down = receive(tie(sending_down, mark(arrived_up)))
    grad_act = forward_down(
        cotangents, arrived_down, flat[2], rows[2], quarter, order, columns, row_blocks
    )
    value, grad_gate, grad_up = silu_parts(
        gate.reshape(hidden, tokens).astype(F32), up_value.reshape(hidden, tokens).astype(F32), grad_act
    )
    shape = (columns, rows_each, tokens)

    def give_back(leaving):
        leaving = leaving.reshape(own_count, capacity, rows_each, block)
        returned = lax.all_to_all(leaving, "own", split_axis=0, concat_axis=0, tiled=True)
        return returned.reshape(places, rows_each, block)

    all_up = lax.all_gather(grad_up.reshape(shape), "dp", axis=0)
    leaving = weight_grad_down(
        value, cotangents, flat[2], rows[2], quarter, order, places, block, columns, row_blocks, factor
    )
    all_gate = lax.all_gather(grad_gate.reshape(shape), "dp", axis=0)
    returned = give_back(leaving)
    leaving = weight_grad(
        x_turned, all_up, flat[1], rows[1], places, row_blocks, factor, (mark(returned),)
    )
    total = unpack(2, returned, source[2], None)
    returned = give_back(leaving)

    up_weights = up_weights.reshape(depth, columns * block)
    gate_weights = gate_weights.reshape(depth, columns * block)
    back = input_part(up_weights, all_up, core, chips, after=(mark(leaving),))
    back = input_part(gate_weights, all_gate, core, chips, back, (mark(returned), mark(total)))
    leaving = weight_grad(
        x_turned, all_gate, flat[0], rows[0], places, row_blocks, factor, (mark(back[0]),)
    )
    total = unpack(1, returned, source[1], total)
    returned = give_back(leaving)

    back = back[0].astype(F32) + lax.ppermute(back[1], "own", swap).astype(F32)
    back = lax.psum_scatter(
        back.astype(BF16), "own", scatter_dimension=0, axis_index_groups=likes
    )
    back = back.reshape(depth // own_count, data_count, local_tokens).transpose(1, 0, 2)
    back = tie(back, mark(total))
    back = in_order(exchange(to_planes(back)), quarter)
    back = back.reshape(data_count, row_blocks // own_count, rows_each, local_tokens)
    input_grad = back.transpose(3, 1, 0, 2).reshape(local_tokens, local_width)
    total = unpack(0, returned, source[0], total, (mark(input_grad),))
    return (input_grad, total)


def solution(mesh):
    placed = (
        P("dp", "own"),
        P("dp", "own"),
        P(None, "own", None, None),
        P(None, "own"),
        P(),
        P(),
        P(),
    )
    return jax.shard_map(
        per_device,
        mesh=mesh,
        in_specs=placed,
        out_specs=(P("dp", "own"), P(None, "own", "dp", None)),
        check_vma=False,
    )
```
